32 devices in a mesh: grp: 2 (over x), row: 16 (over z, y, core).
Axes of the slice: x: 2, y: 2, z: 4, core: 2. Of those that a mesh axis runs over, the one named last changes fastest.
Arguments:
- green_occ: bfloat16 [2048, 1024], P(('grp', 'row')), parts along dimension 0, may hold values from -0.5 to 0.5
- green_virt: bfloat16 [2048, 1024], P(('grp', 'row')), parts along dimension 0, may hold values from -0.5 to 0.5
- coulomb3c: bfloat16 [16, 48, 128, 128], P('row'), may hold values from -1 to 1
- tile_list: int32 [16, 4, 4], P('row'), may hold values 0 or 1
- window: int32 [16, 4], replicated, may hold values from 0 to 31, as said below
Outputs:
- polar: float32 [1536, 240], P(('grp', 'row')), parts along dimension 0
The draws below stay inside these ranges and needn't reach their ends.
There are 2 independent parts, one for each index of `grp`. The reference program is written for one: setup_inputs(seed, part) draws one part's arguments, and reference() takes and returns one part's arrays. A program takes and returns all parts, laid end to end along the dimension named above; an argument that names none is the same for every part. Nothing has to cross between parts.
Inputs may be any that keep to these rules, and one draw needn't show every extreme that they name: The 4 atoms of one RI atom's window are distinct; for an RI atom on row index d they are owned by row indices d - 1, d, d + 1 taken cyclically, atom a being owned by row index a // 2.
All inputs are finite; a program needn't handle non-finite values. No bound on the sum of `tile_list` on one device may be relied on, other than what follows from the above.
Results may differ from the reference program's by a relative error of at most 0.004.
Values may be sent and summed in bfloat16 or wider, within the bound.
No kernel may reach another device: no remote copies, remote signals or barrier semaphores. Data moves between devices by JAX's collectives and lax.ppermute only.
A program may use at most 128 MiB of HBM per device.

```python
import jax
import jax.numpy as jnp
from jax import lax

BA = 32
RIB = 48
NB = 4
REACH = 2
RP = 1
AOD = 2
NRI = 16
NA = 32
NAF = 1024
SPAN = 128
N_ROW = 16


def draw_window(key, part):
    key = jax.random.fold_in(key, 7)
    choices_here = 3 * AOD
    rows = jnp.arange(NRI, dtype=jnp.int32)
    first = (rows // RP - 1) * AOD
    scores = jax.random.randint(key, (NRI, choices_here), 0, 1 << 20, dtype=jnp.int32)
    scores = scores * choices_here + jnp.arange(choices_here, dtype=jnp.int32)[None, :]
    order = jnp.argsort(scores, axis=1)[:, :NB].astype(jnp.int32)
    return ((first[:, None] + order) % NA).astype(jnp.int32)


def with_ends(entries, key, least, largest):
    dims = entries.shape
    place = [jax.random.randint(jax.random.fold_in(key, axis), (), 0, dims[axis]) for axis in range(len(dims))]
    entries = entries.at[tuple(place)].set(least)
    longest = dims.index(max(dims))
    place[longest] = (place[longest] + 1) % dims[longest]
    return entries.at[tuple(place)].set(largest)


def shard_levels(key, dims, shards, smallest, largest):
    level = 1.0
    for axis_at, blocks in shards:
        steps = jax.random.uniform(jax.random.fold_in(jax.random.fold_in(key, 6), axis_at), (blocks,), jnp.float32, smallest / len(shards), largest / len(shards))
        level = level * jnp.repeat(jnp.exp(steps), dims[axis_at] // blocks).reshape((-1,) + (1,) * (len(dims) - 1 - axis_at))
    return level


def scatter_about(rng, shape, scale, limit, cuts=(), kind=jnp.bfloat16):
    drawn = jax.random.normal(rng, shape, jnp.float32) * scale
    if len(cuts) > 0:
        drawn = shard_levels(rng, shape, cuts, -0.22, 0.18) * drawn
    return jnp.clip(drawn, min=-limit, max=limit).astype(kind)


def setup_inputs(seed: int = 0, part: int = 0) -> dict:
    arg_keys = jax.random.split(jax.random.key(seed), 6)
    part_splits = jax.random.split(jax.random.fold_in(arg_keys[5], part), 6)
    return {
        "green_occ": scatter_about(part_splits[0], (NAF, NAF), SPAN ** -0.5, 0.5, ((0, 16),)),
        "green_virt": scatter_about(part_splits[1], (NAF, NAF), SPAN ** -0.5, 0.5, ((0, 16),)),
        "coulomb3c": scatter_about(arg_keys[2], (NRI, RIB, SPAN, SPAN), 0.125, 1.0, ((0, 16),)),
        "tile_list": with_ends((jax.random.randint(arg_keys[3], (NRI, NB, NB), 0, 4) < 3).astype(jnp.int32), jax.random.fold_in(arg_keys[3], 1), 0, 1),
        "window": draw_window(jax.random.fold_in(arg_keys[5], 71), part),
    }


def expand_tiles(tiles, width):
    full = jnp.repeat(jnp.repeat(tiles, width, axis=-2), width, axis=-1)
    return full.astype(jnp.bfloat16)


def reference(green_occ, green_virt, coulomb3c, tile_list, window):
    span = NB * BA
    masked = coulomb3c * expand_tiles(tile_list, BA)[:, None]
    offsets = jnp.arange(BA, dtype=jnp.int32)
    columns = (window[:, :, None] * BA + offsets[None, None, :]).reshape(NRI, span).astype(jnp.int32)

    def contract(index):
        picked = columns[index]
        occ = green_occ[picked][:, picked].astype(jnp.float32)
        virt = green_virt[picked][:, picked].astype(jnp.float32)
        tensor = masked[index].astype(jnp.float32)
        half = jnp.einsum("rkl,km->rml", tensor, occ, precision=lax.Precision.HIGHEST).astype(jnp.bfloat16)
        dressed = jnp.einsum("rml,ls->rms", half.astype(jnp.float32), virt, precision=lax.Precision.HIGHEST)
        return dressed.astype(jnp.bfloat16)

    dressed_all = lax.map(contract, jnp.arange(NRI, dtype=jnp.int32))

    def band_row(index):
        device = index // RP
        mine = window[index]
        flattened = dressed_all[index].reshape(RIB, span * span).astype(jnp.float32)
        blocks = []
        for offset in range(-REACH, REACH + 1):
            for member in range(RP):
                other = (((device + offset) % N_ROW) * RP + member).astype(jnp.int32)
                theirs = window[other]
                match = (mine[:, None] == theirs[None, :]).astype(jnp.float32)
                tensor = masked[other].astype(jnp.float32).reshape(RIB, NB, BA, NB, BA)
                moved = jnp.einsum("ik,jl,rkalb->riajb", match, match, tensor, precision=lax.Precision.HIGHEST)
                moved = moved.reshape(RIB, span * span)
                blocks.append(jnp.dot(flattened, moved.T, precision=lax.Precision.HIGHEST, preferred_element_type=jnp.float32))
        return jnp.concatenate(blocks, axis=1)

    polar = lax.map(band_row, jnp.arange(NRI, dtype=jnp.int32))
    return polar.reshape(NRI * RIB, (2 * REACH + 1) * RP * RIB)
```

```python
import functools

import jax
import jax.numpy as jnp
from jax import lax
from jax.experimental import pallas as pl
from jax.experimental.pallas import tpu as pltpu
from jax.sharding import PartitionSpec as P

BF = jnp.bfloat16
F32 = jnp.float32
MISSING = -(1 << 20)


def dot(a, b):
    return lax.dot_general(a, b, (((1,), (0,)), ((), ())), preferred_element_type=F32)


def dot_t(a, b):
    return lax.dot_general(a, b, (((1,), (1,)), ((), ())), preferred_element_type=F32)


def iota(shape, dim):
    return lax.broadcasted_iota(jnp.int32, shape, dim)


def pick4(index, values):
    return jnp.where(
        index == 0, values[0], jnp.where(index == 1, values[1], jnp.where(index == 2, values[2], values[3]))
    )


def one_hot(shape, dim, bases):
    index = iota(shape, dim)
    position = pick4(index >> 5, bases) + (index & 31)
    return jnp.where(iota(shape, 1 - dim) == position, 1.0, 0.0).astype(BF)


def window_at(win, row):
    return [win[row, i] for i in range(4)]


def find(atoms, wanted):
    slot, there = jnp.int32(0), jnp.float32(0)
    for i in range(4):
        hit = atoms[i] == wanted
        slot = jnp.where(hit, jnp.int32(i), slot)
        there = jnp.where(hit, jnp.float32(1), there)
    return slot, there


def tile_mask(tiles, rows):
    shape = (4 * rows, 128)
    row, lane = iota(shape, 0) // rows, iota(shape, 1) >> 5
    mask = jnp.zeros(shape, F32)
    for i in range(4):
        for j in range(4):
            mask = jnp.where((row == i) & (lane == j), tiles[0, i, j].astype(F32), mask)
    return mask


def near(row, by, count):
    return lax.rem(row + by + count, count)


def column_chunk(row, count):
    return near(row, -1, count) >> 1


def prepare(count, win, tiles, occ, virt, half, g_self, g_right, g_left, far_right, far_left, xs):
    d = lax.axis_index("row")
    mine = window_at(win, d)
    funcs = half.shape[0]

    def greens(out, base, dest):
        first = column_chunk(dest, count)
        for c in range(2):
            chunk = lax.rem(first + c, count // 2)
            columns = pl.ds(pl.multiple_of(chunk * 128, 128), 128)
            out[base + 64 * c : base + 64 * c + 64, :] = occ[:, columns]
            out[base + 128 + 64 * c : base + 192 + 64 * c, :] = virt[:, columns]

    greens(g_self, 0, d)
    greens(g_right, 0, near(d, 1, count))
    greens(g_left, 0, near(d, -1, count))
    greens(far_right, funcs * 32, near(d, 2, count))
    short = tile_mask(tiles, 4)
    g_right[256:272, :] = short.astype(BF)

    mask = tile_mask(tiles, 32).astype(BF)
    left, right = near(d, -1, count) * 2, near(d, 1, count) * 2
    shape = (128, 256)
    column = iota(shape, 1)
    wanted = jnp.where(column < 128, left, right) + ((column >> 5) & 1)
    here = pick4(iota(shape, 0) >> 5, mine)
    same = (here == wanted) & ((iota(shape, 0) & 31) == (column & 31))
    select = jnp.where(same, 1.0, 0.0).astype(BF)
    for r in range(0, funcs, 4):
        block = (half[r : r + 4] * mask[None]).reshape(512, 128)
        x = dot(block, select)
        xs[0, r * 128 : r * 128 + 512, :] = x[:, :128]
        xs[1, r * 128 : r * 128 + 512, :] = x[:, 128:]
    lane = iota((funcs, 128), 1)
    for side, base, out in ((0, left, far_left), (1, right, far_right)):
        slot0, there0 = find(mine, base)
        slot1, there1 = find(mine, base + 1)
        weight = jnp.where(lane < 64, there0, there1)
        for t in range(0, 32, 2):
            parts = []
            for u in (t, t + 1):
                x0 = xs[side, pl.ds(slot0 * 32 + u, funcs, stride=128), :]
                x1 = xs[side, pl.ds(slot1 * 32 + u, funcs, stride=128), :]
                parts.append(jnp.where(lane < 64, x0, x1) * weight)
            out[t * funcs : (t + 2) * funcs, :] = jnp.concatenate(parts, axis=0).astype(BF)


def choose(count, far_rows, win, g_self, g_before, g_after, g_far, out):
    d = lax.axis_index("row")
    atoms = 2 * count
    mine = window_at(win, d)
    theirs = window_at(win, near(d, -1, count))
    row0 = near(d, -2, count) * 2
    col0 = column_chunk(d, count) * 4

    def position(atom, start):
        return lax.rem(atom - start + atoms, atoms) * 32

    def whole(base):
        blocks = []
        for c in range(2):
            at = base + 64 * c
            blocks.append(
                jnp.concatenate(
                    [
                        g_far[far_rows + at : far_rows + at + 64, :],
                        g_before[at : at + 64, :],
                        g_self[at : at + 64, :],
                        g_after[at : at + 64, :],
                    ],
                    axis=0,
                )
            )
        return jnp.concatenate(blocks, axis=1)

    occ, virt = whole(0), whole(128)
    rows_mine = [position(a, row0) for a in mine]
    rows_theirs = [position(a, row0) for a in theirs]
    columns_mine = [position(a, col0) for a in mine]
    columns_both = []
    for i in range(4):
        _, there = find(theirs, mine[i])
        columns_both.append(jnp.where(there > 0, columns_mine[i], jnp.int32(MISSING)))
    for base, rows, columns in ((0, rows_mine, columns_mine), (256, rows_theirs, columns_both)):
        left = one_hot((128, 256), 0, columns)
        x = dot_t(left, occ).astype(BF)
        out[base : base + 128, :] = dot(x, one_hot((256, 128), 1, rows)).astype(BF)
        y = dot(one_hot((128, 256), 0, rows), virt).astype(BF)
        out[base + 128 : base + 256, :] = dot(y, one_hot((256, 128), 1, columns)).astype(BF)


def frame_map(atoms_from, wanted):
    bases = []
    for w in wanted:
        slot, there = find(atoms_from, w)
        bases.append(jnp.where(there > 0, slot * 32, jnp.int32(MISSING)))
    return one_hot((128, 128), 1, bases)


def dress_own(count, win, tiles, tensor, g0, g1, polar0, flat, dressed, far_l, far_r, hs, ms):
    d = lax.axis_index("row")
    funcs = tensor.shape[1]
    mine = window_at(win, d)
    theirs = window_at(win, near(d, -1, count))
    mask = tile_mask(tiles, 32).astype(BF)
    occ = jnp.concatenate([g0[0:128, :], g1[0:128, :]], axis=0)

    def halves(i, carry):
        at = pl.multiple_of(i * 256, 256)
        m0 = tensor[0, 2 * i] * mask
        m1 = tensor[0, 2 * i + 1] * mask
        ms[pl.ds(at, 128), :] = m0.astype(F32)
        ms[pl.ds(at + 128, 128), :] = m1.astype(F32)
        h = dot(occ, jnp.concatenate([m0, m1], axis=1)).astype(BF).astype(F32)
        hs[0, pl.ds(at, 128), :] = h[:128, :128]
        hs[0, pl.ds(at + 128, 128), :] = h[:128, 128:]
        hs[1, pl.ds(at, 128), :] = h[128:, :128]
        hs[1, pl.ds(at + 128, 128), :] = h[128:, 128:]
        return carry

    lax.fori_loop(0, funcs // 2, halves, 0, unroll=2)

    def rows_at(ref, g, start):
        return [ref[g, pl.ds(start + t, funcs, stride=128), :] for t in range(8)]

    virt_a = g0[128:256, :]

    def same_frame(i, total):
        start = pl.multiple_of(i * 8, 8)
        x = dot(jnp.concatenate(rows_at(hs, 0, start), axis=0).astype(BF), virt_a).astype(BF)
        left = jnp.concatenate([x[t * funcs : (t + 1) * funcs] for t in range(8)], axis=1)
        right = jnp.concatenate(
            [ms[pl.ds(start + t, funcs, stride=128), :].astype(BF) for t in range(8)], axis=1
        )
        flat[:, pl.ds(pl.multiple_of(i * 1024, 1024), 1024)] = right
        return total + dot_t(left, right)

    polar0[...] = lax.fori_loop(0, 16, same_frame, jnp.zeros((funcs, funcs), F32))

    to_theirs = frame_map(mine, theirs)
    virts = [g0[128:256, :], g1[128:256, :]]
    slots = [find(mine, a) for a in theirs]
    for g in range(2):
        virt_b = dot(virts[g], to_theirs).astype(BF)

        def their_frame(i, carry):
            j = i >> 2
            slot = pick4(j, [s for s, _ in slots])
            there = pick4(j, [w for _, w in slots])
            start = slot * 32 + (i & 3) * 8
            rows = jnp.concatenate(rows_at(hs, g, start), axis=0) * there
            x = dot(rows.astype(BF), virt_b).astype(BF)
            block = jnp.concatenate([x[t * funcs : (t + 1) * funcs] for t in range(8)], axis=1)
            dressed[g * funcs : (g + 1) * funcs, pl.ds(pl.multiple_of(i * 1024, 1024), 1024)] = block
            return carry

        lax.fori_loop(0, 16, their_frame, 0)

        for by, out in ((-1, far_l), (1, far_r)):
            base = near(d, by, count) * 2
            pair = [base, base + 1, base, base + 1]
            two = dot(virts[g], frame_map(mine, pair)).astype(BF)
            lane = iota((128, 128), 1)
            zero = jnp.zeros((128, 128), BF)
            both = jnp.concatenate(
                [jnp.where(lane < 64, two, zero), jnp.where(lane < 64, zero, two)], axis=0
            )
            slot0, there0 = find(mine, base)
            slot1, there1 = find(mine, base + 1)

            def far_frame(i, carry):
                x0 = jnp.concatenate(rows_at(hs, g, slot0 * 32 + i * 8), axis=0) * there0
                x1 = jnp.concatenate(rows_at(hs, g, slot1 * 32 + i * 8), axis=0) * there1
                x = dot(jnp.concatenate([x0, x1], axis=1).astype(BF), both).astype(BF)
                block = jnp.concatenate([x[t * funcs : (t + 1) * funcs] for t in range(8)], axis=1)
                out[g * funcs : (g + 1) * funcs, pl.ds(pl.multiple_of(i * 1024, 1024), 1024)] = block
                return carry

            lax.fori_loop(0, 4, far_frame, 0)


def join(tensor, g_before, g0, g1, flat, dressed, far_l, far_r, from_left, from_right, own, other, up0, up1, hs, ms):
    funcs = tensor.shape[0]
    full = 2 * funcs
    short = g_before[256:272, :].astype(F32)
    mask = jnp.concatenate(
        [jnp.broadcast_to(short[4 * i : 4 * i + 1, :], (32, 128)) for i in range(4)], axis=0
    ).astype(BF)
    occ = jnp.concatenate([g0[256:384, :], g1[256:384, :]], axis=0)
    virts = [g0[384:512, :], g1[384:512, :]]

    def halves(i, carry):
        at = pl.multiple_of(i * 256, 256)
        m0 = tensor[2 * i] * mask
        m1 = tensor[2 * i + 1] * mask
        ms[pl.ds(at, 128), :] = m0.astype(F32)
        ms[pl.ds(at + 128, 128), :] = m1.astype(F32)
        h = dot(occ, jnp.concatenate([m0, m1], axis=1)).astype(BF).astype(F32)
        hs[0, pl.ds(at, 128), :] = h[:128, :128]
        hs[0, pl.ds(at + 128, 128), :] = h[:128, 128:]
        hs[1, pl.ds(at, 128), :] = h[128:, :128]
        hs[1, pl.ds(at + 128, 128), :] = h[128:, 128:]
        return carry

    lax.fori_loop(0, funcs // 2, halves, 0, unroll=2)

    def bands(i, carry):
        down, up = carry
        start = pl.multiple_of(i * 8, 8)
        columns = pl.ds(pl.multiple_of(i * 1024, 1024), 1024)
        xs = []
        for g in range(2):
            rows = [hs[g, pl.ds(start + t, funcs, stride=128), :] for t in range(8)]
            xs.append(dot(jnp.concatenate(rows, axis=0).astype(BF), virts[g]))
        left = jnp.concatenate(
            [
                jnp.concatenate([x[t * funcs : (t + 1) * funcs] for x in xs], axis=0).astype(BF)
                for t in range(8)
            ],
            axis=1,
        )
        right = jnp.concatenate(
            [ms[pl.ds(start + t, funcs, stride=128), :] for t in range(8)], axis=1
        ).astype(BF)
        return down + dot_t(dressed[:, columns], right), up + dot_t(left, flat[:, columns])

    down, up = lax.fori_loop(
        0, 16, bands, (jnp.zeros((2 * full, funcs), F32), jnp.zeros((full, full), F32))
    )

    def far(dressed_far, e):
        total = jnp.zeros((2 * full, funcs), F32)
        for i in range(4):
            rows = e[i * 8 * funcs : (i + 1) * 8 * funcs, :].astype(F32)
            right = jnp.concatenate([rows[t * funcs : (t + 1) * funcs] for t in range(8)], axis=1)
            total = total + dot_t(dressed_far[:, i * 1024 : (i + 1) * 1024], right.astype(BF))
        return total

    parts = jnp.concatenate(
        [far(far_l, from_left), down, far(far_r, from_right), jnp.zeros((2 * full, 128 - 3 * funcs), F32)], axis=1
    )
    own[...] = parts[:full]
    other[...] = parts[full:]
    up = jnp.concatenate([up, jnp.zeros((full, 128 - full), F32)], axis=1)
    up0[...] = up[:funcs]
    up1[...] = up[funcs:]


def assemble(polar0, own, recv, up0, up1, out):
    first = lax.rem(lax.axis_index("grp"), 2) == 0
    full = polar0.shape[0]
    funcs = full // 2
    a, b = own[...], recv[...]
    low, high = jnp.where(first, a, b), jnp.where(first, b, a)
    c, e = up0[...], up1[...]
    after = jnp.concatenate([jnp.where(first, c, e), jnp.where(first, e, c)], axis=0)
    pieces = []
    for i in range(3):
        part = slice(i * funcs, (i + 1) * funcs)
        if i == 2:
            pieces += [polar0[...], after[:, :full]]
        pieces += [low[:, part], high[:, part]]
    out[...] = jnp.concatenate(pieces, axis=1)


def vmem(count):
    return [pl.BlockSpec(memory_space=pltpu.VMEM)] * count


def smem(count):
    return [pl.BlockSpec(memory_space=pltpu.SMEM)] * count


def call(kernel, name, specs, outs, args, scratch=(), flops=0, moved=0):
    return pl.pallas_call(
        kernel,
        name=name,
        in_specs=specs,
        out_specs=tuple(vmem(len(outs))),
        out_shape=tuple(outs),
        scratch_shapes=list(scratch),
        compiler_params=pltpu.CompilerParams(vmem_limit_bytes=40 << 20),
        cost_estimate=pl.CostEstimate(flops=flops, bytes_accessed=moved, transcendentals=0),
    )(*args)


def body(groups, count, green_occ, green_virt, coulomb3c, tile_list, window):
    full = coulomb3c.shape[1]
    funcs = full // 2
    shape = jax.ShapeDtypeStruct
    half = lax.rem(lax.axis_index("grp"), 2)
    tensor = lax.dynamic_slice_in_dim(coulomb3c[0], half * funcs, funcs, 0)

    def send(array, row_by, swap=False):
        pairs = []
        for g in range(groups):
            for d in range(count):
                to = (g ^ 1 if swap else g) * count + (d + row_by) % count
                pairs.append((g * count + d, to))
        return lax.ppermute(array, ("grp", "row"), pairs)

    wide = send(tensor, 1)
    far_rows = funcs * 32
    g_self, g_right, g_left, far_right, far_left = call(
        functools.partial(prepare, count),
        "prepare",
        smem(2) + vmem(3),
        [
            shape((256, 128), BF),
            shape((272, 128), BF),
            shape((256, 128), BF),
            shape((far_rows + 256, 128), BF),
            shape((far_rows, 128), BF),
        ],
        (window, tile_list, green_occ, green_virt, tensor),
        [pltpu.VMEM((2, funcs * 128, 128), F32)],
        flops=2 * funcs * 128 * 128 * 256,
        moved=2 << 20,
    )
    g_before = send(g_right, 1)
    g_after = send(g_left, -1)
    from_left = send(far_right, 2)
    from_right = send(far_left, -2)
    (mine,) = call(
        functools.partial(choose, count, far_rows),
        "choose",
        smem(1) + vmem(4),
        [shape((512, 128), BF)],
        (window, g_self, g_before, g_after, from_left),
        flops=1 << 25,
        moved=1 << 19,
    )
    partner = send(mine, 0, True)
    polar0, flat, dressed, far_l, far_r = call(
        functools.partial(dress_own, count),
        "dress_own",
        smem(2) + vmem(3),
        [
            shape((full, full), F32),
            shape((full, 128 * 128), BF),
            shape((2 * full, 128 * 128), BF),
            shape((2 * full, 32 * 128), BF),
            shape((2 * full, 32 * 128), BF),
        ],
        (window, tile_list, coulomb3c, mine, partner),
        [pltpu.VMEM((2, full * 128, 128), F32), pltpu.VMEM((full * 128, 128), F32)],
        flops=1 << 31,
        moved=10 << 20,
    )
    own, other, up0, up1 = call(
        join,
        "join",
        vmem(10),
        [
            shape((full, 128), F32),
            shape((full, 128), F32),
            shape((funcs, 128), F32),
            shape((funcs, 128), F32),
        ],
        (wide, g_before, mine, partner, flat, dressed, far_l, far_r, from_left, from_right),
        [pltpu.VMEM((2, funcs * 128, 128), F32), pltpu.VMEM((funcs * 128, 128), F32)],
        flops=1 << 30,
        moved=8 << 20,
    )
    recv = send(other, 0, True)
    after0 = send(up0, -1)
    after1 = send(up1, -1, True)
    (out,) = call(
        assemble,
        "assemble",
        vmem(5),
        [shape((full, 5 * full), F32)],
        (polar0, own, recv, after0, after1),
        moved=1 << 17,
    )
    return out


def solution(mesh):
    placed = (
        P(("grp", "row"), None),
        P(("grp", "row"), None),
        P("row", None, None, None),
        P("row", None, None),
        P(),
    )
    return jax.shard_map(
        functools.partial(body, mesh.shape["grp"], mesh.shape["row"]),
        mesh=mesh,
        in_specs=placed,
        out_specs=P(("grp", "row"), None),
        check_vma=False,
    )
```

```python
import functools

import jax
import jax.numpy as jnp
from jax import lax
from jax.experimental import pallas as pl
from jax.experimental.pallas import tpu as pltpu
from jax.sharding import PartitionSpec as P

BF = jnp.bfloat16
F32 = jnp.float32
MISSING = -(1 << 20)


def dot(a, b):
    return lax.dot_general(a, b, (((1,), (0,)), ((), ())), preferred_element_type=F32)


def dot_t(a, b):
    return lax.dot_general(a, b, (((1,), (1,)), ((), ())), preferred_element_type=F32)


def iota(shape, dim):
    return lax.broadcasted_iota(jnp.int32, shape, dim)


def pick4(index, values):
    return jnp.where(
        index == 0, values[0], jnp.where(index == 1, values[1], jnp.where(index == 2, values[2], values[3]))
    )


def one_hot(shape, dim, bases):
    index = iota(shape, dim)
    position = pick4(index >> 5, bases) + (index & 31)
    return jnp.where(iota(shape, 1 - dim) == position, 1.0, 0.0).astype(BF)


def window_at(win, row):
    return [win[row, i] for i in range(4)]


def find(atoms, wanted):
    slot, there = jnp.int32(0), jnp.float32(0)
    for i in range(4):
        hit = atoms[i] == wanted
        slot = jnp.where(hit, jnp.int32(i), slot)
        there = jnp.where(hit, jnp.float32(1), there)
    return slot, there


def tile_mask(tiles, rows):
    shape = (4 * rows, 128)
    row, lane = iota(shape, 0) // rows, iota(shape, 1) >> 5
    mask = jnp.zeros(shape, F32)
    for i in range(4):
        for j in range(4):
            mask = jnp.where((row == i) & (lane == j), tiles[0, i, j].astype(F32), mask)
    return mask


def near(row, by, count):
    return lax.rem(row + by + count, count)


def column_chunk(row, count):
    return near(row, -1, count) >> 1


def spread(count, win, occ, virt, g_self, g_right, g_left, g_far):
    d = lax.axis_index("row")

    def greens(out, dest):
        first = column_chunk(dest, count)
        for c in range(2):
            chunk = lax.rem(first + c, count // 2)
            columns = pl.ds(pl.multiple_of(chunk * 128, 128), 128)
            out[64 * c : 64 * c + 64, :] = occ[:, columns]
            out[128 + 64 * c : 192 + 64 * c, :] = virt[:, columns]

    greens(g_self, d)
    greens(g_right, near(d, 1, count))
    greens(g_left, near(d, -1, count))
    greens(g_far, near(d, 2, count))


def mask_half(tiles, coulomb, token, tensor, sem):
    funcs = tensor.shape[0]
    half = lax.rem(lax.axis_index("grp"), 2)
    copy = pltpu.make_async_copy(coulomb.at[0, pl.ds(half * funcs, funcs)], tensor, sem)
    copy.start()
    mask = tile_mask(tiles, 32).astype(BF)
    copy.wait()
    tensor[...] = tensor[...] * mask[None]


def far_tiles(count, win, half, far_right, far_left, xs):
    d = lax.axis_index("row")
    mine = window_at(win, d)
    funcs = half.shape[0]
    left, right = near(d, -1, count) * 2, near(d, 1, count) * 2
    shape = (128, 256)
    column = iota(shape, 1)
    wanted = jnp.where(column < 128, left, right) + ((column >> 5) & 1)
    here = pick4(iota(shape, 0) >> 5, mine)
    same = (here == wanted) & ((iota(shape, 0) & 31) == (column & 31))
    select = jnp.where(same, 1.0, 0.0).astype(BF)
    for r in range(0, funcs, 4):
        block = half[r : r + 4].reshape(512, 128)
        x = dot(block, select)
        xs[0, r * 128 : r * 128 + 512, :] = x[:, :128]
        xs[1, r * 128 : r * 128 + 512, :] = x[:, 128:]
    lane = iota((funcs, 128), 1)
    for side, base, out in ((0, left, far_left), (1, right, far_right)):
        slot0, there0 = find(mine, base)
        slot1, there1 = find(mine, base + 1)
        weight = jnp.where(lane < 64, there0, there1)
        for t in range(0, 32, 2):
            parts = []
            for u in (t, t + 1):
                x0 = xs[side, pl.ds(slot0 * 32 + u, funcs, stride=128), :]
                x1 = xs[side, pl.ds(slot1 * 32 + u, funcs, stride=128), :]
                parts.append(jnp.where(lane < 64, x0, x1) * weight)
            out[t * funcs : (t + 2) * funcs, :] = jnp.concatenate(parts, axis=0).astype(BF)


def choose(count, win, g_self, g_before, g_after, g_far, out):
    d = lax.axis_index("row")
    atoms = 2 * count
    mine = window_at(win, d)
    theirs = window_at(win, near(d, -1, count))
    row0 = near(d, -2, count) * 2
    col0 = column_chunk(d, count) * 4

    def position(atom, start):
        return lax.rem(atom - start + atoms, atoms) * 32

    def whole(base):
        blocks = []
        for c in range(2):
            at = base + 64 * c
            blocks.append(
                jnp.concatenate(
                    [
                        g_far[at : at + 64, :],
                        g_before[at : at + 64, :],
                        g_self[at : at + 64, :],
                        g_after[at : at + 64, :],
                    ],
                    axis=0,
                )
            )
        return jnp.concatenate(blocks, axis=1)

    occ, virt = whole(0), whole(128)
    rows_mine = [position(a, row0) for a in mine]
    rows_theirs = [position(a, row0) for a in theirs]
    columns_mine = [position(a, col0) for a in mine]
    columns_both = []
    for i in range(4):
        _, there = find(theirs, mine[i])
        columns_both.append(jnp.where(there > 0, columns_mine[i], jnp.int32(MISSING)))
    for base, rows, columns in ((0, rows_mine, columns_mine), (256, rows_theirs, columns_both)):
        left = one_hot((128, 256), 0, columns)
        x = dot_t(left, occ).astype(BF)
        out[base : base + 128, :] = dot(x, one_hot((256, 128), 1, rows)).astype(BF)
        y = dot(one_hot((128, 256), 0, rows), virt).astype(BF)
        out[base + 128 : base + 256, :] = dot(y, one_hot((256, 128), 1, columns)).astype(BF)


def frame_map(atoms_from, wanted):
    bases = []
    for w in wanted:
        slot, there = find(atoms_from, w)
        bases.append(jnp.where(there > 0, slot * 32, jnp.int32(MISSING)))
    return one_hot((128, 128), 1, bases)


def dress_own(count, win, tiles, tensor, g0, g1, polar0, flat, dressed, far_l, far_r, hs, ms):
    d = lax.axis_index("row")
    funcs = tensor.shape[1]
    mine = window_at(win, d)
    theirs = window_at(win, near(d, -1, count))
    mask = tile_mask(tiles, 32).astype(BF)
    occ = jnp.concatenate([g0[0:128, :], g1[0:128, :]], axis=0)

    def halves(i, carry):
        at = pl.multiple_of(i * 272, 8)
        m0 = tensor[0, 2 * i] * mask
        m1 = tensor[0, 2 * i + 1] * mask
        ms[pl.ds(at, 128), :] = m0.astype(F32)
        ms[pl.ds(at + 136, 128), :] = m1.astype(F32)
        h = dot(occ, jnp.concatenate([m0, m1], axis=1))
        hs[0, pl.ds(at, 128), :] = h[:128, :128]
        hs[0, pl.ds(at + 136, 128), :] = h[:128, 128:]
        hs[1, pl.ds(at, 128), :] = h[128:, :128]
        hs[1, pl.ds(at + 136, 128), :] = h[128:, 128:]
        return carry

    lax.fori_loop(0, funcs // 2, halves, 0, unroll=2)

    def rows_at(ref, g, start):
        return [ref[g, pl.ds(start + t, funcs, stride=136), :] for t in range(8)]

    virt_a = g0[128:256, :]

    def same_frame(i, total):
        start = pl.multiple_of(i * 8, 8)
        x = dot(jnp.concatenate(rows_at(hs, 0, start), axis=0).astype(BF), virt_a).astype(BF)
        left = jnp.concatenate([x[t * funcs : (t + 1) * funcs] for t in range(8)], axis=1)
        right = jnp.concatenate(
            [ms[pl.ds(start + t, funcs, stride=136), :].astype(BF) for t in range(8)], axis=1
        )
        flat[:, pl.ds(pl.multiple_of(i * 1024, 1024), 1024)] = right
        return total + dot_t(left, right)

    polar0[...] = lax.fori_loop(0, 16, same_frame, jnp.zeros((funcs, funcs), F32))

    to_theirs = frame_map(mine, theirs)
    virts = [g0[128:256, :], g1[128:256, :]]
    slots = [find(mine, a) for a in theirs]
    for g in range(2):
        virt_b = dot(virts[g], to_theirs).astype(BF)

        def their_frame(i, carry):
            j = i >> 2
            slot = pick4(j, [s for s, _ in slots])
            there = pick4(j, [w for _, w in slots])
            start = slot * 32 + (i & 3) * 8
            rows = jnp.concatenate(rows_at(hs, g, start), axis=0) * there
            x = dot(rows.astype(BF), virt_b).astype(BF)
            block = jnp.concatenate([x[t * funcs : (t + 1) * funcs] for t in range(8)], axis=1)
            dressed[g * funcs : (g + 1) * funcs, pl.ds(pl.multiple_of(i * 1024, 1024), 1024)] = block
            return carry

        lax.fori_loop(0, 16, their_frame, 0)

        for by, out in ((-1, far_l), (1, far_r)):
            base = near(d, by, count) * 2
            pair = [base, base + 1, base, base + 1]
            two = dot(virts[g], frame_map(mine, pair)).astype(BF)
            lane = iota((128, 128), 1)
            zero = jnp.zeros((128, 128), BF)
            both = jnp.concatenate(
                [jnp.where(lane < 64, two, zero), jnp.where(lane < 64, zero, two)], axis=0
            )
            slot0, there0 = find(mine, base)
            slot1, there1 = find(mine, base + 1)

            def far_frame(i, carry):
                x0 = jnp.concatenate(rows_at(hs, g, slot0 * 32 + i * 8), axis=0) * there0
                x1 = jnp.concatenate(rows_at(hs, g, slot1 * 32 + i * 8), axis=0) * there1
                x = dot(jnp.concatenate([x0, x1], axis=1).astype(BF), both).astype(BF)
                block = jnp.concatenate([x[t * funcs : (t + 1) * funcs] for t in range(8)], axis=1)
                out[g * funcs : (g + 1) * funcs, pl.ds(pl.multiple_of(i * 1024, 1024), 1024)] = block
                return carry

            lax.fori_loop(0, 4, far_frame, 0)


def join(tensor, g0, g1, flat, dressed, far_l, far_r, from_left, from_right, own, other, up0, up1, hs, ms):
    funcs = tensor.shape[0]
    full = 2 * funcs
    occ = jnp.concatenate([g0[256:384, :], g1[256:384, :]], axis=0)
    virts = [g0[384:512, :], g1[384:512, :]]

    def halves(i, carry):
        at = i * 258
        m0 = tensor[2 * i]
        m1 = tensor[2 * i + 1]
        ms[pl.ds(at, 128), :] = m0.astype(F32)
        ms[pl.ds(at + 129, 128), :] = m1.astype(F32)
        h = dot(occ, jnp.concatenate([m0, m1], axis=1))
        hs[0, pl.ds(at, 128), :] = h[:128, :128]
        hs[0, pl.ds(at + 129, 128), :] = h[:128, 128:]
        hs[1, pl.ds(at, 128), :] = h[128:, :128]
        hs[1, pl.ds(at + 129, 128), :] = h[128:, 128:]
        return carry

    lax.fori_loop(0, funcs // 2, halves, 0, unroll=2)

    def bands(i, carry):
        down, up = carry
        start = pl.multiple_of(i * 8, 8)
        columns = pl.ds(pl.multiple_of(i * 1024, 1024), 1024)
        xs = []
        for g in range(2):
            rows = [hs[g, pl.ds(start + t, funcs, stride=129), :] for t in range(8)]
            xs.append(dot(jnp.concatenate(rows, axis=0).astype(BF), virts[g]))
        left = jnp.concatenate(
            [
                jnp.concatenate([x[t * funcs : (t + 1) * funcs] for x in xs], axis=0).astype(BF)
                for t in range(8)
            ],
            axis=1,
        )
        right = jnp.concatenate(
            [ms[pl.ds(start + t, funcs, stride=129), :] for t in range(8)], axis=1
        ).astype(BF)
        return down + dot_t(dressed[:, columns], right), up + dot_t(left, flat[:, columns])

    down, up = lax.fori_loop(
        0, 16, bands, (jnp.zeros((2 * full, funcs), F32), jnp.zeros((full, full), F32))
    )

    def far(dressed_far, e):
        total = jnp.zeros((2 * full, funcs), F32)
        for i in range(4):
            rows = e[i * 8 * funcs : (i + 1) * 8 * funcs, :].astype(F32)
            right = jnp.concatenate([rows[t * funcs : (t + 1) * funcs] for t in range(8)], axis=1)
            total = total + dot_t(dressed_far[:, i * 1024 : (i + 1) * 1024], right.astype(BF))
        return total

    parts = jnp.concatenate(
        [far(far_l, from_left), down, far(far_r, from_right), jnp.zeros((2 * full, 128 - 3 * funcs), F32)], axis=1
    )
    own[...] = parts[:full]
    other[...] = parts[full:]
    up = jnp.concatenate([up, jnp.zeros((full, 128 - full), F32)], axis=1)
    up0[...] = up[:funcs]
    up1[...] = up[funcs:]


def assemble(polar0, own, recv, up0, up1, out):
    first = lax.rem(lax.axis_index("grp"), 2) == 0
    full = polar0.shape[0]
    funcs = full // 2
    a, b = own[...], recv[...]
    low, high = jnp.where(first, a, b), jnp.where(first, b, a)
    c, e = up0[...], up1[...]
    after = jnp.concatenate([jnp.where(first, c, e), jnp.where(first, e, c)], axis=0)
    pieces = []
    for i in range(3):
        part = slice(i * funcs, (i + 1) * funcs)
        if i == 2:
            pieces += [polar0[...], after[:, :full]]
        pieces += [low[:, part], high[:, part]]
    out[...] = jnp.concatenate(pieces, axis=1)


def vmem(count):
    return [pl.BlockSpec(memory_space=pltpu.VMEM)] * count


def smem(count):
    return [pl.BlockSpec(memory_space=pltpu.SMEM)] * count


def call(kernel, name, specs, outs, args, scratch=(), flops=0, moved=0):
    return pl.pallas_call(
        kernel,
        name=name,
        in_specs=specs,
        out_specs=tuple(vmem(len(outs))),
        out_shape=tuple(outs),
        scratch_shapes=list(scratch),
        compiler_params=pltpu.CompilerParams(vmem_limit_bytes=40 << 20),
        cost_estimate=pl.CostEstimate(flops=flops, bytes_accessed=moved, transcendentals=0),
    )(*args)


def body(groups, count, green_occ, green_virt, coulomb3c, tile_list, window):
    full = coulomb3c.shape[1]
    funcs = full // 2
    shape = jax.ShapeDtypeStruct

    def send(array, row_by, swap=False):
        pairs = []
        for g in range(groups):
            for d in range(count):
                to = (g ^ 1 if swap else g) * count + (d + row_by) % count
                pairs.append((g * count + d, to))
        return lax.ppermute(array, ("grp", "row"), pairs)

    far_rows = funcs * 32
    g_self, g_right, g_left, g_far = call(
        functools.partial(spread, count),
        "spread",
        smem(1) + vmem(2),
        [shape((256, 128), BF)] * 4,
        (window, green_occ, green_virt),
    )
    g_before = send(g_right, 1)
    g_after = send(g_left, -1)
    g_beyond = send(g_far, 2)
    (tensor,) = call(
        mask_half,
        "mask_half",
        smem(1) + [pl.BlockSpec(memory_space=pl.ANY)] * 2,
        [shape((funcs, 128, 128), BF)],
        (tile_list, coulomb3c, g_self),
        [pltpu.SemaphoreType.DMA],
    )
    wide = send(tensor, 1)
    far_right, far_left = call(
        functools.partial(far_tiles, count),
        "far_tiles",
        smem(1) + vmem(1),
        [shape((far_rows, 128), BF), shape((far_rows, 128), BF)],
        (window, tensor),
        [pltpu.VMEM((2, funcs * 128, 128), F32)],
        flops=1 << 36,
    )
    from_left = send(far_right, 2)
    from_right = send(far_left, -2)
    g_before, g_after, g_beyond, far_right, far_left = lax.optimization_barrier(
        (g_before, g_after, g_beyond, far_right, far_left)
    )
    (mine,) = call(
        functools.partial(choose, count),
        "choose",
        smem(1) + vmem(4),
        [shape((512, 128), BF)],
        (window, g_self, g_before, g_after, g_beyond),
    )
    partner = send(mine, 0, True)
    polar0, flat, dressed, far_l, far_r = call(
        functools.partial(dress_own, count),
        "dress_own",
        smem(2) + vmem(3),
        [
            shape((full, full), F32),
            shape((full, 128 * 128), BF),
            shape((2 * full, 128 * 128), BF),
            shape((2 * full, 32 * 128), BF),
            shape((2 * full, 32 * 128), BF),
        ],
        (window, tile_list, coulomb3c, mine, partner),
        [pltpu.VMEM((2, full * 136, 128), F32), pltpu.VMEM((full * 136, 128), F32)],
    )
    own, other, up0, up1 = call(
        join,
        "join",
        vmem(9),
        [
            shape((full, 128), F32),
            shape((full, 128), F32),
            shape((funcs, 128), F32),
            shape((funcs, 128), F32),
        ],
        (wide, mine, partner, flat, dressed, far_l, far_r, from_left, from_right),
        [pltpu.VMEM((2, funcs * 129, 128), F32), pltpu.VMEM((funcs * 129, 128), F32)],
    )
    recv = send(other, 0, True)
    after0 = send(up0, -1)
    after1 = send(up1, -1, True)
    (out,) = call(
        assemble,
        "assemble",
        vmem(5),
        [shape((full, 5 * full), F32)],
        (polar0, own, recv, after0, after1),
    )
    return out


def solution(mesh):
    placed = (
        P(("grp", "row"), None),
        P(("grp", "row"), None),
        P("row", None, None, None),
        P("row", None, None),
        P(),
    )
    return jax.shard_map(
        functools.partial(body, mesh.shape["grp"], mesh.shape["row"]),
        mesh=mesh,
        in_specs=placed,
        out_specs=P(("grp", "row"), None),
        check_vma=False,
    )
```

```python
import functools

import jax
import jax.numpy as jnp
from jax import lax
from jax.experimental import pallas as pl
from jax.experimental.pallas import tpu as pltpu
from jax.sharding import PartitionSpec as P

BF = jnp.bfloat16
F32 = jnp.float32
MISSING = -(1 << 20)


def dot(a, b):
    return lax.dot_general(a, b, (((1,), (0,)), ((), ())), preferred_element_type=F32)


def dot_t(a, b):
    return lax.dot_general(a, b, (((1,), (1,)), ((), ())), preferred_element_type=F32)


def iota(shape, dim):
    return lax.broadcasted_iota(jnp.int32, shape, dim)


def pick4(index, values):
    return jnp.where(
        index == 0, values[0], jnp.where(index == 1, values[1], jnp.where(index == 2, values[2], values[3]))
    )


def one_hot(shape, dim, bases):
    index = iota(shape, dim)
    position = pick4(index >> 5, bases) + (index & 31)
    return jnp.where(iota(shape, 1 - dim) == position, 1.0, 0.0).astype(BF)


def window_at(win, row):
    return [win[row, i] for i in range(4)]


def find(atoms, wanted):
    slot, there = jnp.int32(0), jnp.float32(0)
    for i in range(4):
        hit = atoms[i] == wanted
        slot = jnp.where(hit, jnp.int32(i), slot)
        there = jnp.where(hit, jnp.float32(1), there)
    return slot, there


def tile_mask(tiles, rows):
    shape = (4 * rows, 128)
    row, lane = iota(shape, 0) // rows, iota(shape, 1) >> 5
    mask = jnp.zeros(shape, F32)
    for i in range(4):
        for j in range(4):
            mask = jnp.where((row == i) & (lane == j), tiles[0, i, j].astype(F32), mask)
    return mask


def near(row, by, count):
    return lax.rem(row + by + count, count)


def column_chunk(row, count):
    return near(row, -1, count) >> 1


def spread(count, occ, virt, g_self, g_right, g_left, g_far, sem):
    d = lax.axis_index("row")
    copies = []
    for out, by in ((g_right, 1), (g_left, -1), (g_far, 2), (g_self, 0)):
        first = column_chunk(near(d, by, count), count)
        for c in range(2):
            chunk = lax.rem(first + c, count // 2)
            columns = pl.ds(pl.multiple_of(chunk * 128, 128), 128)
            for base, green in ((0, occ), (128, virt)):
                at = base + 64 * c
                copies.append(
                    pltpu.make_async_copy(green.at[:, columns], out.at[at : at + 64], sem.at[len(copies)])
                )
    for copy in copies:
        copy.start()
    for copy in copies:
        copy.wait()


def mask_half(tiles, coulomb, token, tensor, sem):
    funcs = tensor.shape[0]
    half = lax.rem(lax.axis_index("grp"), 2)
    copy = pltpu.make_async_copy(coulomb.at[0, pl.ds(half * funcs, funcs)], tensor, sem)
    copy.start()
    mask = tile_mask(tiles, 32).astype(BF)
    copy.wait()
    tensor[...] = tensor[...] * mask[None]


def far_tiles(count, win, half, far_right, far_left, xs):
    d = lax.axis_index("row")
    mine = window_at(win, d)
    funcs = half.shape[0]
    left, right = near(d, -1, count) * 2, near(d, 1, count) * 2
    shape = (128, 256)
    column = iota(shape, 1)
    wanted = jnp.where(column < 128, left, right) + ((column >> 5) & 1)
    here = pick4(iota(shape, 0) >> 5, mine)
    same = (here == wanted) & ((iota(shape, 0) & 31) == (column & 31))
    select = jnp.where(same, 1.0, 0.0).astype(BF)
    for r in range(0, funcs, 4):
        block = half[r : r + 4].reshape(512, 128)
        x = dot(block, select)
        xs[0, r * 128 : r * 128 + 512, :] = x[:, :128]
        xs[1, r * 128 : r * 128 + 512, :] = x[:, 128:]
    lane = iota((funcs, 128), 1)
    for side, base, out in ((0, left, far_left), (1, right, far_right)):
        slot0, there0 = find(mine, base)
        slot1, there1 = find(mine, base + 1)
        weight = jnp.where(lane < 64, there0, there1)
        for t in range(0, 32, 2):
            parts = []
            for u in (t, t + 1):
                x0 = xs[side, pl.ds(slot0 * 32 + u, funcs, stride=128), :]
                x1 = xs[side, pl.ds(slot1 * 32 + u, funcs, stride=128), :]
                parts.append(jnp.where(lane < 64, x0, x1) * weight)
            out[t * funcs : (t + 2) * funcs, :] = jnp.concatenate(parts, axis=0).astype(BF)


def choose(count, win, g_self, g_before, g_after, g_far, out):
    d = lax.axis_index("row")
    atoms = 2 * count
    mine = window_at(win, d)
    theirs = window_at(win, near(d, -1, count))
    row0 = near(d, -2, count) * 2
    col0 = column_chunk(d, count) * 4

    def position(atom, start):
        return lax.rem(atom - start + atoms, atoms) * 32

    def whole(base):
        blocks = []
        for c in range(2):
            at = base + 64 * c
            blocks.append(
                jnp.concatenate(
                    [
                        g_far[at : at + 64, :],
                        g_before[at : at + 64, :],
                        g_self[at : at + 64, :],
                        g_after[at : at + 64, :],
                    ],
                    axis=0,
                )
            )
        return jnp.concatenate(blocks, axis=1)

    occ, virt = whole(0), whole(128)
    rows_mine = [position(a, row0) for a in mine]
    rows_theirs = [position(a, row0) for a in theirs]
    columns_mine = [position(a, col0) for a in mine]
    columns_both = []
    for i in range(4):
        _, there = find(theirs, mine[i])
        columns_both.append(jnp.where(there > 0, columns_mine[i], jnp.int32(MISSING)))
    for base, rows, columns in ((0, rows_mine, columns_mine), (256, rows_theirs, columns_both)):
        left = one_hot((128, 256), 0, columns)
        x = dot_t(left, occ).astype(BF)
        out[base : base + 128, :] = dot(x, one_hot((256, 128), 1, rows)).astype(BF)
        y = dot(one_hot((128, 256), 0, rows), virt).astype(BF)
        out[base + 128 : base + 256, :] = dot(y, one_hot((256, 128), 1, columns)).astype(BF)


def frame_map(atoms_from, wanted):
    bases = []
    for w in wanted:
        slot, there = find(atoms_from, w)
        bases.append(jnp.where(there > 0, slot * 32, jnp.int32(MISSING)))
    return one_hot((128, 128), 1, bases)


PITCH = 136


def halves(occ, blocks, outs, ms):
    rows = occ.shape[0] // len(outs)
    for i in range(0, len(blocks), 2):
        m0, m1 = blocks[i](), blocks[i + 1]()
        if ms is not None:
            ms[i * PITCH : i * PITCH + 128, :] = m0.astype(F32)
            ms[(i + 1) * PITCH : (i + 1) * PITCH + 128, :] = m1.astype(F32)
        h = dot(occ, jnp.concatenate([m0, m1], axis=1))
        for n, out in enumerate(outs):
            part = h[n * rows : (n + 1) * rows]
            out[i * PITCH : i * PITCH + 128, :] = part[:, :128]
            out[(i + 1) * PITCH : (i + 1) * PITCH + 128, :] = part[:, 128:]


def gather(ref, funcs, start):
    return [ref[pl.ds(start + t, funcs, stride=PITCH), :] for t in range(8)]


def dress(count, own, win, tiles, tensor, greens, *refs):
    if own:
        polar0, flat, dressed, far, hs, ms, same = refs
    else:
        (dressed, far, hs), ms = refs, None
    d = lax.axis_index("row")
    funcs = tensor.shape[1]
    mine = window_at(win, d)
    theirs = window_at(win, near(d, -1, count))
    left, right = near(d, -1, count) * 2, near(d, 1, count) * 2
    mask = tile_mask(tiles, 32).astype(BF)
    occ, virt = greens[0:128, :], greens[128:256, :]
    halves(occ, [functools.partial(lambda r: tensor[0, r] * mask, r) for r in range(funcs)], [hs], ms)
    frames = [
        dot(virt, frame_map(mine, theirs)).astype(BF),
        dot(virt, frame_map(mine, [left, left + 1, right, right + 1])).astype(BF),
    ]
    outs = [dressed, far]
    if own:
        frames, outs = [virt] + frames, [same] + outs
    wide = jnp.concatenate(frames, axis=1)
    for i in range(16):
        x = dot(jnp.concatenate(gather(hs, funcs, i * 8), axis=0).astype(BF), wide)
        for t in range(8):
            at = (i * 8 + t) * 128
            block = x[t * funcs : (t + 1) * funcs].astype(BF)
            for n, out in enumerate(outs):
                out[:, at : at + 128] = block[:, n * 128 : (n + 1) * 128]
        if own:
            for t, rows in enumerate(gather(ms, funcs, i * 8)):
                at = (i * 8 + t) * 128
                flat[:, at : at + 128] = rows.astype(BF)
    if own:
        polar0[...] = dot_t(same[...], flat[...])


def join(
    count,
    win,
    tensor,
    g0,
    g1,
    flat,
    dressed0,
    dressed1,
    far0,
    far1,
    from_left,
    from_right,
    own,
    other,
    up0,
    up1,
    hs0,
    hs1,
    ms,
    backs,
    moved,
    tiles_far,
):
    d = lax.axis_index("row")
    funcs = tensor.shape[0]
    full = 2 * funcs
    mine = window_at(win, d)
    theirs = window_at(win, near(d, -1, count))
    left, right = near(d, -1, count), near(d, 1, count)
    occ = jnp.concatenate([g0[256:384, :], g1[256:384, :]], axis=0)
    halves(occ, [functools.partial(lambda r: tensor[r], r) for r in range(funcs)], [hs0, hs1], ms)
    virts = [g0[384:512, :], g1[384:512, :]]
    lane = iota((funcs, 128), 1)
    for i in range(16):
        slot, there = find(theirs, mine[i // 4])
        xs = []
        for hs, virt in zip((hs0, hs1), virts):
            xs.append(dot(jnp.concatenate(gather(hs, funcs, i * 8), axis=0).astype(BF), virt))
        rows = gather(ms, funcs, slot * 32 + (i % 4) * 8)
        for t in range(8):
            at = (i * 8 + t) * 128
            part = slice(t * funcs, (t + 1) * funcs)
            backs[:, at : at + 128] = jnp.concatenate([x[part] for x in xs], axis=0).astype(BF)
            moved[:, at : at + 128] = (rows[t] * there).astype(BF)
    for t in range(0, 32, 2):
        pair = slice(t * funcs, (t + 2) * funcs)
        for side, e, row in ((0, from_left, left), (1, from_right, right)):
            both = e[pair, :].astype(F32)
            for u in range(2):
                x = both[u * funcs : (u + 1) * funcs]
                turned = pltpu.roll(x, 64, 1)
                for i in range(4):
                    odd = lax.rem(mine[i], 2)
                    here = (lane < 64) if side == 0 else (lane >= 64)
                    value = jnp.where(odd == side, x, turned)
                    at = (i * 32 + t + u) * 128
                    kept = here & (jnp.broadcast_to(mine[i] >> 1, lane.shape) == row)
                    tiles_far[side, :, at : at + 128] = jnp.where(kept, value, 0.0).astype(BF)
    up = dot_t(backs[...], flat[...])
    up = jnp.concatenate([up, jnp.zeros((full, 128 - full), F32)], axis=1)
    up0[...] = up[:funcs]
    up1[...] = up[funcs:]
    for dressed, far, out in ((dressed0, far0, own), (dressed1, far1, other)):
        far_dressed = far[...]
        out[...] = jnp.concatenate(
            [
                dot_t(far_dressed, tiles_far[0]),
                dot_t(dressed[...], moved[...]),
                dot_t(far_dressed, tiles_far[1]),
                jnp.zeros((full, 128 - 3 * funcs), F32),
            ],
            axis=1,
        )


def assemble(polar0, own, recv, up0, up1, out):
    first = lax.rem(lax.axis_index("grp"), 2) == 0
    full = polar0.shape[0]
    funcs = full // 2
    a, b = own[...], recv[...]
    low, high = jnp.where(first, a, b), jnp.where(first, b, a)
    c, e = up0[...], up1[...]
    after = jnp.concatenate([jnp.where(first, c, e), jnp.where(first, e, c)], axis=0)
    pieces = []
    for i in range(3):
        part = slice(i * funcs, (i + 1) * funcs)
        if i == 2:
            pieces += [polar0[...], after[:, :full]]
        pieces += [low[:, part], high[:, part]]
    out[...] = jnp.concatenate(pieces, axis=1)


def vmem(count):
    return [pl.BlockSpec(memory_space=pltpu.VMEM)] * count


def hbm(count):
    return [pl.BlockSpec(memory_space=pltpu.HBM)] * count


def smem(count):
    return [pl.BlockSpec(memory_space=pltpu.SMEM)] * count


def call(kernel, name, specs, outs, args, scratch=(), flops=0, moved=0):
    return pl.pallas_call(
        kernel,
        name=name,
        in_specs=specs,
        out_specs=tuple(vmem(len(outs))),
        out_shape=tuple(outs),
        scratch_shapes=list(scratch),
        compiler_params=pltpu.CompilerParams(vmem_limit_bytes=40 << 20),
        cost_estimate=pl.CostEstimate(flops=flops, bytes_accessed=moved, transcendentals=0),
    )(*args)


def body(groups, count, green_occ, green_virt, coulomb3c, tile_list, window):
    full = coulomb3c.shape[1]
    funcs = full // 2
    shape = jax.ShapeDtypeStruct

    def send(array, row_by, swap=False):
        pairs = []
        for g in range(groups):
            for d in range(count):
                to = (g ^ 1 if swap else g) * count + (d + row_by) % count
                pairs.append((g * count + d, to))
        return lax.ppermute(array, ("grp", "row"), pairs)

    far_rows = funcs * 32
    g_self, g_right, g_left, g_far = call(
        functools.partial(spread, count),
        "spread",
        hbm(2),
        [shape((256, 128), BF)] * 4,
        (green_occ, green_virt),
        [pltpu.SemaphoreType.DMA((16,))],
    )
    g_before = send(g_right, 1)
    g_after = send(g_left, -1)
    g_beyond = send(g_far, 2)
    (tensor,) = call(
        mask_half,
        "mask_half",
        smem(1) + hbm(1) + [pl.BlockSpec(memory_space=pl.ANY)],
        [shape((funcs, 128, 128), BF)],
        (tile_list, coulomb3c, g_self),
        [pltpu.SemaphoreType.DMA],
    )
    wide = send(tensor, 1)
    far_right, far_left = call(
        functools.partial(far_tiles, count),
        "far_tiles",
        smem(1) + vmem(1),
        [shape((far_rows, 128), BF), shape((far_rows, 128), BF)],
        (window, tensor),
        [pltpu.VMEM((2, funcs * 128, 128), F32)],
        flops=1 << 36,
    )
    from_left = send(far_right, 2)
    from_right = send(far_left, -2)
    g_before, g_after, g_beyond, far_right, far_left = lax.optimization_barrier(
        (g_before, g_after, g_beyond, far_right, far_left)
    )
    (mine,) = call(
        functools.partial(choose, count),
        "choose",
        smem(1) + vmem(4),
        [shape((512, 128), BF)],
        (window, g_self, g_before, g_after, g_beyond),
    )
    partner = send(mine, 0, True)
    flat_shape = shape((full, 128 * 128), BF)
    tall = pltpu.VMEM((full * PITCH, 128), F32)
    polar0, flat, dressed0, far0 = call(
        functools.partial(dress, count, True),
        "dress_own",
        smem(2) + vmem(2),
        [shape((full, full), F32), flat_shape, flat_shape, flat_shape],
        (window, tile_list, coulomb3c, mine),
        [tall, tall, pltpu.VMEM((full, 128 * 128), BF)],
    )
    dressed1, far1 = call(
        functools.partial(dress, count, False),
        "dress_partner",
        smem(2) + vmem(2),
        [flat_shape, flat_shape],
        (window, tile_list, coulomb3c, partner),
        [tall],
    )
    short = pltpu.VMEM((funcs * PITCH, 128), F32)
    own, other, up0, up1 = call(
        functools.partial(join, count),
        "join",
        smem(1) + vmem(10),
        [
            shape((full, 128), F32),
            shape((full, 128), F32),
            shape((funcs, 128), F32),
            shape((funcs, 128), F32),
        ],
        (window, wide, mine, partner, flat, dressed0, dressed1, far0, far1, from_left, from_right),
        [
            short,
            short,
            short,
            pltpu.VMEM((full, 128 * 128), BF),
            pltpu.VMEM((funcs, 128 * 128), BF),
            pltpu.VMEM((2, funcs, 128 * 128), BF),
        ],
    )
    recv = send(other, 0, True)
    after0 = send(up0, -1)
    after1 = send(up1, -1, True)
    (out,) = call(
        assemble,
        "assemble",
        vmem(5),
        [shape((full, 5 * full), F32)],
        (polar0, own, recv, after0, after1),
    )
    return out


def solution(mesh):
    placed = (
        P(("grp", "row"), None),
        P(("grp", "row"), None),
        P("row", None, None, None),
        P("row", None, None),
        P(),
    )
    return jax.shard_map(
        functools.partial(body, mesh.shape["grp"], mesh.shape["row"]),
        mesh=mesh,
        in_specs=placed,
        out_specs=P(("grp", "row"), None),
        check_vma=False,
    )
```

```python
import functools

import jax
import jax.numpy as jnp
from jax import lax
from jax.experimental import pallas as pl
from jax.experimental.pallas import tpu as pltpu
from jax.sharding import PartitionSpec as P

BF = jnp.bfloat16
F32 = jnp.float32
MISSING = -(1 << 20)


def dot(a, b):
    return lax.dot_general(a, b, (((1,), (0,)), ((), ())), preferred_element_type=F32)


def dot_t(a, b):
    return lax.dot_general(a, b, (((1,), (1,)), ((), ())), preferred_element_type=F32)


def iota(shape, dim):
    return lax.broadcasted_iota(jnp.int32, shape, dim)


def pick4(index, values):
    return jnp.where(
        index == 0, values[0], jnp.where(index == 1, values[1], jnp.where(index == 2, values[2], values[3]))
    )


def one_hot(shape, dim, bases):
    index = iota(shape, dim)
    position = pick4(index >> 5, bases) + (index & 31)
    return jnp.where(iota(shape, 1 - dim) == position, 1.0, 0.0).astype(BF)


def window_at(win, row):
    return [win[row, i] for i in range(4)]


def find(atoms, wanted):
    slot, there = jnp.int32(0), jnp.float32(0)
    for i in range(4):
        hit = atoms[i] == wanted
        slot = jnp.where(hit, jnp.int32(i), slot)
        there = jnp.where(hit, jnp.float32(1), there)
    return slot, there


def tile_mask(tiles, rows):
    shape = (4 * rows, 128)
    row, lane = iota(shape, 0) // rows, iota(shape, 1) >> 5
    mask = jnp.zeros(shape, F32)
    for i in range(4):
        for j in range(4):
            mask = jnp.where((row == i) & (lane == j), tiles[0, i, j].astype(F32), mask)
    return mask


def near(row, by, count):
    return lax.rem(row + by + count, count)


def column_chunk(row, count):
    return near(row, -1, count) >> 1


def first(count, occ, virt, tiles_hbm, coulomb, g_self, g_right, g_left, g_far, tensor, tiles, sem):
    d = lax.axis_index("row")
    funcs = tensor.shape[0]
    half = lax.rem(lax.axis_index("grp"), 2)
    list_copy = pltpu.make_async_copy(tiles_hbm, tiles, sem.at[0])
    half_copy = pltpu.make_async_copy(coulomb.at[0, pl.ds(half * funcs, funcs)], tensor, sem.at[1])
    copies = [list_copy, half_copy]
    for out, by in ((g_right, 1), (g_left, -1), (g_far, 2), (g_self, 0)):
        start = column_chunk(near(d, by, count), count)
        for c in range(2):
            chunk = lax.rem(start + c, count // 2)
            columns = pl.ds(pl.multiple_of(chunk * 128, 128), 128)
            for base, green in ((0, occ), (128, virt)):
                at = base + 64 * c
                copies.append(
                    pltpu.make_async_copy(green.at[:, columns], out.at[at : at + 64], sem.at[len(copies)])
                )
    for copy in copies:
        copy.start()
    list_copy.wait()
    mask = tile_mask(tiles, 32).astype(BF)
    half_copy.wait()
    tensor[...] = tensor[...] * mask[None]
    for copy in copies[2:]:
        copy.wait()


def far_tiles(count, win, half, far_right, far_left, xs):
    d = lax.axis_index("row")
    mine = window_at(win, d)
    funcs = half.shape[0]
    left, right = near(d, -1, count) * 2, near(d, 1, count) * 2
    shape = (128, 256)
    column = iota(shape, 1)
    wanted = jnp.where(column < 128, left, right) + ((column >> 5) & 1)
    here = pick4(iota(shape, 0) >> 5, mine)
    same = (here == wanted) & ((iota(shape, 0) & 31) == (column & 31))
    select = jnp.where(same, 1.0, 0.0).astype(BF)
    for r in range(0, funcs, 4):
        block = half[r : r + 4].reshape(512, 128)
        x = dot(block, select)
        xs[0, r * 128 : r * 128 + 512, :] = x[:, :128]
        xs[1, r * 128 : r * 128 + 512, :] = x[:, 128:]
    lane = iota((funcs, 128), 1)
    for side, base, out in ((0, left, far_left), (1, right, far_right)):
        slot0, there0 = find(mine, base)
        slot1, there1 = find(mine, base + 1)
        weight = jnp.where(lane < 64, there0, there1)
        for t in range(0, 32, 2):
            parts = []
            for u in (t, t + 1):
                x0 = xs[side, pl.ds(slot0 * 32 + u, funcs, stride=128), :]
                x1 = xs[side, pl.ds(slot1 * 32 + u, funcs, stride=128), :]
                parts.append(jnp.where(lane < 64, x0, x1) * weight)
            out[t * funcs : (t + 2) * funcs, :] = jnp.concatenate(parts, axis=0).astype(BF)


def choose(count, win, g_self, g_before, g_after, g_far, out):
    d = lax.axis_index("row")
    atoms = 2 * count
    mine = window_at(win, d)
    theirs = window_at(win, near(d, -1, count))
    row0 = near(d, -2, count) * 2
    col0 = column_chunk(d, count) * 4

    def position(atom, start):
        return lax.rem(atom - start + atoms, atoms) * 32

    def whole(base):
        blocks = []
        for c in range(2):
            at = base + 64 * c
            blocks.append(
                jnp.concatenate(
                    [
                        g_far[at : at + 64, :],
                        g_before[at : at + 64, :],
                        g_self[at : at + 64, :],
                        g_after[at : at + 64, :],
                    ],
                    axis=0,
                )
            )
        return jnp.concatenate(blocks, axis=1)

    occ, virt = whole(0), whole(128)
    rows_mine = [position(a, row0) for a in mine]
    rows_theirs = [position(a, row0) for a in theirs]
    columns_mine = [position(a, col0) for a in mine]
    columns_both = []
    for i in range(4):
        _, there = find(theirs, mine[i])
        columns_both.append(jnp.where(there > 0, columns_mine[i], jnp.int32(MISSING)))
    for base, rows, columns in ((0, rows_mine, columns_mine), (256, rows_theirs, columns_both)):
        left = one_hot((128, 256), 0, columns)
        x = dot_t(left, occ).astype(BF)
        out[base : base + 128, :] = dot(x, one_hot((256, 128), 1, rows)).astype(BF)
        y = dot(one_hot((128, 256), 0, rows), virt).astype(BF)
        out[base + 128 : base + 256, :] = dot(y, one_hot((256, 128), 1, columns)).astype(BF)


def frame_map(atoms_from, wanted):
    bases = []
    for w in wanted:
        slot, there = find(atoms_from, w)
        bases.append(jnp.where(there > 0, slot * 32, jnp.int32(MISSING)))
    return one_hot((128, 128), 1, bases)


PITCH = 136


def halves(occ, blocks, outs, ms):
    rows = occ.shape[0] // len(outs)
    for i in range(0, len(blocks), 2):
        m0, m1 = blocks[i](), blocks[i + 1]()
        if ms is not None:
            ms[i * PITCH : i * PITCH + 128, :] = m0.astype(F32)
            ms[(i + 1) * PITCH : (i + 1) * PITCH + 128, :] = m1.astype(F32)
        h = dot(occ, jnp.concatenate([m0, m1], axis=1))
        for n, out in enumerate(outs):
            part = h[n * rows : (n + 1) * rows]
            out[i * PITCH : i * PITCH + 128, :] = part[:, :128]
            out[(i + 1) * PITCH : (i + 1) * PITCH + 128, :] = part[:, 128:]


def gather(ref, funcs, start):
    return [ref[pl.ds(start + t, funcs, stride=PITCH), :] for t in range(8)]


def dress(count, own, win, tiles, tensor, greens, *refs):
    if own:
        polar0, flat, dressed, far, hs, ms, same = refs
    else:
        (dressed, far, hs), ms = refs, None
    d = lax.axis_index("row")
    funcs = tensor.shape[1]
    mine = window_at(win, d)
    theirs = window_at(win, near(d, -1, count))
    left, right = near(d, -1, count) * 2, near(d, 1, count) * 2
    mask = tile_mask(tiles, 32).astype(BF)
    occ, virt = greens[0:128, :], greens[128:256, :]
    halves(occ, [functools.partial(lambda r: tensor[0, r] * mask, r) for r in range(funcs)], [hs], ms)
    frames = [
        dot(virt, frame_map(mine, theirs)).astype(BF),
        dot(virt, frame_map(mine, [left, left + 1, right, right + 1])).astype(BF),
    ]
    outs = [dressed, far]
    if own:
        frames, outs = [virt] + frames, [same] + outs
    wide = jnp.concatenate(frames, axis=1)
    for i in range(16):
        x = dot(jnp.concatenate(gather(hs, funcs, i * 8), axis=0).astype(BF), wide)
        for t in range(8):
            at = (i * 8 + t) * 128
            block = x[t * funcs : (t + 1) * funcs].astype(BF)
            for n, out in enumerate(outs):
                out[:, at : at + 128] = block[:, n * 128 : (n + 1) * 128]
        if own:
            for t, rows in enumerate(gather(ms, funcs, i * 8)):
                at = (i * 8 + t) * 128
                flat[:, at : at + 128] = rows.astype(BF)
    if own:
        polar0[...] = dot_t(same[...], flat[...])


def join(count, win, tensor, g0, g1, flat, dressed0, dressed1, down0, down1, up0, up1, hs0, hs1, ms, backs, moved):
    d = lax.axis_index("row")
    funcs = tensor.shape[0]
    full = 2 * funcs
    mine = window_at(win, d)
    theirs = window_at(win, near(d, -1, count))
    occ = jnp.concatenate([g0[256:384, :], g1[256:384, :]], axis=0)
    halves(occ, [functools.partial(lambda r: tensor[r], r) for r in range(funcs)], [hs0, hs1], ms)
    virts = [g0[384:512, :], g1[384:512, :]]
    for i in range(16):
        slot, there = find(theirs, mine[i // 4])
        xs = []
        for hs, virt in zip((hs0, hs1), virts):
            xs.append(dot(jnp.concatenate(gather(hs, funcs, i * 8), axis=0).astype(BF), virt))
        rows = gather(ms, funcs, slot * 32 + (i % 4) * 8)
        for t in range(8):
            at = (i * 8 + t) * 128
            part = slice(t * funcs, (t + 1) * funcs)
            backs[:, at : at + 128] = jnp.concatenate([x[part] for x in xs], axis=0).astype(BF)
            moved[:, at : at + 128] = (rows[t] * there).astype(BF)
    up = dot_t(backs[...], flat[...])
    up = jnp.concatenate([up, jnp.zeros((full, 128 - full), F32)], axis=1)
    up0[...] = up[:funcs]
    up1[...] = up[funcs:]
    for dressed, out in ((dressed0, down0), (dressed1, down1)):
        out[...] = jnp.concatenate(
            [dot_t(dressed[...], moved[...]), jnp.zeros((full, 128 - funcs), F32)], axis=1
        )


def join_far(count, win, far0, far1, from_left, from_right, down0, down1, own, other, tiles_far):
    d = lax.axis_index("row")
    full = far0.shape[0]
    funcs = full // 2
    mine = window_at(win, d)
    left, right = near(d, -1, count), near(d, 1, count)
    lane = iota((funcs, 128), 1)
    for t in range(0, 32, 2):
        pair = slice(t * funcs, (t + 2) * funcs)
        for side, e, row in ((0, from_left, left), (1, from_right, right)):
            both = e[pair, :].astype(F32)
            for u in range(2):
                x = both[u * funcs : (u + 1) * funcs]
                turned = pltpu.roll(x, 64, 1)
                for i in range(4):
                    odd = lax.rem(mine[i], 2)
                    here = (lane < 64) if side == 0 else (lane >= 64)
                    value = jnp.where(odd == side, x, turned)
                    at = (i * 32 + t + u) * 128
                    kept = here & (jnp.broadcast_to(mine[i] >> 1, lane.shape) == row)
                    tiles_far[side, :, at : at + 128] = jnp.where(kept, value, 0.0).astype(BF)
    for far, down, out in ((far0, down0, own), (far1, down1, other)):
        dressed = far[...]
        out[...] = jnp.concatenate(
            [
                dot_t(dressed, tiles_far[0]),
                down[:, :funcs],
                dot_t(dressed, tiles_far[1]),
                jnp.zeros((full, 128 - 3 * funcs), F32),
            ],
            axis=1,
        )


def assemble(polar0, own, recv, up0, up1, out):
    first = lax.rem(lax.axis_index("grp"), 2) == 0
    full = polar0.shape[0]
    funcs = full // 2
    a, b = own[...], recv[...]
    low, high = jnp.where(first, a, b), jnp.where(first, b, a)
    c, e = up0[...], up1[...]
    after = jnp.concatenate([jnp.where(first, c, e), jnp.where(first, e, c)], axis=0)
    pieces = []
    for i in range(3):
        part = slice(i * funcs, (i + 1) * funcs)
        if i == 2:
            pieces += [polar0[...], after[:, :full]]
        pieces += [low[:, part], high[:, part]]
    out[...] = jnp.concatenate(pieces, axis=1)


def vmem(count):
    return [pl.BlockSpec(memory_space=pltpu.VMEM)] * count


def hbm(count):
    return [pl.BlockSpec(memory_space=pltpu.HBM)] * count


def smem(count):
    return [pl.BlockSpec(memory_space=pltpu.SMEM)] * count


def call(kernel, name, specs, outs, args, scratch=(), flops=0, limit=40 << 20):
    return pl.pallas_call(
        kernel,
        name=name,
        in_specs=specs,
        out_specs=tuple(vmem(len(outs))),
        out_shape=tuple(outs),
        scratch_shapes=list(scratch),
        compiler_params=pltpu.CompilerParams(vmem_limit_bytes=limit),
        cost_estimate=pl.CostEstimate(flops=flops, bytes_accessed=0, transcendentals=0),
    )(*args)


def body(groups, count, green_occ, green_virt, coulomb3c, tile_list, window):
    full = coulomb3c.shape[1]
    funcs = full // 2
    shape = jax.ShapeDtypeStruct

    def send(array, row_by, swap=False):
        pairs = []
        for g in range(groups):
            for d in range(count):
                to = (g ^ 1 if swap else g) * count + (d + row_by) % count
                pairs.append((g * count + d, to))
        return lax.ppermute(array, ("grp", "row"), pairs)

    far_rows = funcs * 32
    g_self, g_right, g_left, g_far, tensor = call(
        functools.partial(first, count),
        "first",
        hbm(4),
        [shape((256, 128), BF)] * 4 + [shape((funcs, 128, 128), BF)],
        (green_occ, green_virt, tile_list, coulomb3c),
        [pltpu.SMEM((1, 4, 4), jnp.int32), pltpu.SemaphoreType.DMA((18,))],
        limit=60 << 20,
    )
    g_before = send(g_right, 1)
    g_after = send(g_left, -1)
    g_beyond = send(g_far, 2)
    wide = send(tensor, 1)
    far_right, far_left = call(
        functools.partial(far_tiles, count),
        "far_tiles",
        smem(1) + vmem(1),
        [shape((far_rows, 128), BF), shape((far_rows, 128), BF)],
        (window, tensor),
        [pltpu.VMEM((2, funcs * 128, 128), F32)],
        flops=1 << 36,
    )
    from_left = send(far_right, 2)
    from_right = send(far_left, -2)
    g_before, g_after, g_beyond, far_right, far_left = lax.optimization_barrier(
        (g_before, g_after, g_beyond, far_right, far_left)
    )
    (mine,) = call(
        functools.partial(choose, count),
        "choose",
        smem(1) + vmem(4),
        [shape((512, 128), BF)],
        (window, g_self, g_before, g_after, g_beyond),
    )
    partner = send(mine, 0, True)
    flat_shape = shape((full, 128 * 128), BF)
    tall = pltpu.VMEM((full * PITCH, 128), F32)
    polar0, flat, dressed0, far0 = call(
        functools.partial(dress, count, True),
        "dress_own",
        smem(2) + vmem(2),
        [shape((full, full), F32), flat_shape, flat_shape, flat_shape],
        (window, tile_list, coulomb3c, mine),
        [tall, tall, pltpu.VMEM((full, 128 * 128), BF)],
    )
    dressed1, far1 = call(
        functools.partial(dress, count, False),
        "dress_partner",
        smem(2) + vmem(2),
        [flat_shape, flat_shape],
        (window, tile_list, coulomb3c, partner),
        [tall],
    )
    short = pltpu.VMEM((funcs * PITCH, 128), F32)
    down0, down1, up0, up1 = call(
        functools.partial(join, count),
        "join",
        smem(1) + vmem(6),
        [shape((full, 128), F32)] * 2 + [shape((funcs, 128), F32)] * 2,
        (window, wide, mine, partner, flat, dressed0, dressed1),
        [short, short, short, pltpu.VMEM((full, 128 * 128), BF), pltpu.VMEM((funcs, 128 * 128), BF)],
    )
    after0 = send(up0, -1)
    after1 = send(up1, -1, True)
    own, other = call(
        functools.partial(join_far, count),
        "join_far",
        smem(1) + vmem(6),
        [shape((full, 128), F32)] * 2,
        (window, far0, far1, from_left, from_right, down0, down1),
        [pltpu.VMEM((2, funcs, 128 * 128), BF)],
        flops=1 << 33,
    )
    recv = send(other, 0, True)
    (out,) = call(
        assemble,
        "assemble",
        vmem(5),
        [shape((full, 5 * full), F32)],
        (polar0, own, recv, after0, after1),
    )
    return out


def solution(mesh):
    placed = (
        P(("grp", "row"), None),
        P(("grp", "row"), None),
        P("row", None, None, None),
        P("row", None, None),
        P(),
    )
    return jax.shard_map(
        functools.partial(body, mesh.shape["grp"], mesh.shape["row"]),
        mesh=mesh,
        in_specs=placed,
        out_specs=P(("grp", "row"), None),
        check_vma=False,
    )
```

```python
import functools

import jax
import jax.numpy as jnp
from jax import lax
from jax.experimental import pallas as pl
from jax.experimental.pallas import tpu as pltpu
from jax.sharding import PartitionSpec as P

BF = jnp.bfloat16
F32 = jnp.float32
MISSING = -(1 << 20)


def dot(a, b):
    return lax.dot_general(a, b, (((1,), (0,)), ((), ())), preferred_element_type=F32)


def dot_t(a, b):
    return lax.dot_general(a, b, (((1,), (1,)), ((), ())), preferred_element_type=F32)


def iota(shape, dim):
    return lax.broadcasted_iota(jnp.int32, shape, dim)


def pick4(index, values):
    return jnp.where(
        index == 0, values[0], jnp.where(index == 1, values[1], jnp.where(index == 2, values[2], values[3]))
    )


def one_hot(shape, dim, bases):
    index = iota(shape, dim)
    position = pick4(index >> 5, bases) + (index & 31)
    return jnp.where(iota(shape, 1 - dim) == position, 1.0, 0.0).astype(BF)


def window_at(win, row):
    return [win[row, i] for i in range(4)]


def find(atoms, wanted):
    slot, there = jnp.int32(0), jnp.float32(0)
    for i in range(4):
        hit = atoms[i] == wanted
        slot = jnp.where(hit, jnp.int32(i), slot)
        there = jnp.where(hit, jnp.float32(1), there)
    return slot, there


def tile_mask(tiles, rows):
    shape = (4 * rows, 128)
    row, lane = iota(shape, 0) // rows, iota(shape, 1) >> 5
    mask = jnp.zeros(shape, F32)
    for i in range(4):
        for j in range(4):
            mask = jnp.where((row == i) & (lane == j), tiles[0, i, j].astype(F32), mask)
    return mask


def near(row, by, count):
    return lax.rem(row + by + count, count)


def column_chunk(row, count):
    return near(row, -1, count) >> 1


def first(count, occ, virt, tiles_hbm, coulomb, g_self, g_right, g_left, g_far, tensor, tiles, mask, sem):
    d = lax.axis_index("row")
    funcs = tensor.shape[0]
    half = lax.rem(lax.axis_index("grp"), 2)
    list_copy = pltpu.make_async_copy(tiles_hbm, tiles, sem.at[0])
    list_copy.start()
    copies = []
    for out, by in ((g_right, 1), (g_left, -1), (g_far, 2), (g_self, 0)):
        start = column_chunk(near(d, by, count), count)
        for c in range(2):
            chunk = lax.rem(start + c, count // 2)
            columns = pl.ds(pl.multiple_of(chunk * 128, 128), 128)
            for base, green in ((0, occ), (128, virt)):
                at = base + 64 * c
                copies.append(
                    pltpu.make_async_copy(green.at[:, columns], out.at[at : at + 64], sem.at[len(copies) + 1])
                )
    copies.append(pltpu.make_async_copy(coulomb.at[0, pl.ds(half * funcs, funcs)], tensor, sem.at[17]))
    for copy in copies:
        copy.start()
    list_copy.wait()
    mask[...] = tile_mask(tiles, 4).astype(BF)
    mask_copy = pltpu.make_async_copy(mask, g_right.at[256:272], sem.at[18])
    mask_copy.start()
    for copy in copies:
        copy.wait()
    mask_copy.wait()


def far_tiles(count, win, tiles, tensor, far_right, far_left, mask):
    d = lax.axis_index("row")
    mine = window_at(win, d)
    funcs = tensor.shape[1] // 2
    start = lax.rem(lax.axis_index("grp"), 2) * funcs
    mask[...] = tile_mask(tiles, 32).astype(BF)
    for by, out in ((-1, far_left), (1, far_right)):
        base = near(d, by, count) * 2
        shape = (256, 128)
        row, lane = iota(shape, 0), iota(shape, 1)
        found = [find(mine, base), find(mine, base + 1)]
        here = pick4((row & 127) >> 5, mine) == base + ((lane & 63) >> 5)
        same = here & ((row & 31) == (lane & 31)) & ((row >> 7) == (lane >> 6))
        weight = jnp.where(row < 128, found[0][1], found[1][1])
        select = jnp.where(same, weight, 0.0).astype(BF)
        places = [pl.ds(pl.multiple_of(slot * 32, 32), 32) for slot, _ in found]
        masks = [mask[place, :] for place in places]
        for r in range(0, funcs, 8):
            sides = [
                jnp.concatenate([tensor[0, start + r + u, place, :] * m for u in range(8)], axis=0)
                for place, m in zip(places, masks)
            ]
            x = dot(jnp.concatenate(sides, axis=1), select)
            out[r * 32 : r * 32 + 256, :] = x.astype(BF)


def choose(count, win, g_self, g_before, g_after, g_far, out):
    d = lax.axis_index("row")
    atoms = 2 * count
    mine = window_at(win, d)
    theirs = window_at(win, near(d, -1, count))
    row0 = near(d, -2, count) * 2
    col0 = column_chunk(d, count) * 4

    def position(atom, start):
        return lax.rem(atom - start + atoms, atoms) * 32

    def whole(base):
        blocks = []
        for c in range(2):
            at = base + 64 * c
            blocks.append(
                jnp.concatenate(
                    [
                        g_far[at : at + 64, :],
                        g_before[at : at + 64, :],
                        g_self[at : at + 64, :],
                        g_after[at : at + 64, :],
                    ],
                    axis=0,
                )
            )
        return jnp.concatenate(blocks, axis=1)

    occ, virt = whole(0), whole(128)
    rows_mine = [position(a, row0) for a in mine]
    rows_theirs = [position(a, row0) for a in theirs]
    columns_mine = [position(a, col0) for a in mine]
    columns_both = []
    for i in range(4):
        _, there = find(theirs, mine[i])
        columns_both.append(jnp.where(there > 0, columns_mine[i], jnp.int32(MISSING)))
    for base, rows, columns in ((0, rows_mine, columns_mine), (256, rows_theirs, columns_both)):
        left = one_hot((128, 256), 0, columns)
        x = dot_t(left, occ).astype(BF)
        out[base : base + 128, :] = dot(x, one_hot((256, 128), 1, rows)).astype(BF)
        y = dot(one_hot((128, 256), 0, rows), virt).astype(BF)
        out[base + 128 : base + 256, :] = dot(y, one_hot((256, 128), 1, columns)).astype(BF)


def frame_map(atoms_from, wanted):
    bases = []
    for w in wanted:
        slot, there = find(atoms_from, w)
        bases.append(jnp.where(there > 0, slot * 32, jnp.int32(MISSING)))
    return one_hot((128, 128), 1, bases)


PITCH = 136


def halves(occ, blocks, outs, ms):
    rows = occ.shape[0] // len(outs)
    for i in range(0, len(blocks), 2):
        m0, m1 = blocks[i](), blocks[i + 1]()
        if ms is not None:
            ms[i * PITCH : i * PITCH + 128, :] = m0.astype(F32)
            ms[(i + 1) * PITCH : (i + 1) * PITCH + 128, :] = m1.astype(F32)
        h = dot(occ, jnp.concatenate([m0, m1], axis=1))
        for n, out in enumerate(outs):
            part = h[n * rows : (n + 1) * rows]
            out[i * PITCH : i * PITCH + 128, :] = part[:, :128]
            out[(i + 1) * PITCH : (i + 1) * PITCH + 128, :] = part[:, 128:]


def gather(ref, funcs, start):
    return [ref[pl.ds(start + t, funcs, stride=PITCH), :] for t in range(8)]


def dress(count, own, win, tiles, tensor, greens, *refs):
    if own:
        polar0, flat, dressed, far, hs, ms, same = refs
    else:
        (dressed, far, hs), ms = refs, None
    d = lax.axis_index("row")
    funcs = tensor.shape[1]
    mine = window_at(win, d)
    theirs = window_at(win, near(d, -1, count))
    left, right = near(d, -1, count) * 2, near(d, 1, count) * 2
    mask = tile_mask(tiles, 32).astype(BF)
    occ, virt = greens[0:128, :], greens[128:256, :]
    halves(occ, [functools.partial(lambda r: tensor[0, r] * mask, r) for r in range(funcs)], [hs], ms)
    wide, outs = dot(virt, frame_map(mine, theirs)).astype(BF), [dressed]
    if own:
        wide, outs = jnp.concatenate([virt, wide], axis=1), [same, dressed]
    lane = iota((128, 256), 1)
    atom = jnp.where(lane < 128, left, right)
    column_here = pick4(iota((128, 256), 0) >> 5, mine) == atom + ((lane & 63) >> 5)
    column_here = column_here & ((iota((128, 256), 0) & 31) == (lane & 31))
    both = dot(virt, jnp.where(column_here, 1.0, 0.0).astype(BF))
    row_atom = atom + ((lane & 127) >> 6)
    packs = jnp.concatenate([jnp.where(row_atom == a, both, 0.0).astype(BF) for a in mine], axis=0)
    for c in range(4):
        parts = []
        for i in range(4):
            parts.append(jnp.concatenate(gather(hs, funcs, i * 32 + c * 8), axis=0).astype(BF))
            x = dot(parts[-1], wide)
            for t in range(8):
                at = (i * 32 + c * 8 + t) * 128
                block = x[t * funcs : (t + 1) * funcs].astype(BF)
                for n, out in enumerate(outs):
                    out[:, at : at + 128] = block[:, n * 128 : (n + 1) * 128]
            if own:
                for t, rows in enumerate(gather(ms, funcs, i * 32 + c * 8)):
                    at = (i * 32 + c * 8 + t) * 128
                    flat[:, at : at + 128] = rows.astype(BF)
        x = dot(jnp.concatenate(parts, axis=1), packs)
        for t in range(8):
            at = (c * 8 + t) * 128
            block = x[t * funcs : (t + 1) * funcs].astype(BF)
            far[:, at : at + 128] = block[:, :128]
            far[:, 4096 + at : 4224 + at] = block[:, 128:]
    if own:
        polar0[...] = dot_t(same[...], flat[...])


def stacked(a, b, start, other):
    total = None
    for at in range(0, other.shape[1], 1024):
        left = jnp.concatenate([x[:, start + at : start + at + 1024] for x in (a, b)], axis=0)
        part = dot_t(left, other[:, at : at + 1024])
        total = part if total is None else total + part
    return total


def join(count, win, tensor, g_before, g0, g1, flat, dressed0, dressed1, down, up, hs0, hs1, ms, backs, moved):
    d = lax.axis_index("row")
    funcs = tensor.shape[0]
    full = 2 * funcs
    mine = window_at(win, d)
    theirs = window_at(win, near(d, -1, count))
    short = g_before[256:272, :].astype(F32)
    mask = jnp.concatenate(
        [jnp.broadcast_to(short[4 * i : 4 * i + 1, :], (32, 128)) for i in range(4)], axis=0
    ).astype(BF)
    occ = jnp.concatenate([g0[256:384, :], g1[256:384, :]], axis=0)
    halves(occ, [functools.partial(lambda r: tensor[r] * mask, r) for r in range(funcs)], [hs0, hs1], ms)
    virts = [g0[384:512, :], g1[384:512, :]]
    for i in range(16):
        slot, there = find(theirs, mine[i // 4])
        xs = []
        for hs, virt in zip((hs0, hs1), virts):
            xs.append(dot(jnp.concatenate(gather(hs, funcs, i * 8), axis=0).astype(BF), virt))
        rows = gather(ms, funcs, slot * 32 + (i % 4) * 8)
        for t in range(8):
            at = (i * 8 + t) * 128
            part = slice(t * funcs, (t + 1) * funcs)
            backs[:, at : at + 128] = jnp.concatenate([x[part] for x in xs], axis=0).astype(BF)
            moved[:, at : at + 128] = (rows[t] * there).astype(BF)
    total = dot_t(backs[...], flat[...])
    up[...] = jnp.concatenate([total, jnp.zeros((full, 128 - full), F32)], axis=1)
    total = stacked(dressed0, dressed1, 0, moved)
    down[...] = jnp.concatenate([total, jnp.zeros((2 * full, 128 - funcs), F32)], axis=1)


FAR_PITCH = 40


def join_far(far0, far1, from_left, from_right, down, after, own, other, es, turned):
    full = far0.shape[0]
    funcs = full // 2
    for e in (from_left, from_right):
        side = 0 if e is from_left else 1
        for r in range(funcs):
            at = r * FAR_PITCH
            es[side, at : at + 32, :] = e[r * 32 : (r + 1) * 32, :].astype(F32)
        for t in range(32):
            rows = es[side, pl.ds(t, funcs, stride=FAR_PITCH), :]
            turned[side, :, t * 128 : (t + 1) * 128] = rows.astype(BF)
    far_left = stacked(far0, far1, 0, turned.at[0])
    far_right = stacked(far0, far1, 4096, turned.at[1])
    padding = jnp.zeros((full, 128 - 3 * funcs - full), F32)
    for n, out in enumerate((own, other)):
        part = slice(n * full, (n + 1) * full)
        back = after[n * funcs : (n + 1) * funcs, :full]
        back = jnp.concatenate([back, jnp.zeros((funcs, full), F32)], axis=0)
        out[...] = jnp.concatenate(
            [far_left[part], down[part, :funcs], far_right[part], back, padding], axis=1
        )


def assemble(polar0, own, recv, out):
    is_first = lax.rem(lax.axis_index("grp"), 2) == 0
    full = polar0.shape[0]
    funcs = full // 2
    a, b = own[...], recv[...]
    low, high = jnp.where(is_first, a, b), jnp.where(is_first, b, a)
    back = slice(3 * funcs, 3 * funcs + full)
    after = jnp.concatenate([low[:funcs, back], high[:funcs, back]], axis=0)
    pieces = []
    for i in range(3):
        part = slice(i * funcs, (i + 1) * funcs)
        if i == 2:
            pieces += [polar0[...], after]
        pieces += [low[:, part], high[:, part]]
    out[...] = jnp.concatenate(pieces, axis=1)


def vmem(count):
    return [pl.BlockSpec(memory_space=pltpu.VMEM)] * count


def hbm(count):
    return [pl.BlockSpec(memory_space=pltpu.HBM)] * count


def smem(count):
    return [pl.BlockSpec(memory_space=pltpu.SMEM)] * count


def call(kernel, name, specs, outs, args, scratch=(), flops=0, limit=40 << 20, space=None):
    return pl.pallas_call(
        kernel,
        name=name,
        in_specs=specs,
        out_specs=tuple((space or vmem)(len(outs))),
        out_shape=tuple(outs),
        scratch_shapes=list(scratch),
        compiler_params=pltpu.CompilerParams(vmem_limit_bytes=limit),
        cost_estimate=pl.CostEstimate(flops=flops, bytes_accessed=0, transcendentals=0),
    )(*args)


def body(groups, count, green_occ, green_virt, coulomb3c, tile_list, window):
    full = coulomb3c.shape[1]
    funcs = full // 2
    shape = jax.ShapeDtypeStruct

    def send(array, row_by, swap=False):
        pairs = []
        for g in range(groups):
            for d in range(count):
                to = (g ^ 1 if swap else g) * count + (d + row_by) % count
                pairs.append((g * count + d, to))
        return lax.ppermute(array, ("grp", "row"), pairs)

    far_rows = funcs * 32
    g_self, g_right, g_left, g_far, tensor = call(
        functools.partial(first, count),
        "first",
        hbm(4),
        [
            shape((256, 128), BF),
            shape((272, 128), BF),
            shape((256, 128), BF),
            shape((256, 128), BF),
            shape((funcs, 128, 128), BF),
        ],
        (green_occ, green_virt, tile_list, coulomb3c),
        [pltpu.SMEM((1, 4, 4), jnp.int32), pltpu.VMEM((16, 128), BF), pltpu.SemaphoreType.DMA((19,))],
        limit=60 << 20,
        space=hbm,
    )
    g_before = send(g_right, 1)
    g_after = send(g_left, -1)
    g_beyond = send(g_far, 2)
    wide = send(tensor, 1)
    far_right, far_left = call(
        functools.partial(far_tiles, count),
        "far_tiles",
        smem(2) + vmem(1),
        [shape((far_rows, 128), BF), shape((far_rows, 128), BF)],
        (window, tile_list, coulomb3c),
        [pltpu.VMEM((128, 128), BF)],
        flops=1 << 36,
    )
    from_left = send(far_right, 2)
    from_right = send(far_left, -2)
    g_before, g_after, g_beyond, far_right, far_left = lax.optimization_barrier(
        (g_before, g_after, g_beyond, far_right, far_left)
    )
    (mine,) = call(
        functools.partial(choose, count),
        "choose",
        smem(1) + vmem(4),
        [shape((512, 128), BF)],
        (window, g_self, g_before, g_after, g_beyond),
    )
    partner = send(mine, 0, True)
    flat_shape, far_shape = shape((full, 128 * 128), BF), shape((full, 64 * 128), BF)
    tall = pltpu.VMEM((full * PITCH, 128), F32)
    short = pltpu.VMEM((funcs * PITCH, 128), F32)
    message = shape((full, 128), F32)
    polar0, flat, dressed0, far0 = call(
        functools.partial(dress, count, True),
        "dress_own",
        smem(2) + vmem(2),
        [shape((full, full), F32), flat_shape, flat_shape, far_shape],
        (window, tile_list, coulomb3c, mine),
        [tall, tall, pltpu.VMEM((full, 128 * 128), BF)],
    )
    dressed1, far1 = call(
        functools.partial(dress, count, False),
        "dress_partner",
        smem(2) + vmem(2),
        [flat_shape, far_shape],
        (window, tile_list, coulomb3c, partner),
        [tall],
    )
    down, up = call(
        functools.partial(join, count),
        "join",
        smem(1) + vmem(7),
        [shape((2 * full, 128), F32), message],
        (window, wide, g_before, mine, partner, flat, dressed0, dressed1),
        [short, short, short, pltpu.VMEM((full, 128 * 128), BF), pltpu.VMEM((funcs, 128 * 128), BF)],
    )
    after = send(up, -1)
    own, other = call(
        join_far,
        "join_far",
        vmem(6),
        [message, message],
        (far0, far1, from_left, from_right, down, after),
        [pltpu.VMEM((2, funcs * FAR_PITCH, 128), F32), pltpu.VMEM((2, funcs, 32 * 128), BF)],
    )
    recv = send(other, 0, True)
    (out,) = call(
        assemble,
        "assemble",
        vmem(3),
        [shape((full, 5 * full), F32)],
        (polar0, own, recv),
    )
    return out


def solution(mesh):
    placed = (
        P(("grp", "row"), None),
        P(("grp", "row"), None),
        P("row", None, None, None),
        P("row", None, None),
        P(),
    )
    return jax.shard_map(
        functools.partial(body, mesh.shape["grp"], mesh.shape["row"]),
        mesh=mesh,
        in_specs=placed,
        out_specs=P(("grp", "row"), None),
        check_vma=False,
    )
```

```python
import functools

import jax
import jax.numpy as jnp
from jax import lax
from jax.experimental import pallas as pl
from jax.experimental.pallas import tpu as pltpu
from jax.sharding import PartitionSpec as P

BF = jnp.bfloat16
F32 = jnp.float32
MISSING = -(1 << 20)


def dot(a, b):
    return lax.dot_general(a, b, (((1,), (0,)), ((), ())), preferred_element_type=F32)


def dot_t(a, b):
    return lax.dot_general(a, b, (((1,), (1,)), ((), ())), preferred_element_type=F32)


def iota(shape, dim):
    return lax.broadcasted_iota(jnp.int32, shape, dim)


def pick4(index, values):
    return jnp.where(
        index == 0, values[0], jnp.where(index == 1, values[1], jnp.where(index == 2, values[2], values[3]))
    )


def one_hot(shape, dim, bases):
    index = iota(shape, dim)
    position = pick4(index >> 5, bases) + (index & 31)
    return jnp.where(iota(shape, 1 - dim) == position, 1.0, 0.0).astype(BF)


def window_at(win, row):
    return [win[row, i] for i in range(4)]


def find(atoms, wanted):
    slot, there = jnp.int32(0), jnp.float32(0)
    for i in range(4):
        hit = atoms[i] == wanted
        slot = jnp.where(hit, jnp.int32(i), slot)
        there = jnp.where(hit, jnp.float32(1), there)
    return slot, there


def tile_mask(tiles, rows):
    shape = (4 * rows, 128)
    row, lane = iota(shape, 0) // rows, iota(shape, 1) >> 5
    mask = jnp.zeros(shape, F32)
    for i in range(4):
        for j in range(4):
            mask = jnp.where((row == i) & (lane == j), tiles[0, i, j].astype(F32), mask)
    return mask


def near(row, by, count):
    return lax.rem(row + by + count, count)


def column_chunk(row, count):
    return near(row, -1, count) >> 1


def first(count, occ, virt, tiles_hbm, coulomb, *refs):
    outs, (tiles, gs, part, sem, done) = refs[:5], refs[5:]
    d = lax.axis_index("row")
    funcs = part.shape[0]
    half = lax.rem(lax.axis_index("grp"), 2)
    list_copy = pltpu.make_async_copy(tiles_hbm, tiles, sem.at[16])
    list_copy.start()
    groups = []
    for n, by in enumerate((0, 1, -1, 2)):
        start = column_chunk(near(d, by, count), count)
        copies = []
        for c in range(2):
            chunk = lax.rem(start + c, count // 2)
            columns = pl.ds(pl.multiple_of(chunk * 128, 128), 128)
            for base, green in ((0, occ), (128, virt)):
                at = base + 64 * c
                place = gs.at[n, at : at + 64]
                copies.append(pltpu.make_async_copy(green.at[:, columns], place, sem.at[4 * n + len(copies)]))
        rows = outs[n].shape[0]
        groups.append((copies, pltpu.make_async_copy(gs.at[n, 0:rows], outs[n], done.at[n])))
    for n in range(3):
        piece = pl.ds(half * funcs + n * 8, 8)
        copy = pltpu.make_async_copy(coulomb.at[0, piece], part.at[n * 8 : n * 8 + 8], sem.at[17 + n])
        out = pltpu.make_async_copy(part.at[n * 8 : n * 8 + 8], outs[4].at[n * 8 : n * 8 + 8], done.at[4 + n])
        groups.append(([copy], out))
    for copies, _ in groups:
        for copy in copies:
            copy.start()
    list_copy.wait()
    gs[1, 256:272, :] = tile_mask(tiles, 4).astype(BF)
    for copies, out in groups:
        for copy in copies:
            copy.wait()
        out.start()
    for _, out in groups:
        out.wait()


def far_tiles(count, win, tiles, tensor, far_right, far_left, mask):
    d = lax.axis_index("row")
    mine = window_at(win, d)
    funcs = tensor.shape[1] // 2
    start = lax.rem(lax.axis_index("grp"), 2) * funcs
    mask[...] = tile_mask(tiles, 32).astype(BF)
    for by, out in ((-1, far_left), (1, far_right)):
        base = near(d, by, count) * 2
        shape = (256, 128)
        row, lane = iota(shape, 0), iota(shape, 1)
        found = [find(mine, base), find(mine, base + 1)]
        here = pick4((row & 127) >> 5, mine) == base + ((lane & 63) >> 5)
        same = here & ((row & 31) == (lane & 31)) & ((row >> 7) == (lane >> 6))
        weight = jnp.where(row < 128, found[0][1], found[1][1])
        select = jnp.where(same, weight, 0.0).astype(BF)
        places = [pl.ds(pl.multiple_of(slot * 32, 32), 32) for slot, _ in found]
        masks = [mask[place, :] for place in places]
        for r in range(0, funcs, 8):
            sides = [
                jnp.concatenate([tensor[0, start + r + u, place, :] * m for u in range(8)], axis=0)
                for place, m in zip(places, masks)
            ]
            x = dot(jnp.concatenate(sides, axis=1), select)
            out[r * 32 : r * 32 + 256, :] = x.astype(BF)


def choose(count, win, g_self, g_before, g_after, g_far, out):
    d = lax.axis_index("row")
    atoms = 2 * count
    mine = window_at(win, d)
    theirs = window_at(win, near(d, -1, count))
    row0 = near(d, -2, count) * 2
    col0 = column_chunk(d, count) * 4

    def position(atom, start):
        return lax.rem(atom - start + atoms, atoms) * 32

    def whole(base):
        blocks = []
        for c in range(2):
            at = base + 64 * c
            blocks.append(
                jnp.concatenate(
                    [
                        g_far[at : at + 64, :],
                        g_before[at : at + 64, :],
                        g_self[at : at + 64, :],
                        g_after[at : at + 64, :],
                    ],
                    axis=0,
                )
            )
        return jnp.concatenate(blocks, axis=1)

    occ, virt = whole(0), whole(128)
    rows_mine = [position(a, row0) for a in mine]
    rows_theirs = [position(a, row0) for a in theirs]
    columns_mine = [position(a, col0) for a in mine]
    columns_both = []
    for i in range(4):
        _, there = find(theirs, mine[i])
        columns_both.append(jnp.where(there > 0, columns_mine[i], jnp.int32(MISSING)))
    for base, rows, columns in ((0, rows_mine, columns_mine), (256, rows_theirs, columns_both)):
        left = one_hot((128, 256), 0, columns)
        x = dot_t(left, occ).astype(BF)
        out[base : base + 128, :] = dot(x, one_hot((256, 128), 1, rows)).astype(BF)
        y = dot(one_hot((128, 256), 0, rows), virt).astype(BF)
        out[base + 128 : base + 256, :] = dot(y, one_hot((256, 128), 1, columns)).astype(BF)


def frame_map(atoms_from, wanted):
    bases = []
    for w in wanted:
        slot, there = find(atoms_from, w)
        bases.append(jnp.where(there > 0, slot * 32, jnp.int32(MISSING)))
    return one_hot((128, 128), 1, bases)


PITCH = 136


def halves(occ, blocks, outs, ms):
    rows = occ.shape[0] // len(outs)
    for i in range(0, len(blocks), 2):
        m0, m1 = blocks[i](), blocks[i + 1]()
        if ms is not None:
            ms[i * PITCH : i * PITCH + 128, :] = m0.astype(F32)
            ms[(i + 1) * PITCH : (i + 1) * PITCH + 128, :] = m1.astype(F32)
        h = dot(occ, jnp.concatenate([m0, m1], axis=1))
        for n, out in enumerate(outs):
            part = h[n * rows : (n + 1) * rows]
            out[i * PITCH : i * PITCH + 128, :] = part[:, :128]
            out[(i + 1) * PITCH : (i + 1) * PITCH + 128, :] = part[:, 128:]


def gather(ref, funcs, start):
    return [ref[pl.ds(start + t, funcs, stride=PITCH), :] for t in range(8)]


def dress(count, own, win, tiles, tensor, greens, *refs):
    if own:
        polar0, flat, dressed, far, hs, ms, same = refs
    else:
        (dressed, far, hs), ms = refs, None
    d = lax.axis_index("row")
    funcs = tensor.shape[1]
    mine = window_at(win, d)
    theirs = window_at(win, near(d, -1, count))
    left, right = near(d, -1, count) * 2, near(d, 1, count) * 2
    mask = tile_mask(tiles, 32).astype(BF)
    occ, virt = greens[0:128, :], greens[128:256, :]
    halves(occ, [functools.partial(lambda r: tensor[0, r] * mask, r) for r in range(funcs)], [hs], ms)
    wide, outs = dot(virt, frame_map(mine, theirs)).astype(BF), [dressed]
    if own:
        wide, outs = jnp.concatenate([virt, wide], axis=1), [same, dressed]
    lane = iota((128, 256), 1)
    atom = jnp.where(lane < 128, left, right)
    column_here = pick4(iota((128, 256), 0) >> 5, mine) == atom + ((lane & 63) >> 5)
    column_here = column_here & ((iota((128, 256), 0) & 31) == (lane & 31))
    both = dot(virt, jnp.where(column_here, 1.0, 0.0).astype(BF))
    row_atom = atom + ((lane & 127) >> 6)
    packs = jnp.concatenate([jnp.where(row_atom == a, both, 0.0).astype(BF) for a in mine], axis=0)
    for c in range(4):
        parts = []
        for i in range(4):
            parts.append(jnp.concatenate(gather(hs, funcs, i * 32 + c * 8), axis=0).astype(BF))
            x = dot(parts[-1], wide)
            for t in range(8):
                at = (i * 32 + c * 8 + t) * 128
                block = x[t * funcs : (t + 1) * funcs].astype(BF)
                for n, out in enumerate(outs):
                    out[:, at : at + 128] = block[:, n * 128 : (n + 1) * 128]
            if own:
                for t, rows in enumerate(gather(ms, funcs, i * 32 + c * 8)):
                    at = (i * 32 + c * 8 + t) * 128
                    flat[:, at : at + 128] = rows.astype(BF)
        x = dot(jnp.concatenate(parts, axis=1), packs)
        for t in range(8):
            at = (c * 8 + t) * 128
            block = x[t * funcs : (t + 1) * funcs].astype(BF)
            far[:, at : at + 128] = block[:, :128]
            far[:, 4096 + at : 4224 + at] = block[:, 128:]
    if own:
        polar0[...] = dot_t(same[...], flat[...])


def stacked(a, b, start, other):
    total = None
    for at in range(0, other.shape[1], 1024):
        left = jnp.concatenate([x[:, start + at : start + at + 1024] for x in (a, b)], axis=0)
        part = dot_t(left, other[:, at : at + 1024])
        total = part if total is None else total + part
    return total


def join(count, win, tensor, g_before, g0, g1, flat, dressed0, dressed1, down, up, hs0, hs1, ms, backs, moved):
    d = lax.axis_index("row")
    funcs = tensor.shape[0]
    full = 2 * funcs
    mine = window_at(win, d)
    theirs = window_at(win, near(d, -1, count))
    short = g_before[256:272, :].astype(F32)
    mask = jnp.concatenate(
        [jnp.broadcast_to(short[4 * i : 4 * i + 1, :], (32, 128)) for i in range(4)], axis=0
    ).astype(BF)
    occ = jnp.concatenate([g0[256:384, :], g1[256:384, :]], axis=0)
    halves(occ, [functools.partial(lambda r: tensor[r] * mask, r) for r in range(funcs)], [hs0, hs1], ms)
    virts = [g0[384:512, :], g1[384:512, :]]
    for i in range(16):
        slot, there = find(theirs, mine[i // 4])
        xs = []
        for hs, virt in zip((hs0, hs1), virts):
            xs.append(dot(jnp.concatenate(gather(hs, funcs, i * 8), axis=0).astype(BF), virt))
        rows = gather(ms, funcs, slot * 32 + (i % 4) * 8)
        for t in range(8):
            at = (i * 8 + t) * 128
            part = slice(t * funcs, (t + 1) * funcs)
            backs[:, at : at + 128] = jnp.concatenate([x[part] for x in xs], axis=0).astype(BF)
            moved[:, at : at + 128] = (rows[t] * there).astype(BF)
    total = dot_t(backs[...], flat[...])
    up[...] = jnp.concatenate([total, jnp.zeros((full, 128 - full), F32)], axis=1)
    total = stacked(dressed0, dressed1, 0, moved)
    down[...] = jnp.concatenate([total, jnp.zeros((2 * full, 128 - funcs), F32)], axis=1)


FAR_PITCH = 40


def join_far(far0, far1, from_left, from_right, down, after, own, other, es, turned):
    full = far0.shape[0]
    funcs = full // 2
    for e in (from_left, from_right):
        side = 0 if e is from_left else 1
        for r in range(funcs):
            at = r * FAR_PITCH
            es[side, at : at + 32, :] = e[r * 32 : (r + 1) * 32, :].astype(F32)
        for t in range(32):
            rows = es[side, pl.ds(t, funcs, stride=FAR_PITCH), :]
            turned[side, :, t * 128 : (t + 1) * 128] = rows.astype(BF)
    far_left = stacked(far0, far1, 0, turned.at[0])
    far_right = stacked(far0, far1, 4096, turned.at[1])
    padding = jnp.zeros((full, 128 - 3 * funcs - full), F32)
    for n, out in enumerate((own, other)):
        part = slice(n * full, (n + 1) * full)
        back = after[n * funcs : (n + 1) * funcs, :full]
        back = jnp.concatenate([back, jnp.zeros((funcs, full), F32)], axis=0)
        out[...] = jnp.concatenate(
            [far_left[part], down[part, :funcs], far_right[part], back, padding], axis=1
        )


def assemble(polar0, own, recv, out):
    is_first = lax.rem(lax.axis_index("grp"), 2) == 0
    full = polar0.shape[0]
    funcs = full // 2
    a, b = own[...], recv[...]
    low, high = jnp.where(is_first, a, b), jnp.where(is_first, b, a)
    back = slice(3 * funcs, 3 * funcs + full)
    after = jnp.concatenate([low[:funcs, back], high[:funcs, back]], axis=0)
    pieces = []
    for i in range(3):
        part = slice(i * funcs, (i + 1) * funcs)
        if i == 2:
            pieces += [polar0[...], after]
        pieces += [low[:, part], high[:, part]]
    out[...] = jnp.concatenate(pieces, axis=1)


def vmem(count):
    return [pl.BlockSpec(memory_space=pltpu.VMEM)] * count


def hbm(count):
    return [pl.BlockSpec(memory_space=pltpu.HBM)] * count


def smem(count):
    return [pl.BlockSpec(memory_space=pltpu.SMEM)] * count


def call(kernel, name, specs, outs, args, scratch=(), flops=0, limit=40 << 20, space=None):
    return pl.pallas_call(
        kernel,
        name=name,
        in_specs=specs,
        out_specs=tuple((space or vmem)(len(outs))),
        out_shape=tuple(outs),
        scratch_shapes=list(scratch),
        compiler_params=pltpu.CompilerParams(vmem_limit_bytes=limit),
        cost_estimate=pl.CostEstimate(flops=flops, bytes_accessed=0, transcendentals=0),
    )(*args)


def body(groups, count, green_occ, green_virt, coulomb3c, tile_list, window):
    full = coulomb3c.shape[1]
    funcs = full // 2
    shape = jax.ShapeDtypeStruct

    def send(array, row_by, swap=False):
        pairs = []
        for g in range(groups):
            for d in range(count):
                to = (g ^ 1 if swap else g) * count + (d + row_by) % count
                pairs.append((g * count + d, to))
        return lax.ppermute(array, ("grp", "row"), pairs)

    far_rows = funcs * 32
    g_self, g_right, g_left, g_far, tensor = call(
        functools.partial(first, count),
        "first",
        hbm(4),
        [
            shape((256, 128), BF),
            shape((272, 128), BF),
            shape((256, 128), BF),
            shape((256, 128), BF),
            shape((funcs, 128, 128), BF),
        ],
        (green_occ, green_virt, tile_list, coulomb3c),
        [
            pltpu.SMEM((1, 4, 4), jnp.int32),
            pltpu.VMEM((4, 272, 128), BF),
            pltpu.VMEM((funcs, 128, 128), BF),
            pltpu.SemaphoreType.DMA((20,)),
            pltpu.SemaphoreType.DMA((7,)),
        ],
        limit=60 << 20,
        space=hbm,
    )
    g_before = send(g_right, 1)
    g_after = send(g_left, -1)
    g_beyond = send(g_far, 2)
    wide = send(tensor, 1)
    far_right, far_left = call(
        functools.partial(far_tiles, count),
        "far_tiles",
        smem(2) + vmem(1),
        [shape((far_rows, 128), BF), shape((far_rows, 128), BF)],
        (window, tile_list, coulomb3c),
        [pltpu.VMEM((128, 128), BF)],
        flops=1 << 36,
    )
    from_left = send(far_right, 2)
    from_right = send(far_left, -2)
    g_before, g_after, g_beyond, far_right, far_left = lax.optimization_barrier(
        (g_before, g_after, g_beyond, far_right, far_left)
    )
    (mine,) = call(
        functools.partial(choose, count),
        "choose",
        smem(1) + vmem(4),
        [shape((512, 128), BF)],
        (window, g_self, g_before, g_after, g_beyond),
    )
    partner = send(mine, 0, True)
    flat_shape, far_shape = shape((full, 128 * 128), BF), shape((full, 64 * 128), BF)
    tall = pltpu.VMEM((full * PITCH, 128), F32)
    short = pltpu.VMEM((funcs * PITCH, 128), F32)
    message = shape((full, 128), F32)
    polar0, flat, dressed0, far0 = call(
        functools.partial(dress, count, True),
        "dress_own",
        smem(2) + vmem(2),
        [shape((full, full), F32), flat_shape, flat_shape, far_shape],
        (window, tile_list, coulomb3c, mine),
        [tall, tall, pltpu.VMEM((full, 128 * 128), BF)],
    )
    dressed1, far1 = call(
        functools.partial(dress, count, False),
        "dress_partner",
        smem(2) + vmem(2),
        [flat_shape, far_shape],
        (window, tile_list, coulomb3c, partner),
        [tall],
    )
    down, up = call(
        functools.partial(join, count),
        "join",
        smem(1) + vmem(7),
        [shape((2 * full, 128), F32), message],
        (window, wide, g_before, mine, partner, flat, dressed0, dressed1),
        [short, short, short, pltpu.VMEM((full, 128 * 128), BF), pltpu.VMEM((funcs, 128 * 128), BF)],
    )
    after = send(up, -1)
    own, other = call(
        join_far,
        "join_far",
        vmem(6),
        [message, message],
        (far0, far1, from_left, from_right, down, after),
        [pltpu.VMEM((2, funcs * FAR_PITCH, 128), F32), pltpu.VMEM((2, funcs, 32 * 128), BF)],
    )
    recv = send(other, 0, True)
    (out,) = call(
        assemble,
        "assemble",
        vmem(3),
        [shape((full, 5 * full), F32)],
        (polar0, own, recv),
    )
    return out


def solution(mesh):
    placed = (
        P(("grp", "row"), None),
        P(("grp", "row"), None),
        P("row", None, None, None),
        P("row", None, None),
        P(),
    )
    return jax.shard_map(
        functools.partial(body, mesh.shape["grp"], mesh.shape["row"]),
        mesh=mesh,
        in_specs=placed,
        out_specs=P(("grp", "row"), None),
        check_vma=False,
    )
```

```python
import functools

import jax
import jax.numpy as jnp
from jax import lax
from jax.experimental import pallas as pl
from jax.experimental.pallas import tpu as pltpu
from jax.sharding import PartitionSpec as P

BF = jnp.bfloat16
F32 = jnp.float32
MISSING = -(1 << 20)


def dot(a, b):
    return lax.dot_general(a, b, (((1,), (0,)), ((), ())), preferred_element_type=F32)


def dot_t(a, b):
    return lax.dot_general(a, b, (((1,), (1,)), ((), ())), preferred_element_type=F32)


def iota(shape, dim):
    return lax.broadcasted_iota(jnp.int32, shape, dim)


def pick4(index, values):
    return jnp.where(
        index == 0, values[0], jnp.where(index == 1, values[1], jnp.where(index == 2, values[2], values[3]))
    )


def one_hot(shape, dim, bases):
    index = iota(shape, dim)
    position = pick4(index >> 5, bases) + (index & 31)
    return jnp.where(iota(shape, 1 - dim) == position, 1.0, 0.0).astype(BF)


def window_at(win, row):
    return [win[row, i] for i in range(4)]


def find(atoms, wanted):
    slot, there = jnp.int32(0), jnp.float32(0)
    for i in range(4):
        hit = atoms[i] == wanted
        slot = jnp.where(hit, jnp.int32(i), slot)
        there = jnp.where(hit, jnp.float32(1), there)
    return slot, there


def tile_mask(tiles, rows):
    shape = (4 * rows, 128)
    row, lane = iota(shape, 0) // rows, iota(shape, 1) >> 5
    mask = jnp.zeros(shape, F32)
    for i in range(4):
        for j in range(4):
            mask = jnp.where((row == i) & (lane == j), tiles[0, i, j].astype(F32), mask)
    return mask


def near(row, by, count):
    return lax.rem(row + by + count, count)


def column_chunk(row, count):
    return near(row, -1, count) >> 1


def first(count, occ, virt, tiles_hbm, coulomb, *refs):
    outs, (tiles, gs, part, sem, done) = refs[:5], refs[5:]
    d = lax.axis_index("row")
    funcs = part.shape[0]
    half = lax.rem(lax.axis_index("grp"), 2)
    list_copy = pltpu.make_async_copy(tiles_hbm, tiles, sem.at[16])
    list_copy.start()
    groups = []
    for n, by in enumerate((0, 1, -1, 2)):
        start = column_chunk(near(d, by, count), count)
        copies = []
        for c in range(2):
            chunk = lax.rem(start + c, count // 2)
            columns = pl.ds(pl.multiple_of(chunk * 128, 128), 128)
            for base, green in ((0, occ), (128, virt)):
                at = base + 64 * c
                place = gs.at[n, at : at + 64]
                copies.append(pltpu.make_async_copy(green.at[:, columns], place, sem.at[4 * n + len(copies)]))
        rows = outs[n].shape[0]
        groups.append((copies, pltpu.make_async_copy(gs.at[n, 0:rows], outs[n], done.at[n])))
    for n in range(3):
        piece = pl.ds(half * funcs + n * 8, 8)
        copy = pltpu.make_async_copy(coulomb.at[0, piece], part.at[n * 8 : n * 8 + 8], sem.at[17 + n])
        out = pltpu.make_async_copy(part.at[n * 8 : n * 8 + 8], outs[4].at[n * 8 : n * 8 + 8], done.at[4 + n])
        groups.append(([copy], out))
    for copies, _ in groups:
        for copy in copies:
            copy.start()
    list_copy.wait()
    gs[1, 256:272, :] = tile_mask(tiles, 4).astype(BF)
    for copies, out in groups:
        for copy in copies:
            copy.wait()
        out.start()
    for _, out in groups:
        out.wait()


def far_tiles(count, win, tiles, tensor, far_right, far_left, flat, mask, ms):
    d = lax.axis_index("row")
    mine = window_at(win, d)
    funcs = tensor.shape[1] // 2
    start = lax.rem(lax.axis_index("grp"), 2) * funcs
    mask[...] = tile_mask(tiles, 32).astype(BF)
    for by, out in ((-1, far_left), (1, far_right)):
        base = near(d, by, count) * 2
        shape = (256, 128)
        row, lane = iota(shape, 0), iota(shape, 1)
        found = [find(mine, base), find(mine, base + 1)]
        here = pick4((row & 127) >> 5, mine) == base + ((lane & 63) >> 5)
        same = here & ((row & 31) == (lane & 31)) & ((row >> 7) == (lane >> 6))
        weight = jnp.where(row < 128, found[0][1], found[1][1])
        select = jnp.where(same, weight, 0.0).astype(BF)
        places = [pl.ds(pl.multiple_of(slot * 32, 32), 32) for slot, _ in found]
        masks = [mask[place, :] for place in places]
        for r in range(0, funcs, 8):
            sides = [
                jnp.concatenate([tensor[0, start + r + u, place, :] * m for u in range(8)], axis=0)
                for place, m in zip(places, masks)
            ]
            x = dot(jnp.concatenate(sides, axis=1), select)
            out[r * 32 : r * 32 + 256, :] = x.astype(BF)
    whole = mask[...]
    for r in range(2 * funcs):
        ms[r * PITCH : r * PITCH + 128, :] = (tensor[0, r] * whole).astype(F32)
    for m in range(128):
        rows = ms[pl.ds(m, 2 * funcs, stride=PITCH), :]
        flat[:, m * 128 : (m + 1) * 128] = rows.astype(BF)


def choose(count, win, g_self, g_before, g_after, g_far, out):
    d = lax.axis_index("row")
    atoms = 2 * count
    mine = window_at(win, d)
    theirs = window_at(win, near(d, -1, count))
    row0 = near(d, -2, count) * 2
    col0 = column_chunk(d, count) * 4

    def position(atom, start):
        return lax.rem(atom - start + atoms, atoms) * 32

    def whole(base):
        blocks = []
        for c in range(2):
            at = base + 64 * c
            blocks.append(
                jnp.concatenate(
                    [
                        g_far[at : at + 64, :],
                        g_before[at : at + 64, :],
                        g_self[at : at + 64, :],
                        g_after[at : at + 64, :],
                    ],
                    axis=0,
                )
            )
        return jnp.concatenate(blocks, axis=1)

    occ, virt = whole(0), whole(128)
    rows_mine = [position(a, row0) for a in mine]
    rows_theirs = [position(a, row0) for a in theirs]
    columns_mine = [position(a, col0) for a in mine]
    columns_both = []
    for i in range(4):
        _, there = find(theirs, mine[i])
        columns_both.append(jnp.where(there > 0, columns_mine[i], jnp.int32(MISSING)))
    for base, rows, columns in ((0, rows_mine, columns_mine), (256, rows_theirs, columns_both)):
        left = one_hot((128, 256), 0, columns)
        x = dot_t(left, occ).astype(BF)
        out[base : base + 128, :] = dot(x, one_hot((256, 128), 1, rows)).astype(BF)
        y = dot(one_hot((128, 256), 0, rows), virt).astype(BF)
        out[base + 128 : base + 256, :] = dot(y, one_hot((256, 128), 1, columns)).astype(BF)


def frame_map(atoms_from, wanted):
    bases = []
    for w in wanted:
        slot, there = find(atoms_from, w)
        bases.append(jnp.where(there > 0, slot * 32, jnp.int32(MISSING)))
    return one_hot((128, 128), 1, bases)


PITCH = 136


def halves(occ, blocks, outs):
    rows = occ.shape[0] // len(outs)
    for i in range(0, len(blocks), 2):
        m0, m1 = blocks[i](), blocks[i + 1]()
        h = dot(occ, jnp.concatenate([m0, m1], axis=1))
        for n, out in enumerate(outs):
            part = h[n * rows : (n + 1) * rows]
            out[i * PITCH : i * PITCH + 128, :] = part[:, :128]
            out[(i + 1) * PITCH : (i + 1) * PITCH + 128, :] = part[:, 128:]


def gather(ref, funcs, start):
    return [ref[pl.ds(start + t, funcs, stride=PITCH), :] for t in range(8)]


def dress(count, own, win, tiles, tensor, greens, *refs):
    if own:
        flat, polar0, dressed, far, hs, same = refs
    else:
        dressed, far, hs = refs
    d = lax.axis_index("row")
    funcs = tensor.shape[1]
    mine = window_at(win, d)
    theirs = window_at(win, near(d, -1, count))
    left, right = near(d, -1, count) * 2, near(d, 1, count) * 2
    mask = tile_mask(tiles, 32).astype(BF)
    occ, virt = greens[0:128, :], greens[128:256, :]
    halves(occ, [functools.partial(lambda r: tensor[0, r] * mask, r) for r in range(funcs)], [hs])
    wide, outs = dot(virt, frame_map(mine, theirs)).astype(BF), [dressed]
    if own:
        wide, outs = jnp.concatenate([virt, wide], axis=1), [same, dressed]
    lane = iota((128, 256), 1)
    atom = jnp.where(lane < 128, left, right)
    column_here = pick4(iota((128, 256), 0) >> 5, mine) == atom + ((lane & 63) >> 5)
    column_here = column_here & ((iota((128, 256), 0) & 31) == (lane & 31))
    both = dot(virt, jnp.where(column_here, 1.0, 0.0).astype(BF))
    row_atom = atom + ((lane & 127) >> 6)
    packs = jnp.concatenate([jnp.where(row_atom == a, both, 0.0).astype(BF) for a in mine], axis=0)
    for c in range(4):
        parts = []
        for i in range(4):
            parts.append(jnp.concatenate(gather(hs, funcs, i * 32 + c * 8), axis=0).astype(BF))
            x = dot(parts[-1], wide)
            for t in range(8):
                at = (i * 32 + c * 8 + t) * 128
                block = x[t * funcs : (t + 1) * funcs].astype(BF)
                for n, out in enumerate(outs):
                    out[:, at : at + 128] = block[:, n * 128 : (n + 1) * 128]
        x = dot(jnp.concatenate(parts, axis=1), packs)
        for t in range(8):
            at = (c * 8 + t) * 128
            block = x[t * funcs : (t + 1) * funcs].astype(BF)
            far[:, at : at + 128] = block[:, :128]
            far[:, 4096 + at : 4224 + at] = block[:, 128:]
    if own:
        polar0[...] = dot_t(same[...], flat[...])


def stacked(a, b, start, other):
    total = None
    for at in range(0, other.shape[1], 1024):
        left = jnp.concatenate([x[:, start + at : start + at + 1024] for x in (a, b)], axis=0)
        part = dot_t(left, other[:, at : at + 1024])
        total = part if total is None else total + part
    return total


def neighbour_mask(g_before):
    short = g_before[256:272, :].astype(F32)
    return jnp.concatenate(
        [jnp.broadcast_to(short[4 * i : 4 * i + 1, :], (32, 128)) for i in range(4)], axis=0
    ).astype(BF)


def join_back(tensor, g_before, g0, g1, flat, up, hs0, hs1, backs):
    funcs = tensor.shape[0]
    full = 2 * funcs
    mask = neighbour_mask(g_before)
    occ = jnp.concatenate([g0[256:384, :], g1[256:384, :]], axis=0)
    halves(occ, [functools.partial(lambda r: tensor[r] * mask, r) for r in range(funcs)], [hs0, hs1])
    virts = [g0[384:512, :], g1[384:512, :]]
    for i in range(16):
        xs = []
        for hs, virt in zip((hs0, hs1), virts):
            xs.append(dot(jnp.concatenate(gather(hs, funcs, i * 8), axis=0).astype(BF), virt))
        for t in range(8):
            at = (i * 8 + t) * 128
            part = slice(t * funcs, (t + 1) * funcs)
            backs[:, at : at + 128] = jnp.concatenate([x[part] for x in xs], axis=0).astype(BF)
    total = dot_t(backs[...], flat[...])
    up[...] = jnp.concatenate([total, jnp.zeros((full, 128 - full), F32)], axis=1)


def join(count, win, tensor, g_before, dressed0, dressed1, down, ms, moved):
    d = lax.axis_index("row")
    funcs = tensor.shape[0]
    full = 2 * funcs
    mine = window_at(win, d)
    theirs = window_at(win, near(d, -1, count))
    mask = neighbour_mask(g_before)
    for r in range(funcs):
        ms[r * PITCH : r * PITCH + 128, :] = (tensor[r] * mask).astype(F32)
    for i in range(16):
        slot, there = find(theirs, mine[i // 4])
        rows = gather(ms, funcs, slot * 32 + (i % 4) * 8)
        for t in range(8):
            at = (i * 8 + t) * 128
            moved[:, at : at + 128] = (rows[t] * there).astype(BF)
    total = stacked(dressed0, dressed1, 0, moved)
    down[...] = jnp.concatenate([total, jnp.zeros((2 * full, 128 - funcs), F32)], axis=1)


FAR_PITCH = 40


def join_far(far0, far1, from_left, from_right, down, after, own, other, es, turned):
    full = far0.shape[0]
    funcs = full // 2
    for e in (from_left, from_right):
        side = 0 if e is from_left else 1
        for r in range(funcs):
            at = r * FAR_PITCH
            es[side, at : at + 32, :] = e[r * 32 : (r + 1) * 32, :].astype(F32)
        for t in range(32):
            rows = es[side, pl.ds(t, funcs, stride=FAR_PITCH), :]
            turned[side, :, t * 128 : (t + 1) * 128] = rows.astype(BF)
    far_left = stacked(far0, far1, 0, turned.at[0])
    far_right = stacked(far0, far1, 4096, turned.at[1])
    padding = jnp.zeros((full, 128 - 3 * funcs - full), F32)
    for n, out in enumerate((own, other)):
        part = slice(n * full, (n + 1) * full)
        back = after[n * funcs : (n + 1) * funcs, :full]
        back = jnp.concatenate([back, jnp.zeros((funcs, full), F32)], axis=0)
        out[...] = jnp.concatenate(
            [far_left[part], down[part, :funcs], far_right[part], back, padding], axis=1
        )


def assemble(polar0, own, recv, out):
    is_first = lax.rem(lax.axis_index("grp"), 2) == 0
    full = polar0.shape[0]
    funcs = full // 2
    a, b = own[...], recv[...]
    low, high = jnp.where(is_first, a, b), jnp.where(is_first, b, a)
    back = slice(3 * funcs, 3 * funcs + full)
    after = jnp.concatenate([low[:funcs, back], high[:funcs, back]], axis=0)
    pieces = []
    for i in range(3):
        part = slice(i * funcs, (i + 1) * funcs)
        if i == 2:
            pieces += [polar0[...], after]
        pieces += [low[:, part], high[:, part]]
    out[...] = jnp.concatenate(pieces, axis=1)


def vmem(count):
    return [pl.BlockSpec(memory_space=pltpu.VMEM)] * count


def hbm(count):
    return [pl.BlockSpec(memory_space=pltpu.HBM)] * count


def smem(count):
    return [pl.BlockSpec(memory_space=pltpu.SMEM)] * count


def call(kernel, name, specs, outs, args, scratch=(), flops=0, limit=40 << 20, space=None):
    return pl.pallas_call(
        kernel,
        name=name,
        in_specs=specs,
        out_specs=tuple((space or vmem)(len(outs))),
        out_shape=tuple(outs),
        scratch_shapes=list(scratch),
        compiler_params=pltpu.CompilerParams(vmem_limit_bytes=limit),
        cost_estimate=pl.CostEstimate(flops=flops, bytes_accessed=0, transcendentals=0),
    )(*args)


def body(groups, count, green_occ, green_virt, coulomb3c, tile_list, window):
    full = coulomb3c.shape[1]
    funcs = full // 2
    shape = jax.ShapeDtypeStruct

    def send(array, row_by, swap=False):
        pairs = []
        for g in range(groups):
            for d in range(count):
                to = (g ^ 1 if swap else g) * count + (d + row_by) % count
                pairs.append((g * count + d, to))
        return lax.ppermute(array, ("grp", "row"), pairs)

    far_rows = funcs * 32
    g_self, g_right, g_left, g_far, tensor = call(
        functools.partial(first, count),
        "first",
        hbm(4),
        [
            shape((256, 128), BF),
            shape((272, 128), BF),
            shape((256, 128), BF),
            shape((256, 128), BF),
            shape((funcs, 128, 128), BF),
        ],
        (green_occ, green_virt, tile_list, coulomb3c),
        [
            pltpu.SMEM((1, 4, 4), jnp.int32),
            pltpu.VMEM((4, 272, 128), BF),
            pltpu.VMEM((funcs, 128, 128), BF),
            pltpu.SemaphoreType.DMA((20,)),
            pltpu.SemaphoreType.DMA((7,)),
        ],
        limit=60 << 20,
        space=hbm,
    )
    g_before = send(g_right, 1)
    g_after = send(g_left, -1)
    g_beyond = send(g_far, 2)
    wide = send(tensor, 1)
    flat_shape, far_shape = shape((full, 128 * 128), BF), shape((full, 64 * 128), BF)
    tall = pltpu.VMEM((full * PITCH, 128), F32)
    short = pltpu.VMEM((funcs * PITCH, 128), F32)
    message = shape((full, 128), F32)
    far_right, far_left, flat = call(
        functools.partial(far_tiles, count),
        "far_tiles",
        smem(2) + vmem(1),
        [shape((far_rows, 128), BF), shape((far_rows, 128), BF), flat_shape],
        (window, tile_list, coulomb3c),
        [pltpu.VMEM((128, 128), BF), tall],
        flops=1 << 36,
    )
    g_before, g_after, g_beyond, far_right, far_left = lax.optimization_barrier(
        (g_before, g_after, g_beyond, far_right, far_left)
    )
    (mine,) = call(
        functools.partial(choose, count),
        "choose",
        smem(1) + vmem(4),
        [shape((512, 128), BF)],
        (window, g_self, g_before, g_after, g_beyond),
    )
    partner = send(mine, 0, True)
    polar0, dressed0, far0 = call(
        functools.partial(dress, count, True),
        "dress_own",
        smem(2) + vmem(3),
        [shape((full, full), F32), flat_shape, far_shape],
        (window, tile_list, coulomb3c, mine, flat),
        [tall, pltpu.VMEM((full, 128 * 128), BF)],
    )
    far_right, far_left, polar0 = lax.optimization_barrier((far_right, far_left, polar0))
    from_left = send(far_right, 2)
    from_right = send(far_left, -2)
    dressed1, far1 = call(
        functools.partial(dress, count, False),
        "dress_partner",
        smem(2) + vmem(2),
        [flat_shape, far_shape],
        (window, tile_list, coulomb3c, partner),
        [tall],
    )
    (up,) = call(
        join_back,
        "join_back",
        vmem(5),
        [message],
        (wide, g_before, mine, partner, flat),
        [short, short, pltpu.VMEM((full, 128 * 128), BF)],
    )
    after = send(up, -1)
    (down,) = call(
        functools.partial(join, count),
        "join",
        smem(1) + vmem(4),
        [shape((2 * full, 128), F32)],
        (window, wide, g_before, dressed0, dressed1),
        [short, pltpu.VMEM((funcs, 128 * 128), BF)],
        flops=1 << 34,
    )
    own, other = call(
        join_far,
        "join_far",
        vmem(6),
        [message, message],
        (far0, far1, from_left, from_right, down, after),
        [pltpu.VMEM((2, funcs * FAR_PITCH, 128), F32), pltpu.VMEM((2, funcs, 32 * 128), BF)],
    )
    recv = send(other, 0, True)
    (out,) = call(
        assemble,
        "assemble",
        vmem(3),
        [shape((full, 5 * full), F32)],
        (polar0, own, recv),
    )
    return out


def solution(mesh):
    placed = (
        P(("grp", "row"), None),
        P(("grp", "row"), None),
        P("row", None, None, None),
        P("row", None, None),
        P(),
    )
    return jax.shard_map(
        functools.partial(body, mesh.shape["grp"], mesh.shape["row"]),
        mesh=mesh,
        in_specs=placed,
        out_specs=P(("grp", "row"), None),
        check_vma=False,
    )
```

```python
import functools

import jax
import jax.numpy as jnp
from jax import lax
from jax.experimental import pallas as pl
from jax.experimental.pallas import tpu as pltpu
from jax.sharding import PartitionSpec as P

BF = jnp.bfloat16
F32 = jnp.float32
MISSING = -(1 << 20)


def dot(a, b):
    return lax.dot_general(a, b, (((1,), (0,)), ((), ())), preferred_element_type=F32)


def dot_t(a, b):
    return lax.dot_general(a, b, (((1,), (1,)), ((), ())), preferred_element_type=F32)


def iota(shape, dim):
    return lax.broadcasted_iota(jnp.int32, shape, dim)


def pick4(index, values):
    return jnp.where(
        index == 0, values[0], jnp.where(index == 1, values[1], jnp.where(index == 2, values[2], values[3]))
    )


def one_hot(shape, dim, bases):
    index = iota(shape, dim)
    position = pick4(index >> 5, bases) + (index & 31)
    return jnp.where(iota(shape, 1 - dim) == position, 1.0, 0.0).astype(BF)


def window_at(win, row):
    return [win[row, i] for i in range(4)]


def find(atoms, wanted):
    slot, there = jnp.int32(0), jnp.float32(0)
    for i in range(4):
        hit = atoms[i] == wanted
        slot = jnp.where(hit, jnp.int32(i), slot)
        there = jnp.where(hit, jnp.float32(1), there)
    return slot, there


def tile_mask(tiles, rows):
    shape = (4 * rows, 128)
    row, lane = iota(shape, 0) // rows, iota(shape, 1) >> 5
    mask = jnp.zeros(shape, F32)
    for i in range(4):
        for j in range(4):
            mask = jnp.where((row == i) & (lane == j), tiles[0, i, j].astype(F32), mask)
    return mask


def near(row, by, count):
    return lax.rem(row + by + count, count)


def column_chunk(row, count):
    return near(row, -1, count) >> 1


def first(count, occ, virt, tiles_hbm, coulomb, *refs):
    outs, (tiles, gs, part, sem, done) = refs[:4], refs[4:]
    d = lax.axis_index("row")
    funcs = part.shape[0]
    half = lax.rem(lax.axis_index("grp"), 2)
    list_copy = pltpu.make_async_copy(tiles_hbm, tiles, sem.at[16])
    list_copy.start()
    groups = []
    for n, by in enumerate((0, 1, -1)):
        start = column_chunk(near(d, by, count), count)
        copies = []
        for c in range(2):
            chunk = lax.rem(start + c, count // 2)
            columns = pl.ds(pl.multiple_of(chunk * 128, 128), 128)
            for base, green in ((0, occ), (128, virt)):
                at = base + 64 * c
                place = gs.at[n, at : at + 64]
                copies.append(pltpu.make_async_copy(green.at[:, columns], place, sem.at[4 * n + len(copies)]))
        rows = outs[n].shape[0]
        groups.append((copies, pltpu.make_async_copy(gs.at[n, 0:rows], outs[n], done.at[n])))
    for n in range(3):
        piece = pl.ds(half * funcs + n * 8, 8)
        copy = pltpu.make_async_copy(coulomb.at[0, piece], part.at[n * 8 : n * 8 + 8], sem.at[17 + n])
        out = pltpu.make_async_copy(part.at[n * 8 : n * 8 + 8], outs[3].at[n * 8 : n * 8 + 8], done.at[4 + n])
        groups.append(([copy], out))
    for copies, _ in groups:
        for copy in copies:
            copy.start()
    list_copy.wait()
    gs[1, 256:272, :] = tile_mask(tiles, 4).astype(BF)
    for copies, out in groups:
        for copy in copies:
            copy.wait()
        out.start()
    for _, out in groups:
        out.wait()


def far_tiles(count, win, tiles, tensor, far_right, far_left, flat, mask, ms):
    d = lax.axis_index("row")
    mine = window_at(win, d)
    funcs = tensor.shape[1] // 2
    start = lax.rem(lax.axis_index("grp"), 2) * funcs
    mask[...] = tile_mask(tiles, 32).astype(BF)
    for by, out in ((-1, far_left), (1, far_right)):
        base = near(d, by, count) * 2
        shape = (256, 128)
        row, lane = iota(shape, 0), iota(shape, 1)
        found = [find(mine, base), find(mine, base + 1)]
        here = pick4((row & 127) >> 5, mine) == base + ((lane & 63) >> 5)
        same = here & ((row & 31) == (lane & 31)) & ((row >> 7) == (lane >> 6))
        weight = jnp.where(row < 128, found[0][1], found[1][1])
        select = jnp.where(same, weight, 0.0).astype(BF)
        places = [pl.ds(pl.multiple_of(slot * 32, 32), 32) for slot, _ in found]
        masks = [mask[place, :] for place in places]
        for r in range(0, funcs, 8):
            sides = [
                jnp.concatenate([tensor[0, start + r + u, place, :] * m for u in range(8)], axis=0)
                for place, m in zip(places, masks)
            ]
            x = dot(jnp.concatenate(sides, axis=1), select)
            out[r * 32 : r * 32 + 256, :] = x.astype(BF)
    whole = mask[...]
    for r in range(2 * funcs):
        ms[r * PITCH : r * PITCH + 128, :] = (tensor[0, r] * whole).astype(F32)
    for m in range(128):
        rows = ms[pl.ds(m, 2 * funcs, stride=PITCH), :]
        flat[:, m * 128 : (m + 1) * 128] = rows.astype(BF)


def choose(count, win, g_self, g_before, g_after, out):
    d = lax.axis_index("row")
    atoms = 2 * count
    mine = window_at(win, d)
    row0 = near(d, -1, count) * 2
    col0 = column_chunk(d, count) * 4

    def position(atom, start):
        return lax.rem(atom - start + atoms, atoms) * 32

    def whole(base):
        blocks = []
        for c in range(2):
            at = base + 64 * c
            parts = [g[at : at + 64, :] for g in (g_before, g_self, g_after, g_after)]
            blocks.append(jnp.concatenate(parts, axis=0))
        return jnp.concatenate(blocks, axis=1)

    rows = [position(a, row0) for a in mine]
    columns = [position(a, col0) for a in mine]
    x = dot_t(one_hot((128, 256), 0, columns), whole(0)).astype(BF)
    out[0:128, :] = dot(x, one_hot((256, 128), 1, rows)).astype(BF)
    y = dot(one_hot((128, 256), 0, rows), whole(128)).astype(BF)
    out[128:256, :] = dot(y, one_hot((256, 128), 1, columns)).astype(BF)


def frame_map(atoms_from, wanted):
    bases = []
    for w in wanted:
        slot, there = find(atoms_from, w)
        bases.append(jnp.where(there > 0, slot * 32, jnp.int32(MISSING)))
    return one_hot((128, 128), 1, bases)


PITCH = 136


def halves(occ, blocks, outs):
    rows = occ.shape[0] // len(outs)
    for i in range(0, len(blocks), 2):
        m0, m1 = blocks[i](), blocks[i + 1]()
        h = dot(occ, jnp.concatenate([m0, m1], axis=1))
        for n, out in enumerate(outs):
            part = h[n * rows : (n + 1) * rows]
            out[i * PITCH : i * PITCH + 128, :] = part[:, :128]
            out[(i + 1) * PITCH : (i + 1) * PITCH + 128, :] = part[:, 128:]


def gather(ref, funcs, start):
    return [ref[pl.ds(start + t, funcs, stride=PITCH), :] for t in range(8)]


def dress(count, own, win, tiles, tensor, greens, *refs):
    if own:
        flat, polar0, dressed, far, hs, same = refs
    else:
        dressed, far, hs = refs
    d = lax.axis_index("row")
    funcs = tensor.shape[1]
    mine = window_at(win, d)
    theirs = window_at(win, near(d, -1, count))
    left, right = near(d, -1, count) * 2, near(d, 1, count) * 2
    mask = tile_mask(tiles, 32).astype(BF)
    occ, virt = greens[0:128, :], greens[128:256, :]
    halves(occ, [functools.partial(lambda r: tensor[0, r] * mask, r) for r in range(funcs)], [hs])
    wide, outs = dot(virt, frame_map(mine, theirs)).astype(BF), [dressed]
    if own:
        wide, outs = jnp.concatenate([virt, wide], axis=1), [same, dressed]
    lane = iota((128, 256), 1)
    atom = jnp.where(lane < 128, left, right)
    column_here = pick4(iota((128, 256), 0) >> 5, mine) == atom + ((lane & 63) >> 5)
    column_here = column_here & ((iota((128, 256), 0) & 31) == (lane & 31))
    both = dot(virt, jnp.where(column_here, 1.0, 0.0).astype(BF))
    row_atom = atom + ((lane & 127) >> 6)
    packs = jnp.concatenate([jnp.where(row_atom == a, both, 0.0).astype(BF) for a in mine], axis=0)
    for c in range(4):
        parts = []
        for i in range(4):
            parts.append(jnp.concatenate(gather(hs, funcs, i * 32 + c * 8), axis=0).astype(BF))
            x = dot(parts[-1], wide)
            for t in range(8):
                at = (i * 32 + c * 8 + t) * 128
                block = x[t * funcs : (t + 1) * funcs].astype(BF)
                for n, out in enumerate(outs):
                    out[:, at : at + 128] = block[:, n * 128 : (n + 1) * 128]
        x = dot(jnp.concatenate(parts, axis=1), packs)
        for t in range(8):
            at = (c * 8 + t) * 128
            block = x[t * funcs : (t + 1) * funcs].astype(BF)
            far[:, at : at + 128] = block[:, :128]
            far[:, 4096 + at : 4224 + at] = block[:, 128:]
    if own:
        polar0[...] = dot_t(same[...], flat[...])


def stacked(a, b, start, other):
    total = None
    for at in range(0, other.shape[1], 1024):
        left = jnp.concatenate([x[:, start + at : start + at + 1024] for x in (a, b)], axis=0)
        part = dot_t(left, other[:, at : at + 1024])
        total = part if total is None else total + part
    return total


def neighbour_mask(g_before):
    short = g_before[256:272, :].astype(F32)
    return jnp.concatenate(
        [jnp.broadcast_to(short[4 * i : 4 * i + 1, :], (32, 128)) for i in range(4)], axis=0
    ).astype(BF)


def join_back(count, win, tensor, g_before, before, flat, up, hs0, hs1, backs):
    d = lax.axis_index("row")
    mine = window_at(win, d)
    theirs = window_at(win, near(d, -1, count))
    bases = []
    for a in mine:
        slot, there = find(theirs, a)
        bases.append(jnp.where(there > 0, slot * 32, jnp.int32(MISSING)))
    rows, columns = one_hot((128, 128), 0, bases), one_hot((128, 128), 1, bases)
    funcs = tensor.shape[0]
    full = 2 * funcs
    mask = neighbour_mask(g_before)
    occ = jnp.concatenate([dot(rows, before[at : at + 128, :]).astype(BF) for at in (0, 256)], axis=0)
    halves(occ, [functools.partial(lambda r: tensor[r] * mask, r) for r in range(funcs)], [hs0, hs1])
    virts = [dot(before[at : at + 128, :], columns).astype(BF) for at in (128, 384)]
    for i in range(16):
        xs = []
        for hs, virt in zip((hs0, hs1), virts):
            xs.append(dot(jnp.concatenate(gather(hs, funcs, i * 8), axis=0).astype(BF), virt))
        for t in range(8):
            at = (i * 8 + t) * 128
            part = slice(t * funcs, (t + 1) * funcs)
            backs[:, at : at + 128] = jnp.concatenate([x[part] for x in xs], axis=0).astype(BF)
    total = dot_t(backs[...], flat[...])
    up[...] = jnp.concatenate([total, jnp.zeros((full, 128 - full), F32)], axis=1)


def join(count, win, tensor, g_before, dressed0, dressed1, down, ms, moved):
    d = lax.axis_index("row")
    funcs = tensor.shape[0]
    full = 2 * funcs
    mine = window_at(win, d)
    theirs = window_at(win, near(d, -1, count))
    mask = neighbour_mask(g_before)
    for r in range(funcs):
        ms[r * PITCH : r * PITCH + 128, :] = (tensor[r] * mask).astype(F32)
    for i in range(16):
        slot, there = find(theirs, mine[i // 4])
        rows = gather(ms, funcs, slot * 32 + (i % 4) * 8)
        for t in range(8):
            at = (i * 8 + t) * 128
            moved[:, at : at + 128] = (rows[t] * there).astype(BF)
    total = stacked(dressed0, dressed1, 0, moved)
    down[...] = jnp.concatenate([total, jnp.zeros((2 * full, 128 - funcs), F32)], axis=1)


FAR_PITCH = 40


def join_far(far0, far1, from_left, from_right, down, after, own, other, es, turned):
    full = far0.shape[0]
    funcs = full // 2
    for e in (from_left, from_right):
        side = 0 if e is from_left else 1
        for r in range(funcs):
            at = r * FAR_PITCH
            es[side, at : at + 32, :] = e[r * 32 : (r + 1) * 32, :].astype(F32)
        for t in range(32):
            rows = es[side, pl.ds(t, funcs, stride=FAR_PITCH), :]
            turned[side, :, t * 128 : (t + 1) * 128] = rows.astype(BF)
    far_left = stacked(far0, far1, 0, turned.at[0])
    far_right = stacked(far0, far1, 4096, turned.at[1])
    padding = jnp.zeros((full, 128 - 3 * funcs - full), F32)
    for n, out in enumerate((own, other)):
        part = slice(n * full, (n + 1) * full)
        back = after[n * funcs : (n + 1) * funcs, :full]
        back = jnp.concatenate([back, jnp.zeros((funcs, full), F32)], axis=0)
        out[...] = jnp.concatenate(
            [far_left[part], down[part, :funcs], far_right[part], back, padding], axis=1
        )


def assemble(polar0, own, recv, out):
    is_first = lax.rem(lax.axis_index("grp"), 2) == 0
    full = polar0.shape[0]
    funcs = full // 2
    a, b = own[...], recv[...]
    low, high = jnp.where(is_first, a, b), jnp.where(is_first, b, a)
    back = slice(3 * funcs, 3 * funcs + full)
    after = jnp.concatenate([low[:funcs, back], high[:funcs, back]], axis=0)
    pieces = []
    for i in range(3):
        part = slice(i * funcs, (i + 1) * funcs)
        if i == 2:
            pieces += [polar0[...], after]
        pieces += [low[:, part], high[:, part]]
    out[...] = jnp.concatenate(pieces, axis=1)


def vmem(count):
    return [pl.BlockSpec(memory_space=pltpu.VMEM)] * count


def hbm(count):
    return [pl.BlockSpec(memory_space=pltpu.HBM)] * count


def smem(count):
    return [pl.BlockSpec(memory_space=pltpu.SMEM)] * count


def call(kernel, name, specs, outs, args, scratch=(), flops=0, limit=40 << 20, space=None):
    return pl.pallas_call(
        kernel,
        name=name,
        in_specs=specs,
        out_specs=tuple((space or vmem)(len(outs))),
        out_shape=tuple(outs),
        scratch_shapes=list(scratch),
        compiler_params=pltpu.CompilerParams(vmem_limit_bytes=limit),
        cost_estimate=pl.CostEstimate(flops=flops, bytes_accessed=0, transcendentals=0),
    )(*args)


def body(groups, count, green_occ, green_virt, coulomb3c, tile_list, window):
    full = coulomb3c.shape[1]
    funcs = full // 2
    shape = jax.ShapeDtypeStruct

    def send(array, row_by, swap=False):
        pairs = []
        for g in range(groups):
            for d in range(count):
                to = (g ^ 1 if swap else g) * count + (d + row_by) % count
                pairs.append((g * count + d, to))
        return lax.ppermute(array, ("grp", "row"), pairs)

    far_rows = funcs * 32
    g_self, g_right, g_left, tensor = call(
        functools.partial(first, count),
        "first",
        hbm(4),
        [
            shape((256, 128), BF),
            shape((272, 128), BF),
            shape((256, 128), BF),
            shape((funcs, 128, 128), BF),
        ],
        (green_occ, green_virt, tile_list, coulomb3c),
        [
            pltpu.SMEM((1, 4, 4), jnp.int32),
            pltpu.VMEM((3, 272, 128), BF),
            pltpu.VMEM((funcs, 128, 128), BF),
            pltpu.SemaphoreType.DMA((20,)),
            pltpu.SemaphoreType.DMA((7,)),
        ],
        limit=60 << 20,
        space=hbm,
    )
    g_before = send(g_right, 1)
    g_after = send(g_left, -1)
    wide = send(tensor, 1)
    flat_shape, far_shape = shape((full, 128 * 128), BF), shape((full, 64 * 128), BF)
    tall = pltpu.VMEM((full * PITCH, 128), F32)
    short = pltpu.VMEM((funcs * PITCH, 128), F32)
    message = shape((full, 128), F32)
    far_right, far_left, flat = call(
        functools.partial(far_tiles, count),
        "far_tiles",
        smem(2) + vmem(1),
        [shape((far_rows, 128), BF), shape((far_rows, 128), BF), flat_shape],
        (window, tile_list, coulomb3c),
        [pltpu.VMEM((128, 128), BF), tall],
        flops=1 << 36,
    )
    g_before, g_after, far_right, far_left = lax.optimization_barrier((g_before, g_after, far_right, far_left))
    (mine,) = call(
        functools.partial(choose, count),
        "choose",
        smem(1) + vmem(3),
        [shape((256, 128), BF)],
        (window, g_self, g_before, g_after),
    )
    partner = send(mine, 0, True)
    polar0, dressed0, far0 = call(
        functools.partial(dress, count, True),
        "dress_own",
        smem(2) + vmem(3),
        [shape((full, full), F32), flat_shape, far_shape],
        (window, tile_list, coulomb3c, mine, flat),
        [tall, pltpu.VMEM((full, 128 * 128), BF)],
    )
    far_right, far_left, polar0, partner = lax.optimization_barrier((far_right, far_left, polar0, partner))
    before = send(jnp.concatenate([mine, partner], axis=0), 1)
    from_left = send(far_right, 2)
    from_right = send(far_left, -2)
    dressed1, far1 = call(
        functools.partial(dress, count, False),
        "dress_partner",
        smem(2) + vmem(2),
        [flat_shape, far_shape],
        (window, tile_list, coulomb3c, partner),
        [tall],
    )
    (up,) = call(
        functools.partial(join_back, count),
        "join_back",
        smem(1) + vmem(4),
        [message],
        (window, wide, g_before, before, flat),
        [short, short, pltpu.VMEM((full, 128 * 128), BF)],
    )
    after = send(up, -1)
    (down,) = call(
        functools.partial(join, count),
        "join",
        smem(1) + vmem(4),
        [shape((2 * full, 128), F32)],
        (window, wide, g_before, dressed0, dressed1),
        [short, pltpu.VMEM((funcs, 128 * 128), BF)],
        flops=1 << 34,
    )
    own, other = call(
        join_far,
        "join_far",
        vmem(6),
        [message, message],
        (far0, far1, from_left, from_right, down, after),
        [pltpu.VMEM((2, funcs * FAR_PITCH, 128), F32), pltpu.VMEM((2, funcs, 32 * 128), BF)],
    )
    recv = send(other, 0, True)
    (out,) = call(
        assemble,
        "assemble",
        vmem(3),
        [shape((full, 5 * full), F32)],
        (polar0, own, recv),
    )
    return out


def solution(mesh):
    placed = (
        P(("grp", "row"), None),
        P(("grp", "row"), None),
        P("row", None, None, None),
        P("row", None, None),
        P(),
    )
    return jax.shard_map(
        functools.partial(body, mesh.shape["grp"], mesh.shape["row"]),
        mesh=mesh,
        in_specs=placed,
        out_specs=P(("grp", "row"), None),
        check_vma=False,
    )
```

```python
import functools

import jax
import jax.numpy as jnp
from jax import lax
from jax.experimental import pallas as pl
from jax.experimental.pallas import tpu as pltpu
from jax.sharding import PartitionSpec as P

BF = jnp.bfloat16
F32 = jnp.float32
MISSING = -(1 << 20)


def dot(a, b):
    return lax.dot_general(a, b, (((1,), (0,)), ((), ())), preferred_element_type=F32)


def dot_t(a, b):
    return lax.dot_general(a, b, (((1,), (1,)), ((), ())), preferred_element_type=F32)


def iota(shape, dim):
    return lax.broadcasted_iota(jnp.int32, shape, dim)


def pick4(index, values):
    return jnp.where(
        index == 0, values[0], jnp.where(index == 1, values[1], jnp.where(index == 2, values[2], values[3]))
    )


def one_hot(shape, dim, bases):
    index = iota(shape, dim)
    position = pick4(index >> 5, bases) + (index & 31)
    return jnp.where(iota(shape, 1 - dim) == position, 1.0, 0.0).astype(BF)


def window_at(win, row):
    return [win[row, i] for i in range(4)]


def find(atoms, wanted):
    slot, there = jnp.int32(0), jnp.float32(0)
    for i in range(4):
        hit = atoms[i] == wanted
        slot = jnp.where(hit, jnp.int32(i), slot)
        there = jnp.where(hit, jnp.float32(1), there)
    return slot, there


def tile_mask(tiles, rows):
    shape = (4 * rows, 128)
    row, lane = iota(shape, 0) // rows, iota(shape, 1) >> 5
    mask = jnp.zeros(shape, F32)
    for i in range(4):
        for j in range(4):
            mask = jnp.where((row == i) & (lane == j), tiles[0, i, j].astype(F32), mask)
    return mask


def near(row, by, count):
    return lax.rem(row + by + count, count)


def column_chunk(row, count):
    return near(row, -1, count) >> 1


def first(count, occ, virt, tiles_hbm, coulomb, *refs):
    outs, (tiles, gs, part, sem, done) = refs[:5], refs[5:]
    d = lax.axis_index("row")
    funcs = part.shape[0]
    half = lax.rem(lax.axis_index("grp"), 2)
    list_copy = pltpu.make_async_copy(tiles_hbm, tiles, sem.at[16])
    list_copy.start()
    groups = []
    for n, by in enumerate((0, 1, -1, 2)):
        start = column_chunk(near(d, by, count), count)
        copies = []
        for c in range(2):
            chunk = lax.rem(start + c, count // 2)
            columns = pl.ds(pl.multiple_of(chunk * 128, 128), 128)
            for base, green in ((0, occ), (128, virt)):
                at = base + 64 * c
                place = gs.at[n, at : at + 64]
                copies.append(pltpu.make_async_copy(green.at[:, columns], place, sem.at[4 * n + len(copies)]))
        rows = outs[n].shape[0]
        groups.append((copies, pltpu.make_async_copy(gs.at[n, 0:rows], outs[n], done.at[n])))
    for n in range(3):
        piece = pl.ds(half * funcs + n * 8, 8)
        copy = pltpu.make_async_copy(coulomb.at[0, piece], part.at[n * 8 : n * 8 + 8], sem.at[17 + n])
        out = pltpu.make_async_copy(part.at[n * 8 : n * 8 + 8], outs[4].at[n * 8 : n * 8 + 8], done.at[4 + n])
        groups.append(([copy], out))
    for copies, _ in groups:
        for copy in copies:
            copy.start()
    list_copy.wait()
    short = tile_mask(tiles, 4).astype(BF)
    gs[1, 256:272, :] = short
    gs[3, 256:272, :] = short
    for copies, out in groups:
        for copy in copies:
            copy.wait()
        out.start()
    for _, out in groups:
        out.wait()


def keep(array, out):
    pass


def far_tiles(count, win, tiles, tensor, far_right, far_left, flat, mask, ms):
    d = lax.axis_index("row")
    mine = window_at(win, d)
    funcs = tensor.shape[1] // 2
    start = lax.rem(lax.axis_index("grp"), 2) * funcs
    mask[...] = tile_mask(tiles, 32).astype(BF)
    for by, out in ((-1, far_left), (1, far_right)):
        base = near(d, by, count) * 2
        shape = (256, 128)
        row, lane = iota(shape, 0), iota(shape, 1)
        found = [find(mine, base), find(mine, base + 1)]
        here = pick4((row & 127) >> 5, mine) == base + ((lane & 63) >> 5)
        same = here & ((row & 31) == (lane & 31)) & ((row >> 7) == (lane >> 6))
        weight = jnp.where(row < 128, found[0][1], found[1][1])
        select = jnp.where(same, weight, 0.0).astype(BF)
        places = [pl.ds(pl.multiple_of(slot * 32, 32), 32) for slot, _ in found]
        masks = [mask[place, :] for place in places]
        for r in range(0, funcs, 8):
            sides = [
                jnp.concatenate([tensor[0, start + r + u, place, :] * m for u in range(8)], axis=0)
                for place, m in zip(places, masks)
            ]
            x = dot(jnp.concatenate(sides, axis=1), select)
            out[r * 32 : r * 32 + 256, :] = x.astype(BF)
    whole = mask[...]
    for r in range(2 * funcs):
        ms[r * PITCH : r * PITCH + 128, :] = (tensor[0, r] * whole).astype(F32)
    for m in range(128):
        rows = ms[pl.ds(m, 2 * funcs, stride=PITCH), :]
        flat[:, m * 128 : (m + 1) * 128] = rows.astype(BF)


def choose(count, win, g_self, g_before, g_after, g_far, out):
    d = lax.axis_index("row")
    atoms = 2 * count
    mine = window_at(win, d)
    theirs = window_at(win, near(d, -1, count))
    row0 = near(d, -2, count) * 2
    col0 = column_chunk(d, count) * 4

    def position(atom, start):
        return lax.rem(atom - start + atoms, atoms) * 32

    def whole(base):
        blocks = []
        for c in range(2):
            at = base + 64 * c
            blocks.append(
                jnp.concatenate(
                    [
                        g_far[at : at + 64, :],
                        g_before[at : at + 64, :],
                        g_self[at : at + 64, :],
                        g_after[at : at + 64, :],
                    ],
                    axis=0,
                )
            )
        return jnp.concatenate(blocks, axis=1)

    occ, virt = whole(0), whole(128)
    rows_mine = [position(a, row0) for a in mine]
    rows_theirs = [position(a, row0) for a in theirs]
    columns_mine = [position(a, col0) for a in mine]
    columns_both = []
    for i in range(4):
        _, there = find(theirs, mine[i])
        columns_both.append(jnp.where(there > 0, columns_mine[i], jnp.int32(MISSING)))
    for base, rows, columns in ((0, rows_mine, columns_mine), (256, rows_theirs, columns_both)):
        left = one_hot((128, 256), 0, columns)
        x = dot_t(left, occ).astype(BF)
        out[base : base + 128, :] = dot(x, one_hot((256, 128), 1, rows)).astype(BF)
        y = dot(one_hot((128, 256), 0, rows), virt).astype(BF)
        out[base + 128 : base + 256, :] = dot(y, one_hot((256, 128), 1, columns)).astype(BF)


def frame_map(atoms_from, wanted):
    bases = []
    for w in wanted:
        slot, there = find(atoms_from, w)
        bases.append(jnp.where(there > 0, slot * 32, jnp.int32(MISSING)))
    return one_hot((128, 128), 1, bases)


PITCH = 136


def halves(occ, blocks, outs):
    rows = occ.shape[0] // len(outs)
    for i in range(0, len(blocks), 2):
        m0, m1 = blocks[i](), blocks[i + 1]()
        h = dot(occ, jnp.concatenate([m0, m1], axis=1))
        for n, out in enumerate(outs):
            part = h[n * rows : (n + 1) * rows]
            out[i * PITCH : i * PITCH + 128, :] = part[:, :128]
            out[(i + 1) * PITCH : (i + 1) * PITCH + 128, :] = part[:, 128:]


def gather(ref, funcs, start):
    return [ref[pl.ds(start + t, funcs, stride=PITCH), :] for t in range(8)]


def dress(count, own, win, tiles, tensor, greens, *refs):
    if own:
        flat, polar0, dressed, far, hs, same = refs
    else:
        dressed, far, hs = refs
    d = lax.axis_index("row")
    funcs = tensor.shape[1]
    mine = window_at(win, d)
    theirs = window_at(win, near(d, -1, count))
    left, right = near(d, -1, count) * 2, near(d, 1, count) * 2
    mask = tile_mask(tiles, 32).astype(BF)
    occ, virt = greens[0:128, :], greens[128:256, :]
    halves(occ, [functools.partial(lambda r: tensor[0, r] * mask, r) for r in range(funcs)], [hs])
    wide, outs = dot(virt, frame_map(mine, theirs)).astype(BF), [dressed]
    if own:
        wide, outs = jnp.concatenate([virt, wide], axis=1), [same, dressed]
    lane = iota((128, 256), 1)
    atom = jnp.where(lane < 128, left, right)
    column_here = pick4(iota((128, 256), 0) >> 5, mine) == atom + ((lane & 63) >> 5)
    column_here = column_here & ((iota((128, 256), 0) & 31) == (lane & 31))
    both = dot(virt, jnp.where(column_here, 1.0, 0.0).astype(BF))
    row_atom = atom + ((lane & 127) >> 6)
    packs = jnp.concatenate([jnp.where(row_atom == a, both, 0.0).astype(BF) for a in mine], axis=0)
    for c in range(4):
        parts = []
        for i in range(4):
            parts.append(jnp.concatenate(gather(hs, funcs, i * 32 + c * 8), axis=0).astype(BF))
            x = dot(parts[-1], wide)
            for t in range(8):
                at = (i * 32 + c * 8 + t) * 128
                block = x[t * funcs : (t + 1) * funcs].astype(BF)
                for n, out in enumerate(outs):
                    out[:, at : at + 128] = block[:, n * 128 : (n + 1) * 128]
        x = dot(jnp.concatenate(parts, axis=1), packs)
        for t in range(8):
            at = (c * 8 + t) * 128
            block = x[t * funcs : (t + 1) * funcs].astype(BF)
            far[:, at : at + 128] = block[:, :128]
            far[:, 4096 + at : 4224 + at] = block[:, 128:]
    if own:
        polar0[...] = dot_t(same[...], flat[...])


def stacked(a, b, start, other):
    total = None
    for at in range(0, other.shape[1], 1024):
        left = jnp.concatenate([x[:, start + at : start + at + 1024] for x in (a, b)], axis=0)
        part = dot_t(left, other[:, at : at + 1024])
        total = part if total is None else total + part
    return total


def neighbour_mask(g_before):
    short = g_before[256:272, :].astype(F32)
    return jnp.concatenate(
        [jnp.broadcast_to(short[4 * i : 4 * i + 1, :], (32, 128)) for i in range(4)], axis=0
    ).astype(BF)


def join_back(tensor, g_before, g0, g1, flat, up, hs0, hs1, backs):
    funcs = tensor.shape[0]
    full = 2 * funcs
    mask = neighbour_mask(g_before)
    occ = jnp.concatenate([g0[256:384, :], g1[256:384, :]], axis=0)
    halves(occ, [functools.partial(lambda r: tensor[r] * mask, r) for r in range(funcs)], [hs0, hs1])
    virts = [g0[384:512, :], g1[384:512, :]]
    for i in range(16):
        xs = []
        for hs, virt in zip((hs0, hs1), virts):
            xs.append(dot(jnp.concatenate(gather(hs, funcs, i * 8), axis=0).astype(BF), virt))
        for t in range(8):
            at = (i * 8 + t) * 128
            part = slice(t * funcs, (t + 1) * funcs)
            backs[:, at : at + 128] = jnp.concatenate([x[part] for x in xs], axis=0).astype(BF)
    total = dot_t(backs[...], flat[...])
    up[...] = jnp.concatenate([total, jnp.zeros((full, 128 - full), F32)], axis=1)


def join(count, win, tensor, g_before, dressed0, dressed1, down, ms, moved):
    d = lax.axis_index("row")
    funcs = tensor.shape[0]
    full = 2 * funcs
    mine = window_at(win, d)
    theirs = window_at(win, near(d, -1, count))
    mask = neighbour_mask(g_before)
    for r in range(funcs):
        ms[r * PITCH : r * PITCH + 128, :] = (tensor[r] * mask).astype(F32)
    for i in range(16):
        slot, there = find(theirs, mine[i // 4])
        rows = gather(ms, funcs, slot * 32 + (i % 4) * 8)
        for t in range(8):
            at = (i * 8 + t) * 128
            moved[:, at : at + 128] = (rows[t] * there).astype(BF)
    total = stacked(dressed0, dressed1, 0, moved)
    down[...] = jnp.concatenate([total, jnp.zeros((2 * full, 128 - funcs), F32)], axis=1)


FAR_PITCH = 40


def join_far(far0, far1, from_left, from_right, down, after, own, other, es, turned):
    full = far0.shape[0]
    funcs = full // 2
    for e in (from_left, from_right):
        side = 0 if e is from_left else 1
        for r in range(funcs):
            at = r * FAR_PITCH
            es[side, at : at + 32, :] = e[r * 32 : (r + 1) * 32, :].astype(F32)
        for t in range(32):
            rows = es[side, pl.ds(t, funcs, stride=FAR_PITCH), :]
            turned[side, :, t * 128 : (t + 1) * 128] = rows.astype(BF)
    far_left = stacked(far0, far1, 0, turned.at[0])
    far_right = stacked(far0, far1, 4096, turned.at[1])
    padding = jnp.zeros((full, 128 - 3 * funcs - full), F32)
    for n, out in enumerate((own, other)):
        part = slice(n * full, (n + 1) * full)
        back = after[n * funcs : (n + 1) * funcs, :full]
        back = jnp.concatenate([back, jnp.zeros((funcs, full), F32)], axis=0)
        out[...] = jnp.concatenate(
            [far_left[part], down[part, :funcs], far_right[part], back, padding], axis=1
        )


def assemble(polar0, own, recv, out):
    is_first = lax.rem(lax.axis_index("grp"), 2) == 0
    full = polar0.shape[0]
    funcs = full // 2
    a, b = own[...], recv[...]
    low, high = jnp.where(is_first, a, b), jnp.where(is_first, b, a)
    back = slice(3 * funcs, 3 * funcs + full)
    after = jnp.concatenate([low[:funcs, back], high[:funcs, back]], axis=0)
    pieces = []
    for i in range(3):
        part = slice(i * funcs, (i + 1) * funcs)
        if i == 2:
            pieces += [polar0[...], after]
        pieces += [low[:, part], high[:, part]]
    out[...] = jnp.concatenate(pieces, axis=1)


def vmem(count):
    return [pl.BlockSpec(memory_space=pltpu.VMEM)] * count


def hbm(count):
    return [pl.BlockSpec(memory_space=pltpu.HBM)] * count


def smem(count):
    return [pl.BlockSpec(memory_space=pltpu.SMEM)] * count


def call(kernel, name, specs, outs, args, scratch=(), flops=0, limit=40 << 20, space=None, aliases={}):
    return pl.pallas_call(
        kernel,
        name=name,
        in_specs=specs,
        out_specs=tuple((space or vmem)(len(outs))),
        out_shape=tuple(outs),
        scratch_shapes=list(scratch),
        input_output_aliases=aliases,
        compiler_params=pltpu.CompilerParams(vmem_limit_bytes=limit),
        cost_estimate=pl.CostEstimate(flops=flops, bytes_accessed=0, transcendentals=0),
    )(*args)


def body(groups, count, green_occ, green_virt, coulomb3c, tile_list, window):
    full = coulomb3c.shape[1]
    funcs = full // 2
    shape = jax.ShapeDtypeStruct

    def send(array, row_by, swap=False):
        pairs = []
        for g in range(groups):
            for d in range(count):
                to = (g ^ 1 if swap else g) * count + (d + row_by) % count
                pairs.append((g * count + d, to))
        return lax.ppermute(array, ("grp", "row"), pairs)

    far_rows = funcs * 32
    g_self, g_right, g_left, g_far, tensor = call(
        functools.partial(first, count),
        "first",
        hbm(4),
        [
            shape((256, 128), BF),
            shape((272, 128), BF),
            shape((256, 128), BF),
            shape((272, 128), BF),
            shape((funcs, 128, 128), BF),
        ],
        (green_occ, green_virt, tile_list, coulomb3c),
        [
            pltpu.SMEM((1, 4, 4), jnp.int32),
            pltpu.VMEM((4, 272, 128), BF),
            pltpu.VMEM((funcs, 128, 128), BF),
            pltpu.SemaphoreType.DMA((20,)),
            pltpu.SemaphoreType.DMA((7,)),
        ],
        limit=60 << 20,
        space=hbm,
    )
    g_before = send(g_right, 1)
    g_beyond = send(g_far, 2)
    wide = send(tensor, 1)
    (g_left,) = call(
        keep,
        "keep",
        [pl.BlockSpec(memory_space=pl.ANY)],
        [shape((256, 128), BF)],
        (g_left,),
        flops=1 << 36,
        space=lambda n: [pl.BlockSpec(memory_space=pl.ANY)] * n,
        aliases={0: 0},
    )
    g_after = send(g_left, -1)
    flat_shape, far_shape = shape((full, 128 * 128), BF), shape((full, 64 * 128), BF)
    tall = pltpu.VMEM((full * PITCH, 128), F32)
    short = pltpu.VMEM((funcs * PITCH, 128), F32)
    message = shape((full, 128), F32)
    far_right, far_left, flat = call(
        functools.partial(far_tiles, count),
        "far_tiles",
        smem(2) + vmem(1),
        [shape((far_rows, 128), BF), shape((far_rows, 128), BF), flat_shape],
        (window, tile_list, coulomb3c),
        [pltpu.VMEM((128, 128), BF), tall],
    )
    g_before, g_after, g_beyond, far_right, far_left = lax.optimization_barrier(
        (g_before, g_after, g_beyond, far_right, far_left)
    )
    (mine,) = call(
        functools.partial(choose, count),
        "choose",
        smem(1) + vmem(4),
        [shape((512, 128), BF)],
        (window, g_self, g_before, g_after, g_beyond),
    )
    partner = send(mine, 0, True)
    far_right, far_left, mine = lax.optimization_barrier((far_right, far_left, mine))
    from_left = send(far_right, 2)
    from_right = send(far_left, -2)
    polar0, dressed0, far0 = call(
        functools.partial(dress, count, True),
        "dress_own",
        smem(2) + vmem(3),
        [shape((full, full), F32), flat_shape, far_shape],
        (window, tile_list, coulomb3c, mine, flat),
        [tall, pltpu.VMEM((full, 128 * 128), BF)],
    )
    dressed1, far1 = call(
        functools.partial(dress, count, False),
        "dress_partner",
        smem(2) + vmem(2),
        [flat_shape, far_shape],
        (window, tile_list, coulomb3c, partner),
        [tall],
    )
    (up,) = call(
        join_back,
        "join_back",
        vmem(5),
        [message],
        (wide, g_before, mine, partner, flat),
        [short, short, pltpu.VMEM((full, 128 * 128), BF)],
    )
    after = send(up, -1)
    (down,) = call(
        functools.partial(join, count),
        "join",
        smem(1) + vmem(4),
        [shape((2 * full, 128), F32)],
        (window, wide, g_before, dressed0, dressed1),
        [short, pltpu.VMEM((funcs, 128 * 128), BF)],
        flops=1 << 34,
    )
    own, other = call(
        join_far,
        "join_far",
        vmem(6),
        [message, message],
        (far0, far1, from_left, from_right, down, after),
        [pltpu.VMEM((2, funcs * FAR_PITCH, 128), F32), pltpu.VMEM((2, funcs, 32 * 128), BF)],
    )
    recv = send(other, 0, True)
    (out,) = call(
        assemble,
        "assemble",
        vmem(3),
        [shape((full, 5 * full), F32)],
        (polar0, own, recv),
    )
    return out


def solution(mesh):
    placed = (
        P(("grp", "row"), None),
        P(("grp", "row"), None),
        P("row", None, None, None),
        P("row", None, None),
        P(),
    )
    return jax.shard_map(
        functools.partial(body, mesh.shape["grp"], mesh.shape["row"]),
        mesh=mesh,
        in_specs=placed,
        out_specs=P(("grp", "row"), None),
        check_vma=False,
    )
```

```python
import functools

import jax
import jax.numpy as jnp
from jax import lax
from jax.experimental import pallas as pl
from jax.experimental.pallas import tpu as pltpu
from jax.sharding import PartitionSpec as P

BF = jnp.bfloat16
F32 = jnp.float32
MISSING = -(1 << 20)


def dot(a, b):
    return lax.dot_general(a, b, (((1,), (0,)), ((), ())), preferred_element_type=F32)


def dot_t(a, b):
    return lax.dot_general(a, b, (((1,), (1,)), ((), ())), preferred_element_type=F32)


def iota(shape, dim):
    return lax.broadcasted_iota(jnp.int32, shape, dim)


def pick4(index, values):
    return jnp.where(
        index == 0, values[0], jnp.where(index == 1, values[1], jnp.where(index == 2, values[2], values[3]))
    )


def one_hot(shape, dim, bases):
    index = iota(shape, dim)
    position = pick4(index >> 5, bases) + (index & 31)
    return jnp.where(iota(shape, 1 - dim) == position, 1.0, 0.0).astype(BF)


def window_at(win, row):
    return [win[row, i] for i in range(4)]


def find(atoms, wanted):
    slot, there = jnp.int32(0), jnp.float32(0)
    for i in range(4):
        hit = atoms[i] == wanted
        slot = jnp.where(hit, jnp.int32(i), slot)
        there = jnp.where(hit, jnp.float32(1), there)
    return slot, there


def tile_mask(tiles, rows):
    shape = (4 * rows, 128)
    row, lane = iota(shape, 0) // rows, iota(shape, 1) >> 5
    mask = jnp.zeros(shape, F32)
    for i in range(4):
        for j in range(4):
            mask = jnp.where((row == i) & (lane == j), tiles[0, i, j].astype(F32), mask)
    return mask


def near(row, by, count):
    return lax.rem(row + by + count, count)


def column_chunk(row, count):
    return near(row, -1, count) >> 1


def first(count, occ, virt, tiles_hbm, coulomb, *refs):
    outs, (tiles, gs, part, sem, done) = refs[:5], refs[5:]
    d = lax.axis_index("row")
    funcs = part.shape[0]
    half = lax.rem(lax.axis_index("grp"), 2)
    list_copy = pltpu.make_async_copy(tiles_hbm, tiles, sem.at[16])
    list_copy.start()
    groups = []
    for n, by in enumerate((0, 1, -1, 2)):
        start = column_chunk(near(d, by, count), count)
        copies = []
        for c in range(2):
            chunk = lax.rem(start + c, count // 2)
            columns = pl.ds(pl.multiple_of(chunk * 128, 128), 128)
            for base, green in ((0, occ), (128, virt)):
                at = base + 64 * c
                place = gs.at[n, at : at + 64]
                copies.append(pltpu.make_async_copy(green.at[:, columns], place, sem.at[4 * n + len(copies)]))
        rows = outs[n].shape[0]
        groups.append((copies, pltpu.make_async_copy(gs.at[n, 0:rows], outs[n], done.at[n])))
    for n in range(3):
        piece = pl.ds(half * funcs + n * 8, 8)
        copy = pltpu.make_async_copy(coulomb.at[0, piece], part.at[n * 8 : n * 8 + 8], sem.at[17 + n])
        out = pltpu.make_async_copy(part.at[n * 8 : n * 8 + 8], outs[4].at[n * 8 : n * 8 + 8], done.at[4 + n])
        groups.append(([copy], out))
    for copies, _ in groups:
        for copy in copies:
            copy.start()
    list_copy.wait()
    short = tile_mask(tiles, 4).astype(BF)
    for n in range(1, 4):
        for at in (256, 272, 288):
            gs[n, at : at + 16, :] = short
    for copies, out in groups:
        for copy in copies:
            copy.wait()
        out.start()
    for _, out in groups:
        out.wait()


def far_tiles(count, win, tiles, tensor, far_right, far_left, flat, mask, ms):
    d = lax.axis_index("row")
    mine = window_at(win, d)
    funcs = tensor.shape[1] // 2
    start = lax.rem(lax.axis_index("grp"), 2) * funcs
    mask[...] = tile_mask(tiles, 32).astype(BF)
    for by, out in ((-1, far_left), (1, far_right)):
        base = near(d, by, count) * 2
        shape = (256, 128)
        row, lane = iota(shape, 0), iota(shape, 1)
        found = [find(mine, base), find(mine, base + 1)]
        here = pick4((row & 127) >> 5, mine) == base + ((lane & 63) >> 5)
        same = here & ((row & 31) == (lane & 31)) & ((row >> 7) == (lane >> 6))
        weight = jnp.where(row < 128, found[0][1], found[1][1])
        select = jnp.where(same, weight, 0.0).astype(BF)
        places = [pl.ds(pl.multiple_of(slot * 32, 32), 32) for slot, _ in found]
        masks = [mask[place, :] for place in places]
        for r in range(0, funcs, 8):
            sides = [
                jnp.concatenate([tensor[0, start + r + u, place, :] * m for u in range(8)], axis=0)
                for place, m in zip(places, masks)
            ]
            x = dot(jnp.concatenate(sides, axis=1), select)
            out[r * 32 : r * 32 + 256, :] = x.astype(BF)
    whole = mask[...]
    for r in range(2 * funcs):
        ms[r * PITCH : r * PITCH + 128, :] = (tensor[0, r] * whole).astype(F32)
    for m in range(128):
        rows = ms[pl.ds(m, 2 * funcs, stride=PITCH), :]
        flat[:, m * 128 : (m + 1) * 128] = rows.astype(BF)


def choose(count, win, g_self, g_before, g_after, g_far, out):
    d = lax.axis_index("row")
    atoms = 2 * count
    mine = window_at(win, d)
    theirs = window_at(win, near(d, -1, count))
    row0 = near(d, -2, count) * 2
    col0 = column_chunk(d, count) * 4

    def position(atom, start):
        return lax.rem(atom - start + atoms, atoms) * 32

    def whole(base):
        blocks = []
        for c in range(2):
            at = base + 64 * c
            blocks.append(
                jnp.concatenate(
                    [
                        g_far[at : at + 64, :],
                        g_before[at : at + 64, :],
                        g_self[at : at + 64, :],
                        g_after[at : at + 64, :],
                    ],
                    axis=0,
                )
            )
        return jnp.concatenate(blocks, axis=1)

    occ, virt = whole(0), whole(128)
    rows_mine = [position(a, row0) for a in mine]
    rows_theirs = [position(a, row0) for a in theirs]
    columns_mine = [position(a, col0) for a in mine]
    columns_both = []
    for i in range(4):
        _, there = find(theirs, mine[i])
        columns_both.append(jnp.where(there > 0, columns_mine[i], jnp.int32(MISSING)))
    for base, rows, columns in ((0, rows_mine, columns_mine), (256, rows_theirs, columns_both)):
        left = one_hot((128, 256), 0, columns)
        x = dot_t(left, occ).astype(BF)
        out[base : base + 128, :] = dot(x, one_hot((256, 128), 1, rows)).astype(BF)
        y = dot(one_hot((128, 256), 0, rows), virt).astype(BF)
        out[base + 128 : base + 256, :] = dot(y, one_hot((256, 128), 1, columns)).astype(BF)


def frame_map(atoms_from, wanted):
    bases = []
    for w in wanted:
        slot, there = find(atoms_from, w)
        bases.append(jnp.where(there > 0, slot * 32, jnp.int32(MISSING)))
    return one_hot((128, 128), 1, bases)


PITCH = 136


def halves(occ, blocks, outs):
    rows = occ.shape[0] // len(outs)
    for i in range(0, len(blocks), 2):
        m0, m1 = blocks[i](), blocks[i + 1]()
        h = dot(occ, jnp.concatenate([m0, m1], axis=1))
        for n, out in enumerate(outs):
            part = h[n * rows : (n + 1) * rows]
            out[i * PITCH : i * PITCH + 128, :] = part[:, :128]
            out[(i + 1) * PITCH : (i + 1) * PITCH + 128, :] = part[:, 128:]


def gather(ref, funcs, start):
    return [ref[pl.ds(start + t, funcs, stride=PITCH), :] for t in range(8)]


def dress(count, own, win, tiles, tensor, greens, *refs):
    if own:
        flat, polar0, dressed, far, hs, same = refs
    else:
        dressed, far, hs = refs
    d = lax.axis_index("row")
    funcs = tensor.shape[1]
    mine = window_at(win, d)
    theirs = window_at(win, near(d, -1, count))
    left, right = near(d, -1, count) * 2, near(d, 1, count) * 2
    mask = tile_mask(tiles, 32).astype(BF)
    occ, virt = greens[0:128, :], greens[128:256, :]
    halves(occ, [functools.partial(lambda r: tensor[0, r] * mask, r) for r in range(funcs)], [hs])
    wide, outs = dot(virt, frame_map(mine, theirs)).astype(BF), [dressed]
    if own:
        wide, outs = jnp.concatenate([virt, wide], axis=1), [same, dressed]
    lane = iota((128, 256), 1)
    atom = jnp.where(lane < 128, left, right)
    column_here = pick4(iota((128, 256), 0) >> 5, mine) == atom + ((lane & 63) >> 5)
    column_here = column_here & ((iota((128, 256), 0) & 31) == (lane & 31))
    both = dot(virt, jnp.where(column_here, 1.0, 0.0).astype(BF))
    row_atom = atom + ((lane & 127) >> 6)
    packs = jnp.concatenate([jnp.where(row_atom == a, both, 0.0).astype(BF) for a in mine], axis=0)
    for c in range(4):
        parts = []
        for i in range(4):
            parts.append(jnp.concatenate(gather(hs, funcs, i * 32 + c * 8), axis=0).astype(BF))
            x = dot(parts[-1], wide)
            for t in range(8):
                at = (i * 32 + c * 8 + t) * 128
                block = x[t * funcs : (t + 1) * funcs].astype(BF)
                for n, out in enumerate(outs):
                    out[:, at : at + 128] = block[:, n * 128 : (n + 1) * 128]
        x = dot(jnp.concatenate(parts, axis=1), packs)
        for t in range(8):
            at = (c * 8 + t) * 128
            block = x[t * funcs : (t + 1) * funcs].astype(BF)
            far[:, at : at + 128] = block[:, :128]
            far[:, 4096 + at : 4224 + at] = block[:, 128:]
    if own:
        polar0[...] = dot_t(same[...], flat[...])


def stacked(a, b, start, other):
    total = None
    for at in range(0, other.shape[1], 1024):
        left = jnp.concatenate([x[:, start + at : start + at + 1024] for x in (a, b)], axis=0)
        part = dot_t(left, other[:, at : at + 1024])
        total = part if total is None else total + part
    return total


def neighbour_mask(g_before):
    short = g_before[256:272, :].astype(F32)
    return jnp.concatenate(
        [jnp.broadcast_to(short[4 * i : 4 * i + 1, :], (32, 128)) for i in range(4)], axis=0
    ).astype(BF)


def join_back(tensor, g_before, g0, g1, flat, up, hs0, hs1, backs):
    funcs = tensor.shape[0]
    full = 2 * funcs
    mask = neighbour_mask(g_before)
    occ = jnp.concatenate([g0[256:384, :], g1[256:384, :]], axis=0)
    halves(occ, [functools.partial(lambda r: tensor[r] * mask, r) for r in range(funcs)], [hs0, hs1])
    virts = [g0[384:512, :], g1[384:512, :]]
    for i in range(16):
        xs = []
        for hs, virt in zip((hs0, hs1), virts):
            xs.append(dot(jnp.concatenate(gather(hs, funcs, i * 8), axis=0).astype(BF), virt))
        for t in range(8):
            at = (i * 8 + t) * 128
            part = slice(t * funcs, (t + 1) * funcs)
            backs[:, at : at + 128] = jnp.concatenate([x[part] for x in xs], axis=0).astype(BF)
    total = dot_t(backs[...], flat[...])
    up[...] = jnp.concatenate([total, jnp.zeros((full, 128 - full), F32)], axis=1)


def join(count, win, tensor, g_before, dressed0, dressed1, down, ms, moved):
    d = lax.axis_index("row")
    funcs = tensor.shape[0]
    full = 2 * funcs
    mine = window_at(win, d)
    theirs = window_at(win, near(d, -1, count))
    mask = neighbour_mask(g_before)
    for r in range(funcs):
        ms[r * PITCH : r * PITCH + 128, :] = (tensor[r] * mask).astype(F32)
    for i in range(16):
        slot, there = find(theirs, mine[i // 4])
        rows = gather(ms, funcs, slot * 32 + (i % 4) * 8)
        for t in range(8):
            at = (i * 8 + t) * 128
            moved[:, at : at + 128] = (rows[t] * there).astype(BF)
    total = stacked(dressed0, dressed1, 0, moved)
    down[...] = jnp.concatenate([total, jnp.zeros((2 * full, 128 - funcs), F32)], axis=1)


FAR_PITCH = 40


def join_far(far0, far1, from_left, from_right, down, after, own, other, es, turned):
    full = far0.shape[0]
    funcs = full // 2
    for e in (from_left, from_right):
        side = 0 if e is from_left else 1
        for r in range(funcs):
            at = r * FAR_PITCH
            es[side, at : at + 32, :] = e[r * 32 : (r + 1) * 32, :].astype(F32)
        for t in range(32):
            rows = es[side, pl.ds(t, funcs, stride=FAR_PITCH), :]
            turned[side, :, t * 128 : (t + 1) * 128] = rows.astype(BF)
    far_left = stacked(far0, far1, 0, turned.at[0])
    far_right = stacked(far0, far1, 4096, turned.at[1])
    padding = jnp.zeros((full, 128 - 3 * funcs - full), F32)
    for n, out in enumerate((own, other)):
        part = slice(n * full, (n + 1) * full)
        back = after[n * funcs : (n + 1) * funcs, :full]
        back = jnp.concatenate([back, jnp.zeros((funcs, full), F32)], axis=0)
        out[...] = jnp.concatenate(
            [far_left[part], down[part, :funcs], far_right[part], back, padding], axis=1
        )


def assemble(polar0, own, recv, out):
    is_first = lax.rem(lax.axis_index("grp"), 2) == 0
    full = polar0.shape[0]
    funcs = full // 2
    a, b = own[...], recv[...]
    low, high = jnp.where(is_first, a, b), jnp.where(is_first, b, a)
    back = slice(3 * funcs, 3 * funcs + full)
    after = jnp.concatenate([low[:funcs, back], high[:funcs, back]], axis=0)
    pieces = []
    for i in range(3):
        part = slice(i * funcs, (i + 1) * funcs)
        if i == 2:
            pieces += [polar0[...], after]
        pieces += [low[:, part], high[:, part]]
    out[...] = jnp.concatenate(pieces, axis=1)


def vmem(count):
    return [pl.BlockSpec(memory_space=pltpu.VMEM)] * count


def hbm(count):
    return [pl.BlockSpec(memory_space=pltpu.HBM)] * count


def smem(count):
    return [pl.BlockSpec(memory_space=pltpu.SMEM)] * count


def call(kernel, name, specs, outs, args, scratch=(), flops=0, limit=40 << 20, space=None, aliases={}):
    return pl.pallas_call(
        kernel,
        name=name,
        in_specs=specs,
        out_specs=tuple((space or vmem)(len(outs))),
        out_shape=tuple(outs),
        scratch_shapes=list(scratch),
        input_output_aliases=aliases,
        compiler_params=pltpu.CompilerParams(vmem_limit_bytes=limit),
        cost_estimate=pl.CostEstimate(flops=flops, bytes_accessed=0, transcendentals=0),
    )(*args)


def body(groups, count, green_occ, green_virt, coulomb3c, tile_list, window):
    full = coulomb3c.shape[1]
    funcs = full // 2
    shape = jax.ShapeDtypeStruct

    def send(array, row_by, swap=False):
        pairs = []
        for g in range(groups):
            for d in range(count):
                to = (g ^ 1 if swap else g) * count + (d + row_by) % count
                pairs.append((g * count + d, to))
        return lax.ppermute(array, ("grp", "row"), pairs)

    far_rows = funcs * 32
    g_self, g_right, g_left, g_far, tensor = call(
        functools.partial(first, count),
        "first",
        hbm(4),
        [
            shape((256, 128), BF),
            shape((272, 128), BF),
            shape((304, 128), BF),
            shape((288, 128), BF),
            shape((funcs, 128, 128), BF),
        ],
        (green_occ, green_virt, tile_list, coulomb3c),
        [
            pltpu.SMEM((1, 4, 4), jnp.int32),
            pltpu.VMEM((4, 304, 128), BF),
            pltpu.VMEM((funcs, 128, 128), BF),
            pltpu.SemaphoreType.DMA((20,)),
            pltpu.SemaphoreType.DMA((7,)),
        ],
        limit=60 << 20,
        space=hbm,
    )
    g_before = send(g_right, 1)
    g_beyond = send(g_far, 2)
    g_after = send(g_left, -1)
    wide = send(tensor, 1)
    flat_shape, far_shape = shape((full, 128 * 128), BF), shape((full, 64 * 128), BF)
    tall = pltpu.VMEM((full * PITCH, 128), F32)
    short = pltpu.VMEM((funcs * PITCH, 128), F32)
    message = shape((full, 128), F32)
    far_right, far_left, flat = call(
        functools.partial(far_tiles, count),
        "far_tiles",
        smem(2) + vmem(1),
        [shape((far_rows, 128), BF), shape((far_rows, 128), BF), flat_shape],
        (window, tile_list, coulomb3c),
        [pltpu.VMEM((128, 128), BF), tall],
        flops=1 << 36,
    )
    g_before, g_after, g_beyond, far_right, far_left = lax.optimization_barrier(
        (g_before, g_after, g_beyond, far_right, far_left)
    )
    (mine,) = call(
        functools.partial(choose, count),
        "choose",
        smem(1) + vmem(4),
        [shape((512, 128), BF)],
        (window, g_self, g_before, g_after, g_beyond),
    )
    partner = send(mine, 0, True)
    far_right, far_left, mine = lax.optimization_barrier((far_right, far_left, mine))
    from_left = send(far_right, 2)
    from_right = send(far_left, -2)
    polar0, dressed0, far0 = call(
        functools.partial(dress, count, True),
        "dress_own",
        smem(2) + vmem(3),
        [shape((full, full), F32), flat_shape, far_shape],
        (window, tile_list, coulomb3c, mine, flat),
        [tall, pltpu.VMEM((full, 128 * 128), BF)],
    )
    dressed1, far1 = call(
        functools.partial(dress, count, False),
        "dress_partner",
        smem(2) + vmem(2),
        [flat_shape, far_shape],
        (window, tile_list, coulomb3c, partner),
        [tall],
    )
    (up,) = call(
        join_back,
        "join_back",
        vmem(5),
        [message],
        (wide, g_before, mine, partner, flat),
        [short, short, pltpu.VMEM((full, 128 * 128), BF)],
    )
    after = send(up, -1)
    (down,) = call(
        functools.partial(join, count),
        "join",
        smem(1) + vmem(4),
        [shape((2 * full, 128), F32)],
        (window, wide, g_before, dressed0, dressed1),
        [short, pltpu.VMEM((funcs, 128 * 128), BF)],
        flops=1 << 34,
    )
    own, other = call(
        join_far,
        "join_far",
        vmem(6),
        [message, message],
        (far0, far1, from_left, from_right, down, after),
        [pltpu.VMEM((2, funcs * FAR_PITCH, 128), F32), pltpu.VMEM((2, funcs, 32 * 128), BF)],
    )
    recv = send(other, 0, True)
    (out,) = call(
        assemble,
        "assemble",
        vmem(3),
        [shape((full, 5 * full), F32)],
        (polar0, own, recv),
    )
    return out


def solution(mesh):
    placed = (
        P(("grp", "row"), None),
        P(("grp", "row"), None),
        P("row", None, None, None),
        P("row", None, None),
        P(),
    )
    return jax.shard_map(
        functools.partial(body, mesh.shape["grp"], mesh.shape["row"]),
        mesh=mesh,
        in_specs=placed,
        out_specs=P(("grp", "row"), None),
        check_vma=False,
    )
```

```python
import functools

import jax
import jax.numpy as jnp
from jax import lax
from jax.experimental import pallas as pl
from jax.experimental.pallas import tpu as pltpu
from jax.sharding import PartitionSpec as P

BF = jnp.bfloat16
F32 = jnp.float32
MISSING = -(1 << 20)


def dot(a, b):
    return lax.dot_general(a, b, (((1,), (0,)), ((), ())), preferred_element_type=F32)


def dot_t(a, b):
    return lax.dot_general(a, b, (((1,), (1,)), ((), ())), preferred_element_type=F32)


def iota(shape, dim):
    return lax.broadcasted_iota(jnp.int32, shape, dim)


def pick4(index, values):
    return jnp.where(
        index == 0, values[0], jnp.where(index == 1, values[1], jnp.where(index == 2, values[2], values[3]))
    )


def one_hot(shape, dim, bases):
    index = iota(shape, dim)
    position = pick4(index >> 5, bases) + (index & 31)
    return jnp.where(iota(shape, 1 - dim) == position, 1.0, 0.0).astype(BF)


def window_at(win, row):
    return [win[row, i] for i in range(4)]


def find(atoms, wanted):
    slot, there = jnp.int32(0), jnp.float32(0)
    for i in range(4):
        hit = atoms[i] == wanted
        slot = jnp.where(hit, jnp.int32(i), slot)
        there = jnp.where(hit, jnp.float32(1), there)
    return slot, there


def tile_mask(tiles, rows):
    shape = (4 * rows, 128)
    row, lane = iota(shape, 0) // rows, iota(shape, 1) >> 5
    mask = jnp.zeros(shape, F32)
    for i in range(4):
        for j in range(4):
            mask = jnp.where((row == i) & (lane == j), tiles[0, i, j].astype(F32), mask)
    return mask


def near(row, by, count):
    return lax.rem(row + by + count, count)


def column_chunk(row, count):
    return near(row, -1, count) >> 1


def first(count, occ, virt, tiles_hbm, *refs):
    outs, (tiles, gs, sem, done) = refs[:4], refs[4:]
    d = lax.axis_index("row")
    list_copy = pltpu.make_async_copy(tiles_hbm, tiles, sem.at[16])
    groups = []
    for n, by in enumerate((0, 1, -1, 2)):
        start = column_chunk(near(d, by, count), count)
        copies = []
        for c in range(2):
            chunk = lax.rem(start + c, count // 2)
            columns = pl.ds(pl.multiple_of(chunk * 128, 128), 128)
            for base, green in ((0, occ), (128, virt)):
                at = base + 64 * c
                place = gs.at[n, at : at + 64]
                copies.append(pltpu.make_async_copy(green.at[:, columns], place, sem.at[4 * n + len(copies)]))
        rows = outs[n].shape[0]
        groups.append((copies, pltpu.make_async_copy(gs.at[n, 0:rows], outs[n], done.at[n])))
    list_copy.start()
    for copies, _ in groups:
        for copy in copies:
            copy.start()
    list_copy.wait()
    short = tile_mask(tiles, 4).astype(BF)
    for n in range(1, 4):
        for at in (256, 272, 288):
            gs[n, at : at + 16, :] = short
    for copies, out in groups:
        for copy in copies:
            copy.wait()
        out.start()
    for _, out in groups:
        out.wait()


def take_half(coulomb, tensor, part, sem, done):
    funcs = part.shape[0]
    start = lax.rem(lax.axis_index("grp"), 2) * funcs
    steps = []
    for n in range(3):
        rows = slice(n * 8, n * 8 + 8)
        copy = pltpu.make_async_copy(coulomb.at[0, pl.ds(start + n * 8, 8)], part.at[rows], sem.at[n])
        steps.append((copy, pltpu.make_async_copy(part.at[rows], tensor.at[rows], done.at[n])))
    for copy, _ in steps:
        copy.start()
    for copy, out in steps:
        copy.wait()
        out.start()
    for _, out in steps:
        out.wait()


def far_tiles(count, win, tiles, tensor, far_right, far_left, flat, mask, ms):
    d = lax.axis_index("row")
    mine = window_at(win, d)
    funcs = tensor.shape[1] // 2
    start = lax.rem(lax.axis_index("grp"), 2) * funcs
    mask[...] = tile_mask(tiles, 32).astype(BF)
    for by, out in ((-1, far_left), (1, far_right)):
        base = near(d, by, count) * 2
        shape = (256, 128)
        row, lane = iota(shape, 0), iota(shape, 1)
        found = [find(mine, base), find(mine, base + 1)]
        here = pick4((row & 127) >> 5, mine) == base + ((lane & 63) >> 5)
        same = here & ((row & 31) == (lane & 31)) & ((row >> 7) == (lane >> 6))
        weight = jnp.where(row < 128, found[0][1], found[1][1])
        select = jnp.where(same, weight, 0.0).astype(BF)
        places = [pl.ds(pl.multiple_of(slot * 32, 32), 32) for slot, _ in found]
        masks = [mask[place, :] for place in places]
        for r in range(0, funcs, 8):
            sides = [
                jnp.concatenate([tensor[0, start + r + u, place, :] * m for u in range(8)], axis=0)
                for place, m in zip(places, masks)
            ]
            x = dot(jnp.concatenate(sides, axis=1), select)
            out[r * 32 : r * 32 + 256, :] = x.astype(BF)
    whole = mask[...]
    for r in range(2 * funcs):
        ms[r * PITCH : r * PITCH + 128, :] = (tensor[0, r] * whole).astype(F32)
    for m in range(128):
        rows = ms[pl.ds(m, 2 * funcs, stride=PITCH), :]
        flat[:, m * 128 : (m + 1) * 128] = rows.astype(BF)


def choose(count, win, g_self, g_before, g_after, g_far, out):
    d = lax.axis_index("row")
    atoms = 2 * count
    mine = window_at(win, d)
    theirs = window_at(win, near(d, -1, count))
    row0 = near(d, -2, count) * 2
    col0 = column_chunk(d, count) * 4

    def position(atom, start):
        return lax.rem(atom - start + atoms, atoms) * 32

    def whole(base):
        blocks = []
        for c in range(2):
            at = base + 64 * c
            blocks.append(
                jnp.concatenate(
                    [
                        g_far[at : at + 64, :],
                        g_before[at : at + 64, :],
                        g_self[at : at + 64, :],
                        g_after[at : at + 64, :],
                    ],
                    axis=0,
                )
            )
        return jnp.concatenate(blocks, axis=1)

    occ, virt = whole(0), whole(128)
    rows_mine = [position(a, row0) for a in mine]
    rows_theirs = [position(a, row0) for a in theirs]
    columns_mine = [position(a, col0) for a in mine]
    columns_both = []
    for i in range(4):
        _, there = find(theirs, mine[i])
        columns_both.append(jnp.where(there > 0, columns_mine[i], jnp.int32(MISSING)))
    for base, rows, columns in ((0, rows_mine, columns_mine), (256, rows_theirs, columns_both)):
        left = one_hot((128, 256), 0, columns)
        x = dot_t(left, occ).astype(BF)
        out[base : base + 128, :] = dot(x, one_hot((256, 128), 1, rows)).astype(BF)
        y = dot(one_hot((128, 256), 0, rows), virt).astype(BF)
        out[base + 128 : base + 256, :] = dot(y, one_hot((256, 128), 1, columns)).astype(BF)


def frame_map(atoms_from, wanted):
    bases = []
    for w in wanted:
        slot, there = find(atoms_from, w)
        bases.append(jnp.where(there > 0, slot * 32, jnp.int32(MISSING)))
    return one_hot((128, 128), 1, bases)


PITCH = 136


def halves(occ, blocks, outs):
    rows = occ.shape[0] // len(outs)
    for i in range(0, len(blocks), 2):
        m0, m1 = blocks[i](), blocks[i + 1]()
        h = dot(occ, jnp.concatenate([m0, m1], axis=1))
        for n, out in enumerate(outs):
            part = h[n * rows : (n + 1) * rows]
            out[i * PITCH : i * PITCH + 128, :] = part[:, :128]
            out[(i + 1) * PITCH : (i + 1) * PITCH + 128, :] = part[:, 128:]


def gather(ref, funcs, start):
    return [ref[pl.ds(start + t, funcs, stride=PITCH), :] for t in range(8)]


def dress(count, own, win, tiles, tensor, greens, *refs):
    if own:
        flat, polar0, dressed, far, hs, same = refs
    else:
        dressed, far, hs = refs
    d = lax.axis_index("row")
    funcs = tensor.shape[1]
    mine = window_at(win, d)
    theirs = window_at(win, near(d, -1, count))
    left, right = near(d, -1, count) * 2, near(d, 1, count) * 2
    mask = tile_mask(tiles, 32).astype(BF)
    occ, virt = greens[0:128, :], greens[128:256, :]
    halves(occ, [functools.partial(lambda r: tensor[0, r] * mask, r) for r in range(funcs)], [hs])
    wide, outs = dot(virt, frame_map(mine, theirs)).astype(BF), [dressed]
    if own:
        wide, outs = jnp.concatenate([virt, wide], axis=1), [same, dressed]
    lane = iota((128, 256), 1)
    atom = jnp.where(lane < 128, left, right)
    column_here = pick4(iota((128, 256), 0) >> 5, mine) == atom + ((lane & 63) >> 5)
    column_here = column_here & ((iota((128, 256), 0) & 31) == (lane & 31))
    both = dot(virt, jnp.where(column_here, 1.0, 0.0).astype(BF))
    row_atom = atom + ((lane & 127) >> 6)
    packs = jnp.concatenate([jnp.where(row_atom == a, both, 0.0).astype(BF) for a in mine], axis=0)
    for c in range(4):
        parts = []
        for i in range(4):
            parts.append(jnp.concatenate(gather(hs, funcs, i * 32 + c * 8), axis=0).astype(BF))
            x = dot(parts[-1], wide)
            for t in range(8):
                at = (i * 32 + c * 8 + t) * 128
                block = x[t * funcs : (t + 1) * funcs].astype(BF)
                for n, out in enumerate(outs):
                    out[:, at : at + 128] = block[:, n * 128 : (n + 1) * 128]
        x = dot(jnp.concatenate(parts, axis=1), packs)
        for t in range(8):
            at = (c * 8 + t) * 128
            block = x[t * funcs : (t + 1) * funcs].astype(BF)
            far[:, at : at + 128] = block[:, :128]
            far[:, 4096 + at : 4224 + at] = block[:, 128:]
    if own:
        polar0[...] = dot_t(same[...], flat[...])


def stacked(a, b, start, other):
    total = None
    for at in range(0, other.shape[1], 1024):
        left = jnp.concatenate([x[:, start + at : start + at + 1024] for x in (a, b)], axis=0)
        part = dot_t(left, other[:, at : at + 1024])
        total = part if total is None else total + part
    return total


def neighbour_mask(g_before):
    short = g_before[256:272, :].astype(F32)
    return jnp.concatenate(
        [jnp.broadcast_to(short[4 * i : 4 * i + 1, :], (32, 128)) for i in range(4)], axis=0
    ).astype(BF)


def join_back(tensor, g_before, g0, g1, flat, up, hs0, hs1, backs):
    funcs = tensor.shape[0]
    full = 2 * funcs
    mask = neighbour_mask(g_before)
    occ = jnp.concatenate([g0[256:384, :], g1[256:384, :]], axis=0)
    halves(occ, [functools.partial(lambda r: tensor[r] * mask, r) for r in range(funcs)], [hs0, hs1])
    virts = [g0[384:512, :], g1[384:512, :]]
    for i in range(16):
        xs = []
        for hs, virt in zip((hs0, hs1), virts):
            xs.append(dot(jnp.concatenate(gather(hs, funcs, i * 8), axis=0).astype(BF), virt))
        for t in range(8):
            at = (i * 8 + t) * 128
            part = slice(t * funcs, (t + 1) * funcs)
            backs[:, at : at + 128] = jnp.concatenate([x[part] for x in xs], axis=0).astype(BF)
    total = dot_t(backs[...], flat[...])
    up[...] = jnp.concatenate([total, jnp.zeros((full, 128 - full), F32)], axis=1)


def join(count, win, tensor, g_before, dressed0, dressed1, down, ms, moved):
    d = lax.axis_index("row")
    funcs = tensor.shape[0]
    full = 2 * funcs
    mine = window_at(win, d)
    theirs = window_at(win, near(d, -1, count))
    mask = neighbour_mask(g_before)
    for r in range(funcs):
        ms[r * PITCH : r * PITCH + 128, :] = (tensor[r] * mask).astype(F32)
    for i in range(16):
        slot, there = find(theirs, mine[i // 4])
        rows = gather(ms, funcs, slot * 32 + (i % 4) * 8)
        for t in range(8):
            at = (i * 8 + t) * 128
            moved[:, at : at + 128] = (rows[t] * there).astype(BF)
    total = stacked(dressed0, dressed1, 0, moved)
    down[...] = jnp.concatenate([total, jnp.zeros((2 * full, 128 - funcs), F32)], axis=1)


FAR_PITCH = 40


def join_far(far0, far1, from_left, from_right, down, after, own, other, es, turned):
    full = far0.shape[0]
    funcs = full // 2
    for e in (from_left, from_right):
        side = 0 if e is from_left else 1
        for r in range(funcs):
            at = r * FAR_PITCH
            es[side, at : at + 32, :] = e[r * 32 : (r + 1) * 32, :].astype(F32)
        for t in range(32):
            rows = es[side, pl.ds(t, funcs, stride=FAR_PITCH), :]
            turned[side, :, t * 128 : (t + 1) * 128] = rows.astype(BF)
    far_left = stacked(far0, far1, 0, turned.at[0])
    far_right = stacked(far0, far1, 4096, turned.at[1])
    padding = jnp.zeros((full, 128 - 3 * funcs - full), F32)
    for n, out in enumerate((own, other)):
        part = slice(n * full, (n + 1) * full)
        back = after[n * funcs : (n + 1) * funcs, :full]
        back = jnp.concatenate([back, jnp.zeros((funcs, full), F32)], axis=0)
        out[...] = jnp.concatenate(
            [far_left[part], down[part, :funcs], far_right[part], back, padding], axis=1
        )


def assemble(polar0, own, recv, out):
    is_first = lax.rem(lax.axis_index("grp"), 2) == 0
    full = polar0.shape[0]
    funcs = full // 2
    a, b = own[...], recv[...]
    low, high = jnp.where(is_first, a, b), jnp.where(is_first, b, a)
    back = slice(3 * funcs, 3 * funcs + full)
    after = jnp.concatenate([low[:funcs, back], high[:funcs, back]], axis=0)
    pieces = []
    for i in range(3):
        part = slice(i * funcs, (i + 1) * funcs)
        if i == 2:
            pieces += [polar0[...], after]
        pieces += [low[:, part], high[:, part]]
    out[...] = jnp.concatenate(pieces, axis=1)


def vmem(count):
    return [pl.BlockSpec(memory_space=pltpu.VMEM)] * count


def hbm(count):
    return [pl.BlockSpec(memory_space=pltpu.HBM)] * count


def smem(count):
    return [pl.BlockSpec(memory_space=pltpu.SMEM)] * count


def call(kernel, name, specs, outs, args, scratch=(), flops=0, limit=40 << 20, space=None, aliases={}):
    return pl.pallas_call(
        kernel,
        name=name,
        in_specs=specs,
        out_specs=tuple((space or vmem)(len(outs))),
        out_shape=tuple(outs),
        scratch_shapes=list(scratch),
        input_output_aliases=aliases,
        compiler_params=pltpu.CompilerParams(vmem_limit_bytes=limit),
        cost_estimate=pl.CostEstimate(flops=flops, bytes_accessed=0, transcendentals=0),
    )(*args)


def body(groups, count, green_occ, green_virt, coulomb3c, tile_list, window):
    full = coulomb3c.shape[1]
    funcs = full // 2
    shape = jax.ShapeDtypeStruct

    def send(array, row_by, swap=False):
        pairs = []
        for g in range(groups):
            for d in range(count):
                to = (g ^ 1 if swap else g) * count + (d + row_by) % count
                pairs.append((g * count + d, to))
        return lax.ppermute(array, ("grp", "row"), pairs)

    far_rows = funcs * 32
    g_self, g_right, g_left, g_far = call(
        functools.partial(first, count),
        "first",
        hbm(3),
        [
            shape((256, 128), BF),
            shape((272, 128), BF),
            shape((304, 128), BF),
            shape((288, 128), BF),
        ],
        (green_occ, green_virt, tile_list),
        [
            pltpu.SMEM((1, 4, 4), jnp.int32),
            pltpu.VMEM((4, 304, 128), BF),
            pltpu.SemaphoreType.DMA((17,)),
            pltpu.SemaphoreType.DMA((4,)),
        ],
        limit=60 << 20,
        space=hbm,
    )
    g_before = send(g_right, 1)
    g_beyond = send(g_far, 2)
    g_after = send(g_left, -1)
    tensor, _ = lax.optimization_barrier((coulomb3c, g_self))
    (tensor,) = call(
        take_half,
        "take_half",
        hbm(1),
        [shape((funcs, 128, 128), BF)],
        (tensor,),
        [
            pltpu.VMEM((funcs, 128, 128), BF),
            pltpu.SemaphoreType.DMA((3,)),
            pltpu.SemaphoreType.DMA((3,)),
        ],
        limit=60 << 20,
        space=hbm,
    )
    wide = send(tensor, 1)
    flat_shape, far_shape = shape((full, 128 * 128), BF), shape((full, 64 * 128), BF)
    tall = pltpu.VMEM((full * PITCH, 128), F32)
    short = pltpu.VMEM((funcs * PITCH, 128), F32)
    message = shape((full, 128), F32)
    far_right, far_left, flat = call(
        functools.partial(far_tiles, count),
        "far_tiles",
        smem(2) + vmem(1),
        [shape((far_rows, 128), BF), shape((far_rows, 128), BF), flat_shape],
        (window, tile_list, coulomb3c),
        [pltpu.VMEM((128, 128), BF), tall],
        flops=1 << 36,
    )
    g_before, g_after, g_beyond, far_right, far_left = lax.optimization_barrier(
        (g_before, g_after, g_beyond, far_right, far_left)
    )
    (mine,) = call(
        functools.partial(choose, count),
        "choose",
        smem(1) + vmem(4),
        [shape((512, 128), BF)],
        (window, g_self, g_before, g_after, g_beyond),
    )
    partner = send(mine, 0, True)
    polar0, dressed0, far0 = call(
        functools.partial(dress, count, True),
        "dress_own",
        smem(2) + vmem(3),
        [shape((full, full), F32), flat_shape, far_shape],
        (window, tile_list, coulomb3c, mine, flat),
        [tall, pltpu.VMEM((full, 128 * 128), BF)],
    )
    far_right, far_left, polar0 = lax.optimization_barrier((far_right, far_left, polar0))
    from_left = send(far_right, 2)
    from_right = send(far_left, -2)
    dressed1, far1 = call(
        functools.partial(dress, count, False),
        "dress_partner",
        smem(2) + vmem(2),
        [flat_shape, far_shape],
        (window, tile_list, coulomb3c, partner),
        [tall],
    )
    (up,) = call(
        join_back,
        "join_back",
        vmem(5),
        [message],
        (wide, g_before, mine, partner, flat),
        [short, short, pltpu.VMEM((full, 128 * 128), BF)],
    )
    after = send(up, -1)
    (down,) = call(
        functools.partial(join, count),
        "join",
        smem(1) + vmem(4),
        [shape((2 * full, 128), F32)],
        (window, wide, g_before, dressed0, dressed1),
        [short, pltpu.VMEM((funcs, 128 * 128), BF)],
        flops=1 << 34,
    )
    own, other = call(
        join_far,
        "join_far",
        vmem(6),
        [message, message],
        (far0, far1, from_left, from_right, down, after),
        [pltpu.VMEM((2, funcs * FAR_PITCH, 128), F32), pltpu.VMEM((2, funcs, 32 * 128), BF)],
    )
    recv = send(other, 0, True)
    (out,) = call(
        assemble,
        "assemble",
        vmem(3),
        [shape((full, 5 * full), F32)],
        (polar0, own, recv),
    )
    return out


def solution(mesh):
    placed = (
        P(("grp", "row"), None),
        P(("grp", "row"), None),
        P("row", None, None, None),
        P("row", None, None),
        P(),
    )
    return jax.shard_map(
        functools.partial(body, mesh.shape["grp"], mesh.shape["row"]),
        mesh=mesh,
        in_specs=placed,
        out_specs=P(("grp", "row"), None),
        check_vma=False,
    )
```

```python
import functools

import jax
import jax.numpy as jnp
from jax import lax
from jax.experimental import pallas as pl
from jax.experimental.pallas import tpu as pltpu
from jax.sharding import PartitionSpec as P

BF = jnp.bfloat16
F32 = jnp.float32
MISSING = -(1 << 20)


def dot(a, b):
    return lax.dot_general(a, b, (((1,), (0,)), ((), ())), preferred_element_type=F32)


def dot_t(a, b):
    return lax.dot_general(a, b, (((1,), (1,)), ((), ())), preferred_element_type=F32)


def iota(shape, dim):
    return lax.broadcasted_iota(jnp.int32, shape, dim)


def pick4(index, values):
    return jnp.where(
        index == 0, values[0], jnp.where(index == 1, values[1], jnp.where(index == 2, values[2], values[3]))
    )


def one_hot(shape, dim, bases):
    index = iota(shape, dim)
    position = pick4(index >> 5, bases) + (index & 31)
    return jnp.where(iota(shape, 1 - dim) == position, 1.0, 0.0).astype(BF)


def window_at(win, row):
    return [win[row, i] for i in range(4)]


def find(atoms, wanted):
    slot, there = jnp.int32(0), jnp.float32(0)
    for i in range(4):
        hit = atoms[i] == wanted
        slot = jnp.where(hit, jnp.int32(i), slot)
        there = jnp.where(hit, jnp.float32(1), there)
    return slot, there


def tile_mask(tiles, rows):
    shape = (4 * rows, 128)
    row, lane = iota(shape, 0) // rows, iota(shape, 1) >> 5
    mask = jnp.zeros(shape, F32)
    for i in range(4):
        for j in range(4):
            mask = jnp.where((row == i) & (lane == j), tiles[0, i, j].astype(F32), mask)
    return mask


def near(row, by, count):
    return lax.rem(row + by + count, count)


def column_chunk(row, count):
    return near(row, -1, count) >> 1


def first(count, occ, virt, tiles_hbm, *refs):
    outs, (tiles, gs, sem, done) = refs[:4], refs[4:]
    d = lax.axis_index("row")
    list_copy = pltpu.make_async_copy(tiles_hbm, tiles, sem.at[16])
    groups = []
    for n, by in enumerate((0, 1, -1, 2)):
        start = column_chunk(near(d, by, count), count)
        copies = []
        for c in range(2):
            chunk = lax.rem(start + c, count // 2)
            columns = pl.ds(pl.multiple_of(chunk * 128, 128), 128)
            for base, green in ((0, occ), (128, virt)):
                at = base + 64 * c
                place = gs.at[n, at : at + 64]
                copies.append(pltpu.make_async_copy(green.at[:, columns], place, sem.at[4 * n + len(copies)]))
        rows = outs[n].shape[0]
        groups.append((copies, pltpu.make_async_copy(gs.at[n, 0:rows], outs[n], done.at[n])))
    list_copy.start()
    for copies, _ in groups:
        for copy in copies:
            copy.start()
    list_copy.wait()
    short = tile_mask(tiles, 4).astype(BF)
    for n in range(1, 4):
        for at in (256, 272, 288):
            gs[n, at : at + 16, :] = short
    for copies, out in groups:
        for copy in copies:
            copy.wait()
        out.start()
    for _, out in groups:
        out.wait()


def far_tiles(count, win, tiles, tensor, far_right, far_left, part, mask):
    d = lax.axis_index("row")
    mine = window_at(win, d)
    funcs = tensor.shape[1] // 2
    start = lax.rem(lax.axis_index("grp"), 2) * funcs
    mask[...] = tile_mask(tiles, 32).astype(BF)
    for r in range(funcs):
        part[r] = tensor[0, start + r]
    for by, out in ((-1, far_left), (1, far_right)):
        base = near(d, by, count) * 2
        shape = (256, 128)
        row, lane = iota(shape, 0), iota(shape, 1)
        found = [find(mine, base), find(mine, base + 1)]
        here = pick4((row & 127) >> 5, mine) == base + ((lane & 63) >> 5)
        same = here & ((row & 31) == (lane & 31)) & ((row >> 7) == (lane >> 6))
        weight = jnp.where(row < 128, found[0][1], found[1][1])
        select = jnp.where(same, weight, 0.0).astype(BF)
        places = [pl.ds(pl.multiple_of(slot * 32, 32), 32) for slot, _ in found]
        masks = [mask[place, :] for place in places]
        for r in range(0, funcs, 8):
            sides = [
                jnp.concatenate([tensor[0, start + r + u, place, :] * m for u in range(8)], axis=0)
                for place, m in zip(places, masks)
            ]
            x = dot(jnp.concatenate(sides, axis=1), select)
            out[r * 32 : r * 32 + 256, :] = x.astype(BF)


def flatten(tiles, tensor, flat, ms):
    funcs = tensor.shape[1]
    mask = tile_mask(tiles, 32).astype(BF)
    for r in range(funcs):
        ms[r * PITCH : r * PITCH + 128, :] = (tensor[0, r] * mask).astype(F32)
    for m in range(128):
        rows = ms[pl.ds(m, funcs, stride=PITCH), :]
        flat[:, m * 128 : (m + 1) * 128] = rows.astype(BF)


def choose(count, win, g_self, g_before, g_after, g_far, out):
    d = lax.axis_index("row")
    atoms = 2 * count
    mine = window_at(win, d)
    theirs = window_at(win, near(d, -1, count))
    row0 = near(d, -2, count) * 2
    col0 = column_chunk(d, count) * 4

    def position(atom, start):
        return lax.rem(atom - start + atoms, atoms) * 32

    def whole(base):
        blocks = []
        for c in range(2):
            at = base + 64 * c
            blocks.append(
                jnp.concatenate(
                    [
                        g_far[at : at + 64, :],
                        g_before[at : at + 64, :],
                        g_self[at : at + 64, :],
                        g_after[at : at + 64, :],
                    ],
                    axis=0,
                )
            )
        return jnp.concatenate(blocks, axis=1)

    occ, virt = whole(0), whole(128)
    rows_mine = [position(a, row0) for a in mine]
    rows_theirs = [position(a, row0) for a in theirs]
    columns_mine = [position(a, col0) for a in mine]
    columns_both = []
    for i in range(4):
        _, there = find(theirs, mine[i])
        columns_both.append(jnp.where(there > 0, columns_mine[i], jnp.int32(MISSING)))
    for base, rows, columns in ((0, rows_mine, columns_mine), (256, rows_theirs, columns_both)):
        left = one_hot((128, 256), 0, columns)
        x = dot_t(left, occ).astype(BF)
        out[base : base + 128, :] = dot(x, one_hot((256, 128), 1, rows)).astype(BF)
        y = dot(one_hot((128, 256), 0, rows), virt).astype(BF)
        out[base + 128 : base + 256, :] = dot(y, one_hot((256, 128), 1, columns)).astype(BF)


def frame_map(atoms_from, wanted):
    bases = []
    for w in wanted:
        slot, there = find(atoms_from, w)
        bases.append(jnp.where(there > 0, slot * 32, jnp.int32(MISSING)))
    return one_hot((128, 128), 1, bases)


PITCH = 136


def halves(occ, blocks, outs):
    rows = occ.shape[0] // len(outs)
    for i in range(0, len(blocks), 2):
        m0, m1 = blocks[i](), blocks[i + 1]()
        h = dot(occ, jnp.concatenate([m0, m1], axis=1))
        for n, out in enumerate(outs):
            part = h[n * rows : (n + 1) * rows]
            out[i * PITCH : i * PITCH + 128, :] = part[:, :128]
            out[(i + 1) * PITCH : (i + 1) * PITCH + 128, :] = part[:, 128:]


def gather(ref, funcs, start):
    return [ref[pl.ds(start + t, funcs, stride=PITCH), :] for t in range(8)]


def dress(count, own, win, tiles, tensor, greens, *refs):
    if own:
        flat, polar0, dressed, far, hs, same = refs
    else:
        dressed, far, hs = refs
    d = lax.axis_index("row")
    funcs = tensor.shape[1]
    mine = window_at(win, d)
    theirs = window_at(win, near(d, -1, count))
    left, right = near(d, -1, count) * 2, near(d, 1, count) * 2
    mask = tile_mask(tiles, 32).astype(BF)
    occ, virt = greens[0:128, :], greens[128:256, :]
    halves(occ, [functools.partial(lambda r: tensor[0, r] * mask, r) for r in range(funcs)], [hs])
    wide, outs = dot(virt, frame_map(mine, theirs)).astype(BF), [dressed]
    if own:
        wide, outs = jnp.concatenate([virt, wide], axis=1), [same, dressed]
    lane = iota((128, 256), 1)
    atom = jnp.where(lane < 128, left, right)
    column_here = pick4(iota((128, 256), 0) >> 5, mine) == atom + ((lane & 63) >> 5)
    column_here = column_here & ((iota((128, 256), 0) & 31) == (lane & 31))
    both = dot(virt, jnp.where(column_here, 1.0, 0.0).astype(BF))
    row_atom = atom + ((lane & 127) >> 6)
    packs = jnp.concatenate([jnp.where(row_atom == a, both, 0.0).astype(BF) for a in mine], axis=0)
    for c in range(4):
        parts = []
        for i in range(4):
            parts.append(jnp.concatenate(gather(hs, funcs, i * 32 + c * 8), axis=0).astype(BF))
            x = dot(parts[-1], wide)
            for t in range(8):
                at = (i * 32 + c * 8 + t) * 128
                block = x[t * funcs : (t + 1) * funcs].astype(BF)
                for n, out in enumerate(outs):
                    out[:, at : at + 128] = block[:, n * 128 : (n + 1) * 128]
        x = dot(jnp.concatenate(parts, axis=1), packs)
        for t in range(8):
            at = (c * 8 + t) * 128
            block = x[t * funcs : (t + 1) * funcs].astype(BF)
            far[:, at : at + 128] = block[:, :128]
            far[:, 4096 + at : 4224 + at] = block[:, 128:]
    if own:
        polar0[...] = dot_t(same[...], flat[...])


def stacked(a, b, start, other):
    total = None
    for at in range(0, other.shape[1], 1024):
        left = jnp.concatenate([x[:, start + at : start + at + 1024] for x in (a, b)], axis=0)
        part = dot_t(left, other[:, at : at + 1024])
        total = part if total is None else total + part
    return total


def neighbour_mask(g_before):
    short = g_before[256:272, :].astype(F32)
    return jnp.concatenate(
        [jnp.broadcast_to(short[4 * i : 4 * i + 1, :], (32, 128)) for i in range(4)], axis=0
    ).astype(BF)


def join_back(tensor, g_before, g0, g1, flat, up, hs0, hs1, backs):
    funcs = tensor.shape[0]
    full = 2 * funcs
    mask = neighbour_mask(g_before)
    occ = jnp.concatenate([g0[256:384, :], g1[256:384, :]], axis=0)
    halves(occ, [functools.partial(lambda r: tensor[r] * mask, r) for r in range(funcs)], [hs0, hs1])
    virts = [g0[384:512, :], g1[384:512, :]]
    for i in range(16):
        xs = []
        for hs, virt in zip((hs0, hs1), virts):
            xs.append(dot(jnp.concatenate(gather(hs, funcs, i * 8), axis=0).astype(BF), virt))
        for t in range(8):
            at = (i * 8 + t) * 128
            part = slice(t * funcs, (t + 1) * funcs)
            backs[:, at : at + 128] = jnp.concatenate([x[part] for x in xs], axis=0).astype(BF)
    total = dot_t(backs[...], flat[...])
    up[...] = jnp.concatenate([total, jnp.zeros((full, 128 - full), F32)], axis=1)


def join(count, win, tensor, g_before, dressed0, dressed1, down, ms, moved):
    d = lax.axis_index("row")
    funcs = tensor.shape[0]
    full = 2 * funcs
    mine = window_at(win, d)
    theirs = window_at(win, near(d, -1, count))
    mask = neighbour_mask(g_before)
    for r in range(funcs):
        ms[r * PITCH : r * PITCH + 128, :] = (tensor[r] * mask).astype(F32)
    for i in range(16):
        slot, there = find(theirs, mine[i // 4])
        rows = gather(ms, funcs, slot * 32 + (i % 4) * 8)
        for t in range(8):
            at = (i * 8 + t) * 128
            moved[:, at : at + 128] = (rows[t] * there).astype(BF)
    total = stacked(dressed0, dressed1, 0, moved)
    down[...] = jnp.concatenate([total, jnp.zeros((2 * full, 128 - funcs), F32)], axis=1)


FAR_PITCH = 40


def join_far(far0, far1, from_left, from_right, down, after, own, other, es, turned):
    full = far0.shape[0]
    funcs = full // 2
    for e in (from_left, from_right):
        side = 0 if e is from_left else 1
        for r in range(funcs):
            at = r * FAR_PITCH
            es[side, at : at + 32, :] = e[r * 32 : (r + 1) * 32, :].astype(F32)
        for t in range(32):
            rows = es[side, pl.ds(t, funcs, stride=FAR_PITCH), :]
            turned[side, :, t * 128 : (t + 1) * 128] = rows.astype(BF)
    far_left = stacked(far0, far1, 0, turned.at[0])
    far_right = stacked(far0, far1, 4096, turned.at[1])
    padding = jnp.zeros((full, 128 - 3 * funcs - full), F32)
    for n, out in enumerate((own, other)):
        part = slice(n * full, (n + 1) * full)
        back = after[n * funcs : (n + 1) * funcs, :full]
        back = jnp.concatenate([back, jnp.zeros((funcs, full), F32)], axis=0)
        out[...] = jnp.concatenate(
            [far_left[part], down[part, :funcs], far_right[part], back, padding], axis=1
        )


def assemble(polar0, own, recv, out):
    is_first = lax.rem(lax.axis_index("grp"), 2) == 0
    full = polar0.shape[0]
    funcs = full // 2
    a, b = own[...], recv[...]
    low, high = jnp.where(is_first, a, b), jnp.where(is_first, b, a)
    back = slice(3 * funcs, 3 * funcs + full)
    after = jnp.concatenate([low[:funcs, back], high[:funcs, back]], axis=0)
    pieces = []
    for i in range(3):
        part = slice(i * funcs, (i + 1) * funcs)
        if i == 2:
            pieces += [polar0[...], after]
        pieces += [low[:, part], high[:, part]]
    out[...] = jnp.concatenate(pieces, axis=1)


def vmem(count):
    return [pl.BlockSpec(memory_space=pltpu.VMEM)] * count


def hbm(count):
    return [pl.BlockSpec(memory_space=pltpu.HBM)] * count


def smem(count):
    return [pl.BlockSpec(memory_space=pltpu.SMEM)] * count


def call(kernel, name, specs, outs, args, scratch=(), flops=0, limit=40 << 20, space=None, aliases={}):
    return pl.pallas_call(
        kernel,
        name=name,
        in_specs=specs,
        out_specs=tuple((space or vmem)(len(outs))),
        out_shape=tuple(outs),
        scratch_shapes=list(scratch),
        input_output_aliases=aliases,
        compiler_params=pltpu.CompilerParams(vmem_limit_bytes=limit),
        cost_estimate=pl.CostEstimate(flops=flops, bytes_accessed=0, transcendentals=0),
    )(*args)


def body(groups, count, green_occ, green_virt, coulomb3c, tile_list, window):
    full = coulomb3c.shape[1]
    funcs = full // 2
    shape = jax.ShapeDtypeStruct

    def send(array, row_by, swap=False):
        pairs = []
        for g in range(groups):
            for d in range(count):
                to = (g ^ 1 if swap else g) * count + (d + row_by) % count
                pairs.append((g * count + d, to))
        return lax.ppermute(array, ("grp", "row"), pairs)

    far_rows = funcs * 32
    g_self, g_right, g_left, g_far = call(
        functools.partial(first, count),
        "first",
        hbm(3),
        [
            shape((256, 128), BF),
            shape((272, 128), BF),
            shape((304, 128), BF),
            shape((288, 128), BF),
        ],
        (green_occ, green_virt, tile_list),
        [
            pltpu.SMEM((1, 4, 4), jnp.int32),
            pltpu.VMEM((4, 304, 128), BF),
            pltpu.SemaphoreType.DMA((17,)),
            pltpu.SemaphoreType.DMA((4,)),
        ],
        limit=60 << 20,
        space=hbm,
    )
    g_before = send(g_right, 1)
    g_beyond = send(g_far, 2)
    g_after = send(g_left, -1)
    flat_shape, far_shape = shape((full, 128 * 128), BF), shape((full, 64 * 128), BF)
    tall = pltpu.VMEM((full * PITCH, 128), F32)
    short = pltpu.VMEM((funcs * PITCH, 128), F32)
    message = shape((full, 128), F32)
    far_right, far_left, tensor = call(
        functools.partial(far_tiles, count),
        "far_tiles",
        smem(2) + vmem(1),
        [shape((far_rows, 128), BF), shape((far_rows, 128), BF), shape((funcs, 128, 128), BF)],
        (window, tile_list, coulomb3c),
        [pltpu.VMEM((128, 128), BF)],
    )
    from_right = send(far_left, -2)
    wide = send(tensor, 1)
    here, _ = lax.optimization_barrier((tile_list, far_left))
    (flat,) = call(
        flatten,
        "flatten",
        smem(1) + vmem(1),
        [flat_shape],
        (here, coulomb3c),
        [tall],
        flops=1 << 36,
    )
    g_before, g_after, g_far, flat = lax.optimization_barrier((g_before, g_after, g_beyond, flat))
    (mine,) = call(
        functools.partial(choose, count),
        "choose",
        smem(1) + vmem(4),
        [shape((512, 128), BF)],
        (window, g_self, g_before, g_after, g_far),
    )
    partner = send(mine, 0, True)
    far_right, mine = lax.optimization_barrier((far_right, mine))
    from_left = send(far_right, 2)
    polar0, dressed0, far0 = call(
        functools.partial(dress, count, True),
        "dress_own",
        smem(2) + vmem(3),
        [shape((full, full), F32), flat_shape, far_shape],
        (window, tile_list, coulomb3c, mine, flat),
        [tall, pltpu.VMEM((full, 128 * 128), BF)],
    )
    partner, from_right = lax.optimization_barrier((partner, from_right))
    dressed1, far1 = call(
        functools.partial(dress, count, False),
        "dress_partner",
        smem(2) + vmem(2),
        [flat_shape, far_shape],
        (window, tile_list, coulomb3c, partner),
        [tall],
    )
    (up,) = call(
        join_back,
        "join_back",
        vmem(5),
        [message],
        (wide, g_before, mine, partner, flat),
        [short, short, pltpu.VMEM((full, 128 * 128), BF)],
    )
    after = send(up, -1)
    (down,) = call(
        functools.partial(join, count),
        "join",
        smem(1) + vmem(4),
        [shape((2 * full, 128), F32)],
        (window, wide, g_before, dressed0, dressed1),
        [short, pltpu.VMEM((funcs, 128 * 128), BF)],
        flops=1 << 34,
    )
    own, other = call(
        join_far,
        "join_far",
        vmem(6),
        [message, message],
        (far0, far1, from_left, from_right, down, after),
        [pltpu.VMEM((2, funcs * FAR_PITCH, 128), F32), pltpu.VMEM((2, funcs, 32 * 128), BF)],
    )
    recv = send(other, 0, True)
    (out,) = call(
        assemble,
        "assemble",
        vmem(3),
        [shape((full, 5 * full), F32)],
        (polar0, own, recv),
    )
    return out


def solution(mesh):
    placed = (
        P(("grp", "row"), None),
        P(("grp", "row"), None),
        P("row", None, None, None),
        P("row", None, None),
        P(),
    )
    return jax.shard_map(
        functools.partial(body, mesh.shape["grp"], mesh.shape["row"]),
        mesh=mesh,
        in_specs=placed,
        out_specs=P(("grp", "row"), None),
        check_vma=False,
    )
```

```python
import functools

import jax
import jax.numpy as jnp
from jax import lax
from jax.experimental import pallas as pl
from jax.experimental.pallas import tpu as pltpu
from jax.sharding import PartitionSpec as P

BF = jnp.bfloat16
F32 = jnp.float32
MISSING = -(1 << 20)


def dot(a, b):
    return lax.dot_general(a, b, (((1,), (0,)), ((), ())), preferred_element_type=F32)


def dot_t(a, b):
    return lax.dot_general(a, b, (((1,), (1,)), ((), ())), preferred_element_type=F32)


def iota(shape, dim):
    return lax.broadcasted_iota(jnp.int32, shape, dim)


def pick4(index, values):
    return jnp.where(
        index == 0, values[0], jnp.where(index == 1, values[1], jnp.where(index == 2, values[2], values[3]))
    )


def one_hot(shape, dim, bases):
    index = iota(shape, dim)
    position = pick4(index >> 5, bases) + (index & 31)
    return jnp.where(iota(shape, 1 - dim) == position, 1.0, 0.0).astype(BF)


def window_at(win, row):
    return [win[row, i] for i in range(4)]


def find(atoms, wanted):
    slot, there = jnp.int32(0), jnp.float32(0)
    for i in range(4):
        hit = atoms[i] == wanted
        slot = jnp.where(hit, jnp.int32(i), slot)
        there = jnp.where(hit, jnp.float32(1), there)
    return slot, there


def tile_mask(tiles, rows):
    shape = (4 * rows, 128)
    row, lane = iota(shape, 0) // rows, iota(shape, 1) >> 5
    mask = jnp.zeros(shape, F32)
    for i in range(4):
        for j in range(4):
            mask = jnp.where((row == i) & (lane == j), tiles[0, i, j].astype(F32), mask)
    return mask


def near(row, by, count):
    return lax.rem(row + by + count, count)


def column_chunk(row, count):
    return near(row, -1, count) >> 1


def first(count, occ, virt, tiles_hbm, coulomb, *refs):
    outs, (tiles, gs, part, sem, done) = refs[:5], refs[5:]
    d = lax.axis_index("row")
    funcs = part.shape[0]
    half = lax.rem(lax.axis_index("grp"), 2)
    list_copy = pltpu.make_async_copy(tiles_hbm, tiles, sem.at[16])
    list_copy.start()
    groups = []
    for n, by in enumerate((0, 1, -1, 2)):
        start = column_chunk(near(d, by, count), count)
        copies = []
        for c in range(2):
            chunk = lax.rem(start + c, count // 2)
            columns = pl.ds(pl.multiple_of(chunk * 128, 128), 128)
            for base, green in ((0, occ), (128, virt)):
                at = base + 64 * c
                place = gs.at[n, at : at + 64]
                copies.append(pltpu.make_async_copy(green.at[:, columns], place, sem.at[4 * n + len(copies)]))
        rows = outs[n].shape[0]
        groups.append((copies, pltpu.make_async_copy(gs.at[n, 0:rows], outs[n], done.at[n])))
    for n in range(3):
        piece = pl.ds(half * funcs + n * 8, 8)
        copy = pltpu.make_async_copy(coulomb.at[0, piece], part.at[n * 8 : n * 8 + 8], sem.at[17 + n])
        out = pltpu.make_async_copy(part.at[n * 8 : n * 8 + 8], outs[4].at[n * 8 : n * 8 + 8], done.at[4 + n])
        groups.append(([copy], out))
    for copies, _ in groups:
        for copy in copies:
            copy.start()
    list_copy.wait()
    short = tile_mask(tiles, 4).astype(BF)
    for n in range(1, 4):
        for at in (256, 272, 288):
            gs[n, at : at + 16, :] = short
    for copies, out in groups:
        for copy in copies:
            copy.wait()
        out.start()
    for _, out in groups:
        out.wait()


def far_tiles(count, win, tiles, tensor, far_right, far_left, flat, mask, ms):
    d = lax.axis_index("row")
    mine = window_at(win, d)
    funcs = tensor.shape[1] // 2
    start = lax.rem(lax.axis_index("grp"), 2) * funcs
    mask[...] = tile_mask(tiles, 32).astype(BF)
    for by, out in ((-1, far_left), (1, far_right)):
        base = near(d, by, count) * 2
        shape = (256, 128)
        row, lane = iota(shape, 0), iota(shape, 1)
        found = [find(mine, base), find(mine, base + 1)]
        here = pick4((row & 127) >> 5, mine) == base + ((lane & 63) >> 5)
        same = here & ((row & 31) == (lane & 31)) & ((row >> 7) == (lane >> 6))
        weight = jnp.where(row < 128, found[0][1], found[1][1])
        select = jnp.where(same, weight, 0.0).astype(BF)
        places = [pl.ds(pl.multiple_of(slot * 32, 32), 32) for slot, _ in found]
        masks = [mask[place, :] for place in places]
        for r in range(0, funcs, 8):
            sides = [
                jnp.concatenate([tensor[0, start + r + u, place, :] * m for u in range(8)], axis=0)
                for place, m in zip(places, masks)
            ]
            x = dot(jnp.concatenate(sides, axis=1), select)
            out[r * 32 : r * 32 + 256, :] = x.astype(BF)
    whole = mask[...]
    for r in range(2 * funcs):
        ms[r * PITCH : r * PITCH + 128, :] = (tensor[0, r] * whole).astype(F32)
    for m in range(128):
        rows = ms[pl.ds(m, 2 * funcs, stride=PITCH), :]
        flat[:, m * 128 : (m + 1) * 128] = rows.astype(BF)


def choose(count, win, g_self, g_before, g_after, g_far, out):
    d = lax.axis_index("row")
    atoms = 2 * count
    mine = window_at(win, d)
    theirs = window_at(win, near(d, -1, count))
    row0 = near(d, -2, count) * 2
    col0 = column_chunk(d, count) * 4

    def position(atom, start):
        return lax.rem(atom - start + atoms, atoms) * 32

    def whole(base):
        blocks = []
        for c in range(2):
            at = base + 64 * c
            blocks.append(
                jnp.concatenate(
                    [
                        g_far[at : at + 64, :],
                        g_before[at : at + 64, :],
                        g_self[at : at + 64, :],
                        g_after[at : at + 64, :],
                    ],
                    axis=0,
                )
            )
        return jnp.concatenate(blocks, axis=1)

    occ, virt = whole(0), whole(128)
    rows_mine = [position(a, row0) for a in mine]
    rows_theirs = [position(a, row0) for a in theirs]
    columns_mine = [position(a, col0) for a in mine]
    columns_both = []
    for i in range(4):
        _, there = find(theirs, mine[i])
        columns_both.append(jnp.where(there > 0, columns_mine[i], jnp.int32(MISSING)))
    for base, rows, columns in ((0, rows_mine, columns_mine), (256, rows_theirs, columns_both)):
        left = one_hot((128, 256), 0, columns)
        x = dot_t(left, occ).astype(BF)
        out[base : base + 128, :] = dot(x, one_hot((256, 128), 1, rows)).astype(BF)
        y = dot(one_hot((128, 256), 0, rows), virt).astype(BF)
        out[base + 128 : base + 256, :] = dot(y, one_hot((256, 128), 1, columns)).astype(BF)


def frame_map(atoms_from, wanted):
    bases = []
    for w in wanted:
        slot, there = find(atoms_from, w)
        bases.append(jnp.where(there > 0, slot * 32, jnp.int32(MISSING)))
    return one_hot((128, 128), 1, bases)


PITCH = 136


def halves(occ, blocks, outs):
    rows = occ.shape[0] // len(outs)
    for i in range(0, len(blocks), 2):
        m0, m1 = blocks[i](), blocks[i + 1]()
        h = dot(occ, jnp.concatenate([m0, m1], axis=1))
        for n, out in enumerate(outs):
            part = h[n * rows : (n + 1) * rows]
            out[i * PITCH : i * PITCH + 128, :] = part[:, :128]
            out[(i + 1) * PITCH : (i + 1) * PITCH + 128, :] = part[:, 128:]


def gather(ref, funcs, start):
    return [ref[pl.ds(start + t, funcs, stride=PITCH), :] for t in range(8)]


def dress(count, own, win, tiles, tensor, greens, *refs):
    if own:
        flat, polar0, dressed, far, hs, same = refs
    else:
        dressed, far, hs = refs
    d = lax.axis_index("row")
    funcs = tensor.shape[1]
    mine = window_at(win, d)
    theirs = window_at(win, near(d, -1, count))
    left, right = near(d, -1, count) * 2, near(d, 1, count) * 2
    mask = tile_mask(tiles, 32).astype(BF)
    occ, virt = greens[0:128, :], greens[128:256, :]
    halves(occ, [functools.partial(lambda r: tensor[0, r] * mask, r) for r in range(funcs)], [hs])
    wide, outs = dot(virt, frame_map(mine, theirs)).astype(BF), [dressed]
    if own:
        wide, outs = jnp.concatenate([virt, wide], axis=1), [same, dressed]
    lane = iota((128, 256), 1)
    atom = jnp.where(lane < 128, left, right)
    column_here = pick4(iota((128, 256), 0) >> 5, mine) == atom + ((lane & 63) >> 5)
    column_here = column_here & ((iota((128, 256), 0) & 31) == (lane & 31))
    both = dot(virt, jnp.where(column_here, 1.0, 0.0).astype(BF))
    row_atom = atom + ((lane & 127) >> 6)
    packs = jnp.concatenate([jnp.where(row_atom == a, both, 0.0).astype(BF) for a in mine], axis=0)
    for c in range(4):
        parts = []
        for i in range(4):
            parts.append(jnp.concatenate(gather(hs, funcs, i * 32 + c * 8), axis=0).astype(BF))
            x = dot(parts[-1], wide)
            for t in range(8):
                at = (i * 32 + c * 8 + t) * 128
                block = x[t * funcs : (t + 1) * funcs].astype(BF)
                for n, out in enumerate(outs):
                    out[:, at : at + 128] = block[:, n * 128 : (n + 1) * 128]
        x = dot(jnp.concatenate(parts, axis=1), packs)
        for t in range(8):
            at = (c * 8 + t) * 128
            block = x[t * funcs : (t + 1) * funcs].astype(BF)
            far[:, at : at + 128] = block[:, :128]
            far[:, 4096 + at : 4224 + at] = block[:, 128:]
    if own:
        polar0[...] = dot_t(same[...], flat[...])


def stacked(a, b, start, other):
    total = None
    for at in range(0, other.shape[1], 1024):
        left = jnp.concatenate([x[:, start + at : start + at + 1024] for x in (a, b)], axis=0)
        part = dot_t(left, other[:, at : at + 1024])
        total = part if total is None else total + part
    return total


def neighbour_mask(g_before):
    short = g_before[256:272, :].astype(F32)
    return jnp.concatenate(
        [jnp.broadcast_to(short[4 * i : 4 * i + 1, :], (32, 128)) for i in range(4)], axis=0
    ).astype(BF)


def join_back(tensor, g_before, g0, g1, flat, up, hs0, hs1, backs):
    funcs = tensor.shape[0]
    full = 2 * funcs
    mask = neighbour_mask(g_before)
    occ = jnp.concatenate([g0[256:384, :], g1[256:384, :]], axis=0)
    halves(occ, [functools.partial(lambda r: tensor[r] * mask, r) for r in range(funcs)], [hs0, hs1])
    virts = [g0[384:512, :], g1[384:512, :]]
    for i in range(16):
        xs = []
        for hs, virt in zip((hs0, hs1), virts):
            xs.append(dot(jnp.concatenate(gather(hs, funcs, i * 8), axis=0).astype(BF), virt))
        for t in range(8):
            at = (i * 8 + t) * 128
            part = slice(t * funcs, (t + 1) * funcs)
            backs[:, at : at + 128] = jnp.concatenate([x[part] for x in xs], axis=0).astype(BF)
    total = dot_t(backs[...], flat[...])
    up[...] = jnp.concatenate([total, jnp.zeros((full, 128 - full), F32)], axis=1)


def join(count, win, tensor, g_before, dressed0, dressed1, down, ms, moved):
    d = lax.axis_index("row")
    funcs = tensor.shape[0]
    full = 2 * funcs
    mine = window_at(win, d)
    theirs = window_at(win, near(d, -1, count))
    mask = neighbour_mask(g_before)
    for r in range(funcs):
        ms[r * PITCH : r * PITCH + 128, :] = (tensor[r] * mask).astype(F32)
    for i in range(16):
        slot, there = find(theirs, mine[i // 4])
        rows = gather(ms, funcs, slot * 32 + (i % 4) * 8)
        for t in range(8):
            at = (i * 8 + t) * 128
            moved[:, at : at + 128] = (rows[t] * there).astype(BF)
    total = stacked(dressed0, dressed1, 0, moved)
    down[...] = jnp.concatenate([total, jnp.zeros((2 * full, 128 - funcs), F32)], axis=1)


FAR_PITCH = 40


def join_far(far0, far1, from_left, from_right, down, after, own, other, es, turned):
    full = far0.shape[0]
    funcs = full // 2
    for e in (from_left, from_right):
        side = 0 if e is from_left else 1
        for r in range(funcs):
            at = r * FAR_PITCH
            es[side, at : at + 32, :] = e[r * 32 : (r + 1) * 32, :].astype(F32)
        for t in range(32):
            rows = es[side, pl.ds(t, funcs, stride=FAR_PITCH), :]
            turned[side, :, t * 128 : (t + 1) * 128] = rows.astype(BF)
    far_left = stacked(far0, far1, 0, turned.at[0])
    far_right = stacked(far0, far1, 4096, turned.at[1])
    padding = jnp.zeros((full, 128 - 3 * funcs - full), F32)
    for n, out in enumerate((own, other)):
        part = slice(n * full, (n + 1) * full)
        back = after[n * funcs : (n + 1) * funcs, :full]
        back = jnp.concatenate([back, jnp.zeros((funcs, full), F32)], axis=0)
        out[...] = jnp.concatenate(
            [far_left[part], down[part, :funcs], far_right[part], back, padding], axis=1
        )


def assemble(polar0, own, recv, out):
    is_first = lax.rem(lax.axis_index("grp"), 2) == 0
    full = polar0.shape[0]
    funcs = full // 2
    a, b = own[...], recv[...]
    low, high = jnp.where(is_first, a, b), jnp.where(is_first, b, a)
    back = slice(3 * funcs, 3 * funcs + full)
    after = jnp.concatenate([low[:funcs, back], high[:funcs, back]], axis=0)
    pieces = []
    for i in range(3):
        part = slice(i * funcs, (i + 1) * funcs)
        if i == 2:
            pieces += [polar0[...], after]
        pieces += [low[:, part], high[:, part]]
    out[...] = jnp.concatenate(pieces, axis=1)


def vmem(count):
    return [pl.BlockSpec(memory_space=pltpu.VMEM)] * count


def hbm(count):
    return [pl.BlockSpec(memory_space=pltpu.HBM)] * count


def smem(count):
    return [pl.BlockSpec(memory_space=pltpu.SMEM)] * count


def call(kernel, name, specs, outs, args, scratch=(), flops=0, limit=40 << 20, space=None, aliases={}):
    return pl.pallas_call(
        kernel,
        name=name,
        in_specs=specs,
        out_specs=tuple((space or vmem)(len(outs))),
        out_shape=tuple(outs),
        scratch_shapes=list(scratch),
        input_output_aliases=aliases,
        compiler_params=pltpu.CompilerParams(vmem_limit_bytes=limit),
        cost_estimate=pl.CostEstimate(flops=flops, bytes_accessed=0, transcendentals=0),
    )(*args)


def body(groups, count, green_occ, green_virt, coulomb3c, tile_list, window):
    full = coulomb3c.shape[1]
    funcs = full // 2
    shape = jax.ShapeDtypeStruct

    def send(array, row_by, swap=False):
        pairs = []
        for g in range(groups):
            for d in range(count):
                to = (g ^ 1 if swap else g) * count + (d + row_by) % count
                pairs.append((g * count + d, to))
        return lax.ppermute(array, ("grp", "row"), pairs)

    far_rows = funcs * 32
    g_self, g_right, g_left, g_far, tensor = call(
        functools.partial(first, count),
        "first",
        hbm(4),
        [
            shape((256, 128), BF),
            shape((272, 128), BF),
            shape((304, 128), BF),
            shape((288, 128), BF),
            shape((funcs, 128, 128), BF),
        ],
        (green_occ, green_virt, tile_list, coulomb3c),
        [
            pltpu.SMEM((1, 4, 4), jnp.int32),
            pltpu.VMEM((4, 304, 128), BF),
            pltpu.VMEM((funcs, 128, 128), BF),
            pltpu.SemaphoreType.DMA((20,)),
            pltpu.SemaphoreType.DMA((7,)),
        ],
        limit=60 << 20,
        space=hbm,
    )
    g_before = send(g_right, 1)
    g_beyond = send(g_far, 2)
    g_after = send(g_left, -1)
    wide = send(tensor, 1)
    flat_shape, far_shape = shape((full, 128 * 128), BF), shape((full, 64 * 128), BF)
    tall = pltpu.VMEM((full * PITCH, 128), F32)
    short = pltpu.VMEM((funcs * PITCH, 128), F32)
    message = shape((full, 128), F32)
    far_right, far_left, flat = call(
        functools.partial(far_tiles, count),
        "far_tiles",
        smem(2) + vmem(1),
        [shape((far_rows, 128), BF), shape((far_rows, 128), BF), flat_shape],
        (window, tile_list, coulomb3c),
        [pltpu.VMEM((128, 128), BF), tall],
        flops=1 << 36,
    )
    g_before, g_after, g_beyond, far_right, far_left = lax.optimization_barrier(
        (g_before, g_after, g_beyond, far_right, far_left)
    )
    (mine,) = call(
        functools.partial(choose, count),
        "choose",
        smem(1) + vmem(4),
        [shape((512, 128), BF)],
        (window, g_self, g_before, g_after, g_beyond),
    )
    partner = send(mine, 0, True)
    far_right, mine = lax.optimization_barrier((far_right, mine))
    from_left = send(far_right, 2)
    polar0, dressed0, far0 = call(
        functools.partial(dress, count, True),
        "dress_own",
        smem(2) + vmem(3),
        [shape((full, full), F32), flat_shape, far_shape],
        (window, tile_list, coulomb3c, mine, flat),
        [tall, pltpu.VMEM((full, 128 * 128), BF)],
    )
    far_left, polar0 = lax.optimization_barrier((far_left, polar0))
    from_right = send(far_left, -2)
    dressed1, far1 = call(
        functools.partial(dress, count, False),
        "dress_partner",
        smem(2) + vmem(2),
        [flat_shape, far_shape],
        (window, tile_list, coulomb3c, partner),
        [tall],
    )
    (up,) = call(
        join_back,
        "join_back",
        vmem(5),
        [message],
        (wide, g_before, mine, partner, flat),
        [short, short, pltpu.VMEM((full, 128 * 128), BF)],
    )
    after = send(up, -1)
    (down,) = call(
        functools.partial(join, count),
        "join",
        smem(1) + vmem(4),
        [shape((2 * full, 128), F32)],
        (window, wide, g_before, dressed0, dressed1),
        [short, pltpu.VMEM((funcs, 128 * 128), BF)],
        flops=1 << 34,
    )
    own, other = call(
        join_far,
        "join_far",
        vmem(6),
        [message, message],
        (far0, far1, from_left, from_right, down, after),
        [pltpu.VMEM((2, funcs * FAR_PITCH, 128), F32), pltpu.VMEM((2, funcs, 32 * 128), BF)],
    )
    recv = send(other, 0, True)
    (out,) = call(
        assemble,
        "assemble",
        vmem(3),
        [shape((full, 5 * full), F32)],
        (polar0, own, recv),
    )
    return out


def solution(mesh):
    placed = (
        P(("grp", "row"), None),
        P(("grp", "row"), None),
        P("row", None, None, None),
        P("row", None, None),
        P(),
    )
    return jax.shard_map(
        functools.partial(body, mesh.shape["grp"], mesh.shape["row"]),
        mesh=mesh,
        in_specs=placed,
        out_specs=P(("grp", "row"), None),
        check_vma=False,
    )
```

```python
import functools

import jax
import jax.numpy as jnp
from jax import lax
from jax.experimental import pallas as pl
from jax.experimental.pallas import tpu as pltpu
from jax.sharding import PartitionSpec as P

BF = jnp.bfloat16
F32 = jnp.float32
MISSING = -(1 << 20)


def dot(a, b):
    return lax.dot_general(a, b, (((1,), (0,)), ((), ())), preferred_element_type=F32)


def dot_t(a, b):
    return lax.dot_general(a, b, (((1,), (1,)), ((), ())), preferred_element_type=F32)


def iota(shape, dim):
    return lax.broadcasted_iota(jnp.int32, shape, dim)


def pick4(index, values):
    return jnp.where(
        index == 0, values[0], jnp.where(index == 1, values[1], jnp.where(index == 2, values[2], values[3]))
    )


def one_hot(shape, dim, bases):
    index = iota(shape, dim)
    position = pick4(index >> 5, bases) + (index & 31)
    return jnp.where(iota(shape, 1 - dim) == position, 1.0, 0.0).astype(BF)


def window_at(win, row):
    return [win[row, i] for i in range(4)]


def find(atoms, wanted):
    slot, there = jnp.int32(0), jnp.float32(0)
    for i in range(4):
        hit = atoms[i] == wanted
        slot = jnp.where(hit, jnp.int32(i), slot)
        there = jnp.where(hit, jnp.float32(1), there)
    return slot, there


def tile_mask(tiles, rows):
    shape = (4 * rows, 128)
    row, lane = iota(shape, 0) // rows, iota(shape, 1) >> 5
    mask = jnp.zeros(shape, F32)
    for i in range(4):
        for j in range(4):
            mask = jnp.where((row == i) & (lane == j), tiles[0, i, j].astype(F32), mask)
    return mask


def near(row, by, count):
    return lax.rem(row + by + count, count)


def column_chunk(row, count):
    return near(row, -1, count) >> 1


def first(count, occ, virt, tiles_hbm, coulomb, *refs):
    outs, (tiles, gs, part, sem, done) = refs[:5], refs[5:]
    d = lax.axis_index("row")
    funcs = part.shape[0]
    half = lax.rem(lax.axis_index("grp"), 2)
    list_copy = pltpu.make_async_copy(tiles_hbm, tiles, sem.at[16])
    list_copy.start()
    groups = []
    for n, by in enumerate((0, 1, -1, 2)):
        start = column_chunk(near(d, by, count), count)
        copies = []
        for c in range(2):
            chunk = lax.rem(start + c, count // 2)
            columns = pl.ds(pl.multiple_of(chunk * 128, 128), 128)
            for base, green in ((0, occ), (128, virt)):
                at = base + 64 * c
                place = gs.at[n, at : at + 64]
                copies.append(pltpu.make_async_copy(green.at[:, columns], place, sem.at[4 * n + len(copies)]))
        rows = outs[n].shape[0]
        groups.append((copies, pltpu.make_async_copy(gs.at[n, 0:rows], outs[n], done.at[n])))
    for n in range(3):
        piece = pl.ds(half * funcs + n * 8, 8)
        copy = pltpu.make_async_copy(coulomb.at[0, piece], part.at[n * 8 : n * 8 + 8], sem.at[17 + n])
        out = pltpu.make_async_copy(part.at[n * 8 : n * 8 + 8], outs[4].at[n * 8 : n * 8 + 8], done.at[4 + n])
        groups.append(([copy], out))
    for copies, _ in groups:
        for copy in copies:
            copy.start()
    list_copy.wait()
    short = tile_mask(tiles, 4).astype(BF)
    for n in range(1, 4):
        for at in (256, 272, 288):
            gs[n, at : at + 16, :] = short
    for copies, out in groups:
        for copy in copies:
            copy.wait()
        out.start()
    for _, out in groups:
        out.wait()


def far_tiles(count, win, tiles, tensor, token, far_right, far_left, mask):
    d = lax.axis_index("row")
    mine = window_at(win, d)
    funcs = tensor.shape[1] // 2
    start = lax.rem(lax.axis_index("grp"), 2) * funcs
    mask[...] = tile_mask(tiles, 32).astype(BF)
    for by, out in ((-1, far_left), (1, far_right)):
        base = near(d, by, count) * 2
        shape = (256, 128)
        row, lane = iota(shape, 0), iota(shape, 1)
        found = [find(mine, base), find(mine, base + 1)]
        here = pick4((row & 127) >> 5, mine) == base + ((lane & 63) >> 5)
        same = here & ((row & 31) == (lane & 31)) & ((row >> 7) == (lane >> 6))
        weight = jnp.where(row < 128, found[0][1], found[1][1])
        select = jnp.where(same, weight, 0.0).astype(BF)
        places = [pl.ds(pl.multiple_of(slot * 32, 32), 32) for slot, _ in found]
        masks = [mask[place, :] for place in places]
        for r in range(0, funcs, 8):
            sides = [
                jnp.concatenate([tensor[0, start + r + u, place, :] * m for u in range(8)], axis=0)
                for place, m in zip(places, masks)
            ]
            x = dot(jnp.concatenate(sides, axis=1), select)
            out[r * 32 : r * 32 + 256, :] = x.astype(BF)


def flatten(tiles, tensor, flat, ms):
    funcs = tensor.shape[1]
    mask = tile_mask(tiles, 32).astype(BF)
    for r in range(funcs):
        ms[r * PITCH : r * PITCH + 128, :] = (tensor[0, r] * mask).astype(F32)
    for m in range(128):
        rows = ms[pl.ds(m, funcs, stride=PITCH), :]
        flat[:, m * 128 : (m + 1) * 128] = rows.astype(BF)


def choose(count, win, g_self, g_before, g_after, g_far, out):
    d = lax.axis_index("row")
    atoms = 2 * count
    mine = window_at(win, d)
    theirs = window_at(win, near(d, -1, count))
    row0 = near(d, -2, count) * 2
    col0 = column_chunk(d, count) * 4

    def position(atom, start):
        return lax.rem(atom - start + atoms, atoms) * 32

    def whole(base):
        blocks = []
        for c in range(2):
            at = base + 64 * c
            blocks.append(
                jnp.concatenate(
                    [
                        g_far[at : at + 64, :],
                        g_before[at : at + 64, :],
                        g_self[at : at + 64, :],
                        g_after[at : at + 64, :],
                    ],
                    axis=0,
                )
            )
        return jnp.concatenate(blocks, axis=1)

    occ, virt = whole(0), whole(128)
    rows_mine = [position(a, row0) for a in mine]
    rows_theirs = [position(a, row0) for a in theirs]
    columns_mine = [position(a, col0) for a in mine]
    columns_both = []
    for i in range(4):
        _, there = find(theirs, mine[i])
        columns_both.append(jnp.where(there > 0, columns_mine[i], jnp.int32(MISSING)))
    for base, rows, columns in ((0, rows_mine, columns_mine), (256, rows_theirs, columns_both)):
        left = one_hot((128, 256), 0, columns)
        x = dot_t(left, occ).astype(BF)
        out[base : base + 128, :] = dot(x, one_hot((256, 128), 1, rows)).astype(BF)
        y = dot(one_hot((128, 256), 0, rows), virt).astype(BF)
        out[base + 128 : base + 256, :] = dot(y, one_hot((256, 128), 1, columns)).astype(BF)


def frame_map(atoms_from, wanted):
    bases = []
    for w in wanted:
        slot, there = find(atoms_from, w)
        bases.append(jnp.where(there > 0, slot * 32, jnp.int32(MISSING)))
    return one_hot((128, 128), 1, bases)


PITCH = 136


def halves(occ, blocks, outs):
    rows = occ.shape[0] // len(outs)
    for i in range(0, len(blocks), 2):
        m0, m1 = blocks[i](), blocks[i + 1]()
        h = dot(occ, jnp.concatenate([m0, m1], axis=1))
        for n, out in enumerate(outs):
            part = h[n * rows : (n + 1) * rows]
            out[i * PITCH : i * PITCH + 128, :] = part[:, :128]
            out[(i + 1) * PITCH : (i + 1) * PITCH + 128, :] = part[:, 128:]


def gather(ref, funcs, start):
    return [ref[pl.ds(start + t, funcs, stride=PITCH), :] for t in range(8)]


def dress(count, own, win, tiles, tensor, greens, *refs):
    if own:
        flat, polar0, dressed, far, hs, same = refs
    else:
        dressed, far, hs = refs
    d = lax.axis_index("row")
    funcs = tensor.shape[1]
    mine = window_at(win, d)
    theirs = window_at(win, near(d, -1, count))
    left, right = near(d, -1, count) * 2, near(d, 1, count) * 2
    mask = tile_mask(tiles, 32).astype(BF)
    occ, virt = greens[0:128, :], greens[128:256, :]
    halves(occ, [functools.partial(lambda r: tensor[0, r] * mask, r) for r in range(funcs)], [hs])
    wide, outs = dot(virt, frame_map(mine, theirs)).astype(BF), [dressed]
    if own:
        wide, outs = jnp.concatenate([virt, wide], axis=1), [same, dressed]
    lane = iota((128, 256), 1)
    atom = jnp.where(lane < 128, left, right)
    column_here = pick4(iota((128, 256), 0) >> 5, mine) == atom + ((lane & 63) >> 5)
    column_here = column_here & ((iota((128, 256), 0) & 31) == (lane & 31))
    both = dot(virt, jnp.where(column_here, 1.0, 0.0).astype(BF))
    row_atom = atom + ((lane & 127) >> 6)
    packs = jnp.concatenate([jnp.where(row_atom == a, both, 0.0).astype(BF) for a in mine], axis=0)
    for c in range(4):
        parts = []
        for i in range(4):
            parts.append(jnp.concatenate(gather(hs, funcs, i * 32 + c * 8), axis=0).astype(BF))
            x = dot(parts[-1], wide)
            for t in range(8):
                at = (i * 32 + c * 8 + t) * 128
                block = x[t * funcs : (t + 1) * funcs].astype(BF)
                for n, out in enumerate(outs):
                    out[:, at : at + 128] = block[:, n * 128 : (n + 1) * 128]
        x = dot(jnp.concatenate(parts, axis=1), packs)
        for t in range(8):
            at = (c * 8 + t) * 128
            block = x[t * funcs : (t + 1) * funcs].astype(BF)
            far[:, at : at + 128] = block[:, :128]
            far[:, 4096 + at : 4224 + at] = block[:, 128:]
    if own:
        polar0[...] = dot_t(same[...], flat[...])


def stacked(a, b, start, other):
    total = None
    for at in range(0, other.shape[1], 1024):
        left = jnp.concatenate([x[:, start + at : start + at + 1024] for x in (a, b)], axis=0)
        part = dot_t(left, other[:, at : at + 1024])
        total = part if total is None else total + part
    return total


def neighbour_mask(g_before):
    short = g_before[256:272, :].astype(F32)
    return jnp.concatenate(
        [jnp.broadcast_to(short[4 * i : 4 * i + 1, :], (32, 128)) for i in range(4)], axis=0
    ).astype(BF)


def join_back(tensor, g_before, g0, g1, flat, up, hs0, hs1, backs):
    funcs = tensor.shape[0]
    full = 2 * funcs
    mask = neighbour_mask(g_before)
    occ = jnp.concatenate([g0[256:384, :], g1[256:384, :]], axis=0)
    halves(occ, [functools.partial(lambda r: tensor[r] * mask, r) for r in range(funcs)], [hs0, hs1])
    virts = [g0[384:512, :], g1[384:512, :]]
    for i in range(16):
        xs = []
        for hs, virt in zip((hs0, hs1), virts):
            xs.append(dot(jnp.concatenate(gather(hs, funcs, i * 8), axis=0).astype(BF), virt))
        for t in range(8):
            at = (i * 8 + t) * 128
            part = slice(t * funcs, (t + 1) * funcs)
            backs[:, at : at + 128] = jnp.concatenate([x[part] for x in xs], axis=0).astype(BF)
    total = dot_t(backs[...], flat[...])
    up[...] = jnp.concatenate([total, jnp.zeros((full, 128 - full), F32)], axis=1)


def join(count, win, tensor, g_before, dressed0, dressed1, down, ms, moved):
    d = lax.axis_index("row")
    funcs = tensor.shape[0]
    full = 2 * funcs
    mine = window_at(win, d)
    theirs = window_at(win, near(d, -1, count))
    mask = neighbour_mask(g_before)
    for r in range(funcs):
        ms[r * PITCH : r * PITCH + 128, :] = (tensor[r] * mask).astype(F32)
    for i in range(16):
        slot, there = find(theirs, mine[i // 4])
        rows = gather(ms, funcs, slot * 32 + (i % 4) * 8)
        for t in range(8):
            at = (i * 8 + t) * 128
            moved[:, at : at + 128] = (rows[t] * there).astype(BF)
    total = stacked(dressed0, dressed1, 0, moved)
    down[...] = jnp.concatenate([total, jnp.zeros((2 * full, 128 - funcs), F32)], axis=1)


FAR_PITCH = 40


def join_far(far0, far1, from_left, from_right, down, after, own, other, es, turned):
    full = far0.shape[0]
    funcs = full // 2
    for e in (from_left, from_right):
        side = 0 if e is from_left else 1
        for r in range(funcs):
            at = r * FAR_PITCH
            es[side, at : at + 32, :] = e[r * 32 : (r + 1) * 32, :].astype(F32)
        for t in range(32):
            rows = es[side, pl.ds(t, funcs, stride=FAR_PITCH), :]
            turned[side, :, t * 128 : (t + 1) * 128] = rows.astype(BF)
    far_left = stacked(far0, far1, 0, turned.at[0])
    far_right = stacked(far0, far1, 4096, turned.at[1])
    padding = jnp.zeros((full, 128 - 3 * funcs - full), F32)
    for n, out in enumerate((own, other)):
        part = slice(n * full, (n + 1) * full)
        back = after[n * funcs : (n + 1) * funcs, :full]
        back = jnp.concatenate([back, jnp.zeros((funcs, full), F32)], axis=0)
        out[...] = jnp.concatenate(
            [far_left[part], down[part, :funcs], far_right[part], back, padding], axis=1
        )


def assemble(polar0, own, recv, out):
    is_first = lax.rem(lax.axis_index("grp"), 2) == 0
    full = polar0.shape[0]
    funcs = full // 2
    a, b = own[...], recv[...]
    low, high = jnp.where(is_first, a, b), jnp.where(is_first, b, a)
    back = slice(3 * funcs, 3 * funcs + full)
    after = jnp.concatenate([low[:funcs, back], high[:funcs, back]], axis=0)
    pieces = []
    for i in range(3):
        part = slice(i * funcs, (i + 1) * funcs)
        if i == 2:
            pieces += [polar0[...], after]
        pieces += [low[:, part], high[:, part]]
    out[...] = jnp.concatenate(pieces, axis=1)


def vmem(count):
    return [pl.BlockSpec(memory_space=pltpu.VMEM)] * count


def hbm(count):
    return [pl.BlockSpec(memory_space=pltpu.HBM)] * count


def smem(count):
    return [pl.BlockSpec(memory_space=pltpu.SMEM)] * count


def call(kernel, name, specs, outs, args, scratch=(), flops=0, limit=40 << 20, space=None, aliases={}):
    return pl.pallas_call(
        kernel,
        name=name,
        in_specs=specs,
        out_specs=tuple((space or vmem)(len(outs))),
        out_shape=tuple(outs),
        scratch_shapes=list(scratch),
        input_output_aliases=aliases,
        compiler_params=pltpu.CompilerParams(vmem_limit_bytes=limit),
        cost_estimate=pl.CostEstimate(flops=flops, bytes_accessed=0, transcendentals=0),
    )(*args)


def body(groups, count, green_occ, green_virt, coulomb3c, tile_list, window):
    full = coulomb3c.shape[1]
    funcs = full // 2
    shape = jax.ShapeDtypeStruct

    def send(array, row_by, swap=False):
        pairs = []
        for g in range(groups):
            for d in range(count):
                to = (g ^ 1 if swap else g) * count + (d + row_by) % count
                pairs.append((g * count + d, to))
        return lax.ppermute(array, ("grp", "row"), pairs)

    far_rows = funcs * 32
    g_self, g_right, g_left, g_far, tensor = call(
        functools.partial(first, count),
        "first",
        hbm(4),
        [
            shape((256, 128), BF),
            shape((272, 128), BF),
            shape((304, 128), BF),
            shape((288, 128), BF),
            shape((funcs, 128, 128), BF),
        ],
        (green_occ, green_virt, tile_list, coulomb3c),
        [
            pltpu.SMEM((1, 4, 4), jnp.int32),
            pltpu.VMEM((4, 304, 128), BF),
            pltpu.VMEM((funcs, 128, 128), BF),
            pltpu.SemaphoreType.DMA((20,)),
            pltpu.SemaphoreType.DMA((7,)),
        ],
        limit=60 << 20,
        space=hbm,
    )
    g_before = send(g_right, 1)
    g_beyond = send(g_far, 2)
    g_after = send(g_left, -1)
    wide = send(tensor, 1)
    flat_shape, far_shape = shape((full, 128 * 128), BF), shape((full, 64 * 128), BF)
    tall = pltpu.VMEM((full * PITCH, 128), F32)
    short = pltpu.VMEM((funcs * PITCH, 128), F32)
    message = shape((full, 128), F32)
    far_right, far_left = call(
        functools.partial(far_tiles, count),
        "far_tiles",
        smem(2) + vmem(1) + [pl.BlockSpec(memory_space=pl.ANY)],
        [shape((far_rows, 128), BF), shape((far_rows, 128), BF)],
        (window, tile_list, coulomb3c, g_self),
        [pltpu.VMEM((128, 128), BF)],
    )
    from_right = send(far_left, -2)
    here, _ = lax.optimization_barrier((tile_list, far_left))
    (flat,) = call(
        flatten,
        "flatten",
        smem(1) + vmem(1),
        [flat_shape],
        (here, coulomb3c),
        [tall],
        flops=1 << 36,
    )
    g_before, g_after, g_beyond, flat = lax.optimization_barrier((g_before, g_after, g_beyond, flat))
    (mine,) = call(
        functools.partial(choose, count),
        "choose",
        smem(1) + vmem(4),
        [shape((512, 128), BF)],
        (window, g_self, g_before, g_after, g_beyond),
    )
    partner = send(mine, 0, True)
    far_right, mine = lax.optimization_barrier((far_right, mine))
    from_left = send(far_right, 2)
    polar0, dressed0, far0 = call(
        functools.partial(dress, count, True),
        "dress_own",
        smem(2) + vmem(3),
        [shape((full, full), F32), flat_shape, far_shape],
        (window, tile_list, coulomb3c, mine, flat),
        [tall, pltpu.VMEM((full, 128 * 128), BF)],
    )
    dressed1, far1 = call(
        functools.partial(dress, count, False),
        "dress_partner",
        smem(2) + vmem(2),
        [flat_shape, far_shape],
        (window, tile_list, coulomb3c, partner),
        [tall],
    )
    wide, from_right = lax.optimization_barrier((wide, from_right))
    (up,) = call(
        join_back,
        "join_back",
        vmem(5),
        [message],
        (wide, g_before, mine, partner, flat),
        [short, short, pltpu.VMEM((full, 128 * 128), BF)],
    )
    after = send(up, -1)
    (down,) = call(
        functools.partial(join, count),
        "join",
        smem(1) + vmem(4),
        [shape((2 * full, 128), F32)],
        (window, wide, g_before, dressed0, dressed1),
        [short, pltpu.VMEM((funcs, 128 * 128), BF)],
        flops=1 << 34,
    )
    own, other = call(
        join_far,
        "join_far",
        vmem(6),
        [message, message],
        (far0, far1, from_left, from_right, down, after),
        [pltpu.VMEM((2, funcs * FAR_PITCH, 128), F32), pltpu.VMEM((2, funcs, 32 * 128), BF)],
    )
    recv = send(other, 0, True)
    (out,) = call(
        assemble,
        "assemble",
        vmem(3),
        [shape((full, 5 * full), F32)],
        (polar0, own, recv),
    )
    return out


def solution(mesh):
    placed = (
        P(("grp", "row"), None),
        P(("grp", "row"), None),
        P("row", None, None, None),
        P("row", None, None),
        P(),
    )
    return jax.shard_map(
        functools.partial(body, mesh.shape["grp"], mesh.shape["row"]),
        mesh=mesh,
        in_specs=placed,
        out_specs=P(("grp", "row"), None),
        check_vma=False,
    )
```

```python
import functools

import jax
import jax.numpy as jnp
from jax import lax
from jax.experimental import pallas as pl
from jax.experimental.pallas import tpu as pltpu
from jax.sharding import PartitionSpec as P

BF = jnp.bfloat16
F32 = jnp.float32
MISSING = -(1 << 20)


def dot(a, b):
    return lax.dot_general(a, b, (((1,), (0,)), ((), ())), preferred_element_type=F32)


def dot_t(a, b):
    return lax.dot_general(a, b, (((1,), (1,)), ((), ())), preferred_element_type=F32)


def iota(shape, dim):
    return lax.broadcasted_iota(jnp.int32, shape, dim)


def pick4(index, values):
    return jnp.where(
        index == 0, values[0], jnp.where(index == 1, values[1], jnp.where(index == 2, values[2], values[3]))
    )


def one_hot(shape, dim, bases):
    index = iota(shape, dim)
    position = pick4(index >> 5, bases) + (index & 31)
    return jnp.where(iota(shape, 1 - dim) == position, 1.0, 0.0).astype(BF)


def window_at(win, row):
    return [win[row, i] for i in range(4)]


def find(atoms, wanted):
    slot, there = jnp.int32(0), jnp.float32(0)
    for i in range(4):
        hit = atoms[i] == wanted
        slot = jnp.where(hit, jnp.int32(i), slot)
        there = jnp.where(hit, jnp.float32(1), there)
    return slot, there


def tile_mask(tiles, rows):
    shape = (4 * rows, 128)
    row, lane = iota(shape, 0) // rows, iota(shape, 1) >> 5
    mask = jnp.zeros(shape, F32)
    for i in range(4):
        for j in range(4):
            mask = jnp.where((row == i) & (lane == j), tiles[0, i, j].astype(F32), mask)
    return mask


def near(row, by, count):
    return lax.rem(row + by + count, count)


def column_chunk(row, count):
    return near(row, -1, count) >> 1


def first(count, occ, virt, tiles_hbm, coulomb, *refs):
    outs, (tiles, gs, part, sem, done) = refs[:5], refs[5:]
    d = lax.axis_index("row")
    funcs = part.shape[0]
    half = lax.rem(lax.axis_index("grp"), 2)
    list_copy = pltpu.make_async_copy(tiles_hbm, tiles, sem.at[16])
    list_copy.start()
    groups = []
    for n, by in enumerate((0, 1, -1, 2)):
        start = column_chunk(near(d, by, count), count)
        copies = []
        for c in range(2):
            chunk = lax.rem(start + c, count // 2)
            columns = pl.ds(pl.multiple_of(chunk * 128, 128), 128)
            for base, green in ((0, occ), (128, virt)):
                at = base + 64 * c
                place = gs.at[n, at : at + 64]
                copies.append(pltpu.make_async_copy(green.at[:, columns], place, sem.at[4 * n + len(copies)]))
        rows = outs[n].shape[0]
        groups.append((copies, pltpu.make_async_copy(gs.at[n, 0:rows], outs[n], done.at[n])))
    for n in range(3):
        piece = pl.ds(half * funcs + n * 8, 8)
        copy = pltpu.make_async_copy(coulomb.at[0, piece], part.at[n * 8 : n * 8 + 8], sem.at[17 + n])
        out = pltpu.make_async_copy(part.at[n * 8 : n * 8 + 8], outs[4].at[n * 8 : n * 8 + 8], done.at[4 + n])
        groups.append(([copy], out))
    for copies, _ in groups:
        for copy in copies:
            copy.start()
    list_copy.wait()
    short = tile_mask(tiles, 4).astype(BF)
    for n in range(1, 4):
        for at in (256, 272, 288):
            gs[n, at : at + 16, :] = short
    for copies, out in groups:
        for copy in copies:
            copy.wait()
        out.start()
    for _, out in groups:
        out.wait()


def far_tiles(count, win, tiles, tensor, far_right, far_left, mask):
    d = lax.axis_index("row")
    mine = window_at(win, d)
    funcs = tensor.shape[1] // 2
    start = lax.rem(lax.axis_index("grp"), 2) * funcs
    mask[...] = tile_mask(tiles, 32).astype(BF)
    for by, out in ((-1, far_left), (1, far_right)):
        base = near(d, by, count) * 2
        shape = (256, 128)
        row, lane = iota(shape, 0), iota(shape, 1)
        found = [find(mine, base), find(mine, base + 1)]
        here = pick4((row & 127) >> 5, mine) == base + ((lane & 63) >> 5)
        same = here & ((row & 31) == (lane & 31)) & ((row >> 7) == (lane >> 6))
        weight = jnp.where(row < 128, found[0][1], found[1][1])
        select = jnp.where(same, weight, 0.0).astype(BF)
        places = [pl.ds(pl.multiple_of(slot * 32, 32), 32) for slot, _ in found]
        masks = [mask[place, :] for place in places]
        for r in range(0, funcs, 8):
            sides = [
                jnp.concatenate([tensor[0, start + r + u, place, :] * m for u in range(8)], axis=0)
                for place, m in zip(places, masks)
            ]
            x = dot(jnp.concatenate(sides, axis=1), select)
            out[r * 32 : r * 32 + 256, :] = x.astype(BF)


def choose(count, win, g_self, g_before, g_after, g_far, out):
    d = lax.axis_index("row")
    atoms = 2 * count
    mine = window_at(win, d)
    theirs = window_at(win, near(d, -1, count))
    row0 = near(d, -2, count) * 2
    col0 = column_chunk(d, count) * 4

    def position(atom, start):
        return lax.rem(atom - start + atoms, atoms) * 32

    def whole(base):
        blocks = []
        for c in range(2):
            at = base + 64 * c
            blocks.append(
                jnp.concatenate(
                    [
                        g_far[at : at + 64, :],
                        g_before[at : at + 64, :],
                        g_self[at : at + 64, :],
                        g_after[at : at + 64, :],
                    ],
                    axis=0,
                )
            )
        return jnp.concatenate(blocks, axis=1)

    occ, virt = whole(0), whole(128)
    rows_mine = [position(a, row0) for a in mine]
    rows_theirs = [position(a, row0) for a in theirs]
    columns_mine = [position(a, col0) for a in mine]
    columns_both = []
    for i in range(4):
        _, there = find(theirs, mine[i])
        columns_both.append(jnp.where(there > 0, columns_mine[i], jnp.int32(MISSING)))
    for base, rows, columns in ((0, rows_mine, columns_mine), (256, rows_theirs, columns_both)):
        left = one_hot((128, 256), 0, columns)
        x = dot_t(left, occ).astype(BF)
        out[base : base + 128, :] = dot(x, one_hot((256, 128), 1, rows)).astype(BF)
        y = dot(one_hot((128, 256), 0, rows), virt).astype(BF)
        out[base + 128 : base + 256, :] = dot(y, one_hot((256, 128), 1, columns)).astype(BF)


def frame_map(atoms_from, wanted):
    bases = []
    for w in wanted:
        slot, there = find(atoms_from, w)
        bases.append(jnp.where(there > 0, slot * 32, jnp.int32(MISSING)))
    return one_hot((128, 128), 1, bases)


PITCH = 136


def halves(occ, blocks, outs, ms):
    rows = occ.shape[0] // len(outs)
    for i in range(0, len(blocks), 2):
        m0, m1 = blocks[i](), blocks[i + 1]()
        if ms is not None:
            ms[i * PITCH : i * PITCH + 128, :] = m0.astype(F32)
            ms[(i + 1) * PITCH : (i + 1) * PITCH + 128, :] = m1.astype(F32)
        h = dot(occ, jnp.concatenate([m0, m1], axis=1))
        for n, out in enumerate(outs):
            part = h[n * rows : (n + 1) * rows]
            out[i * PITCH : i * PITCH + 128, :] = part[:, :128]
            out[(i + 1) * PITCH : (i + 1) * PITCH + 128, :] = part[:, 128:]


def gather(ref, funcs, start):
    return [ref[pl.ds(start + t, funcs, stride=PITCH), :] for t in range(8)]


def dress(count, own, win, tiles, tensor, greens, *refs):
    if own:
        polar0, flat, dressed, far, hs, ms, same = refs
    else:
        (dressed, far, hs), ms = refs, None
    d = lax.axis_index("row")
    funcs = tensor.shape[1]
    mine = window_at(win, d)
    theirs = window_at(win, near(d, -1, count))
    left, right = near(d, -1, count) * 2, near(d, 1, count) * 2
    mask = tile_mask(tiles, 32).astype(BF)
    occ, virt = greens[0:128, :], greens[128:256, :]
    halves(occ, [functools.partial(lambda r: tensor[0, r] * mask, r) for r in range(funcs)], [hs], ms)
    wide, outs = dot(virt, frame_map(mine, theirs)).astype(BF), [dressed]
    if own:
        wide, outs = jnp.concatenate([virt, wide], axis=1), [same, dressed]
    lane = iota((128, 256), 1)
    atom = jnp.where(lane < 128, left, right)
    column_here = pick4(iota((128, 256), 0) >> 5, mine) == atom + ((lane & 63) >> 5)
    column_here = column_here & ((iota((128, 256), 0) & 31) == (lane & 31))
    both = dot(virt, jnp.where(column_here, 1.0, 0.0).astype(BF))
    row_atom = atom + ((lane & 127) >> 6)
    packs = jnp.concatenate([jnp.where(row_atom == a, both, 0.0).astype(BF) for a in mine], axis=0)
    for c in range(4):
        parts = []
        for i in range(4):
            parts.append(jnp.concatenate(gather(hs, funcs, i * 32 + c * 8), axis=0).astype(BF))
            x = dot(parts[-1], wide)
            for t in range(8):
                at = (i * 32 + c * 8 + t) * 128
                block = x[t * funcs : (t + 1) * funcs].astype(BF)
                for n, out in enumerate(outs):
                    out[:, at : at + 128] = block[:, n * 128 : (n + 1) * 128]
            if own:
                for t, rows in enumerate(gather(ms, funcs, i * 32 + c * 8)):
                    at = (i * 32 + c * 8 + t) * 128
                    flat[:, at : at + 128] = rows.astype(BF)
        x = dot(jnp.concatenate(parts, axis=1), packs)
        for t in range(8):
            at = (c * 8 + t) * 128
            block = x[t * funcs : (t + 1) * funcs].astype(BF)
            far[:, at : at + 128] = block[:, :128]
            far[:, 4096 + at : 4224 + at] = block[:, 128:]
    if own:
        polar0[...] = dot_t(same[...], flat[...])


def stacked(a, b, start, other):
    total = None
    for at in range(0, other.shape[1], 1024):
        left = jnp.concatenate([x[:, start + at : start + at + 1024] for x in (a, b)], axis=0)
        part = dot_t(left, other[:, at : at + 1024])
        total = part if total is None else total + part
    return total


def neighbour_mask(g_before):
    short = g_before[256:272, :].astype(F32)
    return jnp.concatenate(
        [jnp.broadcast_to(short[4 * i : 4 * i + 1, :], (32, 128)) for i in range(4)], axis=0
    ).astype(BF)


def join_back(tensor, g_before, g0, g1, flat, up, hs0, hs1, backs):
    funcs = tensor.shape[0]
    full = 2 * funcs
    mask = neighbour_mask(g_before)
    occ = jnp.concatenate([g0[256:384, :], g1[256:384, :]], axis=0)
    halves(occ, [functools.partial(lambda r: tensor[r] * mask, r) for r in range(funcs)], [hs0, hs1], None)
    virts = [g0[384:512, :], g1[384:512, :]]
    for i in range(16):
        xs = []
        for hs, virt in zip((hs0, hs1), virts):
            xs.append(dot(jnp.concatenate(gather(hs, funcs, i * 8), axis=0).astype(BF), virt))
        for t in range(8):
            at = (i * 8 + t) * 128
            part = slice(t * funcs, (t + 1) * funcs)
            backs[:, at : at + 128] = jnp.concatenate([x[part] for x in xs], axis=0).astype(BF)
    total = dot_t(backs[...], flat[...])
    up[...] = jnp.concatenate([total, jnp.zeros((full, 128 - full), F32)], axis=1)


def join(count, win, tensor, g_before, dressed0, dressed1, down, ms, moved):
    d = lax.axis_index("row")
    funcs = tensor.shape[0]
    full = 2 * funcs
    mine = window_at(win, d)
    theirs = window_at(win, near(d, -1, count))
    mask = neighbour_mask(g_before)
    for r in range(funcs):
        ms[r * PITCH : r * PITCH + 128, :] = (tensor[r] * mask).astype(F32)
    for i in range(16):
        slot, there = find(theirs, mine[i // 4])
        rows = gather(ms, funcs, slot * 32 + (i % 4) * 8)
        for t in range(8):
            at = (i * 8 + t) * 128
            moved[:, at : at + 128] = (rows[t] * there).astype(BF)
    total = stacked(dressed0, dressed1, 0, moved)
    down[...] = jnp.concatenate([total, jnp.zeros((2 * full, 128 - funcs), F32)], axis=1)


FAR_PITCH = 40


def join_far(far0, far1, from_left, from_right, down, after, own, other, es, turned):
    full = far0.shape[0]
    funcs = full // 2
    for e in (from_left, from_right):
        side = 0 if e is from_left else 1
        for r in range(funcs):
            at = r * FAR_PITCH
            es[side, at : at + 32, :] = e[r * 32 : (r + 1) * 32, :].astype(F32)
        for t in range(32):
            rows = es[side, pl.ds(t, funcs, stride=FAR_PITCH), :]
            turned[side, :, t * 128 : (t + 1) * 128] = rows.astype(BF)
    far_left = stacked(far0, far1, 0, turned.at[0])
    far_right = stacked(far0, far1, 4096, turned.at[1])
    padding = jnp.zeros((full, 128 - 3 * funcs - full), F32)
    for n, out in enumerate((own, other)):
        part = slice(n * full, (n + 1) * full)
        back = after[n * funcs : (n + 1) * funcs, :full]
        back = jnp.concatenate([back, jnp.zeros((funcs, full), F32)], axis=0)
        out[...] = jnp.concatenate(
            [far_left[part], down[part, :funcs], far_right[part], back, padding], axis=1
        )


def assemble(polar0, own, recv, out):
    is_first = lax.rem(lax.axis_index("grp"), 2) == 0
    full = polar0.shape[0]
    funcs = full // 2
    a, b = own[...], recv[...]
    low, high = jnp.where(is_first, a, b), jnp.where(is_first, b, a)
    back = slice(3 * funcs, 3 * funcs + full)
    after = jnp.concatenate([low[:funcs, back], high[:funcs, back]], axis=0)
    pieces = []
    for i in range(3):
        part = slice(i * funcs, (i + 1) * funcs)
        if i == 2:
            pieces += [polar0[...], after]
        pieces += [low[:, part], high[:, part]]
    out[...] = jnp.concatenate(pieces, axis=1)


def vmem(count):
    return [pl.BlockSpec(memory_space=pltpu.VMEM)] * count


def hbm(count):
    return [pl.BlockSpec(memory_space=pltpu.HBM)] * count


def smem(count):
    return [pl.BlockSpec(memory_space=pltpu.SMEM)] * count


def call(kernel, name, specs, outs, args, scratch=(), flops=0, limit=40 << 20, space=None):
    return pl.pallas_call(
        kernel,
        name=name,
        in_specs=specs,
        out_specs=tuple((space or vmem)(len(outs))),
        out_shape=tuple(outs),
        scratch_shapes=list(scratch),
        compiler_params=pltpu.CompilerParams(vmem_limit_bytes=limit),
        cost_estimate=pl.CostEstimate(flops=flops, bytes_accessed=0, transcendentals=0),
    )(*args)


def body(groups, count, green_occ, green_virt, coulomb3c, tile_list, window):
    full = coulomb3c.shape[1]
    funcs = full // 2
    shape = jax.ShapeDtypeStruct

    def send(array, row_by, swap=False):
        pairs = []
        for g in range(groups):
            for d in range(count):
                to = (g ^ 1 if swap else g) * count + (d + row_by) % count
                pairs.append((g * count + d, to))
        return lax.ppermute(array, ("grp", "row"), pairs)

    far_rows = funcs * 32
    g_self, g_right, g_left, g_far, tensor = call(
        functools.partial(first, count),
        "first",
        hbm(4),
        [
            shape((256, 128), BF),
            shape((272, 128), BF),
            shape((304, 128), BF),
            shape((288, 128), BF),
            shape((funcs, 128, 128), BF),
        ],
        (green_occ, green_virt, tile_list, coulomb3c),
        [
            pltpu.SMEM((1, 4, 4), jnp.int32),
            pltpu.VMEM((4, 304, 128), BF),
            pltpu.VMEM((funcs, 128, 128), BF),
            pltpu.SemaphoreType.DMA((20,)),
            pltpu.SemaphoreType.DMA((7,)),
        ],
        limit=60 << 20,
        space=hbm,
    )
    g_before = send(g_right, 1)
    g_after = send(g_left, -1)
    g_beyond = send(g_far, 2)
    wide = send(tensor, 1)
    far_right, far_left = call(
        functools.partial(far_tiles, count),
        "far_tiles",
        smem(2) + vmem(1),
        [shape((far_rows, 128), BF), shape((far_rows, 128), BF)],
        (window, tile_list, coulomb3c),
        [pltpu.VMEM((128, 128), BF)],
        flops=1 << 36,
    )
    from_left = send(far_right, 2)
    from_right = send(far_left, -2)
    g_before, g_after, g_beyond, far_right, far_left = lax.optimization_barrier(
        (g_before, g_after, g_beyond, far_right, far_left)
    )
    (mine,) = call(
        functools.partial(choose, count),
        "choose",
        smem(1) + vmem(4),
        [shape((512, 128), BF)],
        (window, g_self, g_before, g_after, g_beyond),
    )
    partner = send(mine, 0, True)
    flat_shape, far_shape = shape((full, 128 * 128), BF), shape((full, 64 * 128), BF)
    tall = pltpu.VMEM((full * PITCH, 128), F32)
    short = pltpu.VMEM((funcs * PITCH, 128), F32)
    message = shape((full, 128), F32)
    polar0, flat, dressed0, far0 = call(
        functools.partial(dress, count, True),
        "dress_own",
        smem(2) + vmem(2),
        [shape((full, full), F32), flat_shape, flat_shape, far_shape],
        (window, tile_list, coulomb3c, mine),
        [tall, tall, pltpu.VMEM((full, 128 * 128), BF)],
    )
    dressed1, far1 = call(
        functools.partial(dress, count, False),
        "dress_partner",
        smem(2) + vmem(2),
        [flat_shape, far_shape],
        (window, tile_list, coulomb3c, partner),
        [tall],
    )
    g_before, dressed1 = lax.optimization_barrier((g_before, dressed1))
    (up,) = call(
        join_back,
        "join_back",
        vmem(5),
        [message],
        (wide, g_before, mine, partner, flat),
        [short, short, pltpu.VMEM((full, 128 * 128), BF)],
    )
    after = send(up, -1)
    (down,) = call(
        functools.partial(join, count),
        "join",
        smem(1) + vmem(4),
        [shape((2 * full, 128), F32)],
        (window, wide, g_before, dressed0, dressed1),
        [short, pltpu.VMEM((funcs, 128 * 128), BF)],
    )
    own, other = call(
        join_far,
        "join_far",
        vmem(6),
        [message, message],
        (far0, far1, from_left, from_right, down, after),
        [pltpu.VMEM((2, funcs * FAR_PITCH, 128), F32), pltpu.VMEM((2, funcs, 32 * 128), BF)],
    )
    recv = send(other, 0, True)
    (out,) = call(
        assemble,
        "assemble",
        vmem(3),
        [shape((full, 5 * full), F32)],
        (polar0, own, recv),
    )
    return out


def solution(mesh):
    placed = (
        P(("grp", "row"), None),
        P(("grp", "row"), None),
        P("row", None, None, None),
        P("row", None, None),
        P(),
    )
    return jax.shard_map(
        functools.partial(body, mesh.shape["grp"], mesh.shape["row"]),
        mesh=mesh,
        in_specs=placed,
        out_specs=P(("grp", "row"), None),
        check_vma=False,
    )
```

```python
import functools

import jax
import jax.numpy as jnp
from jax import lax
from jax.experimental import pallas as pl
from jax.experimental.pallas import tpu as pltpu
from jax.sharding import PartitionSpec as P

BF = jnp.bfloat16
F32 = jnp.float32
MISSING = -(1 << 20)


def dot(a, b):
    return lax.dot_general(a, b, (((1,), (0,)), ((), ())), preferred_element_type=F32)


def dot_t(a, b):
    return lax.dot_general(a, b, (((1,), (1,)), ((), ())), preferred_element_type=F32)


def iota(shape, dim):
    return lax.broadcasted_iota(jnp.int32, shape, dim)


def pick4(index, values):
    return jnp.where(
        index == 0, values[0], jnp.where(index == 1, values[1], jnp.where(index == 2, values[2], values[3]))
    )


def one_hot(shape, dim, bases):
    index = iota(shape, dim)
    position = pick4(index >> 5, bases) + (index & 31)
    return jnp.where(iota(shape, 1 - dim) == position, 1.0, 0.0).astype(BF)


def window_at(win, row):
    return [win[row, i] for i in range(4)]


def find(atoms, wanted):
    slot, there = jnp.int32(0), jnp.float32(0)
    for i in range(4):
        hit = atoms[i] == wanted
        slot = jnp.where(hit, jnp.int32(i), slot)
        there = jnp.where(hit, jnp.float32(1), there)
    return slot, there


def tile_mask(tiles, rows):
    shape = (4 * rows, 128)
    row, lane = iota(shape, 0) // rows, iota(shape, 1) >> 5
    mask = jnp.zeros(shape, F32)
    for i in range(4):
        for j in range(4):
            mask = jnp.where((row == i) & (lane == j), tiles[0, i, j].astype(F32), mask)
    return mask


def near(row, by, count):
    return lax.rem(row + by + count, count)


def column_chunk(row, count):
    return near(row, -1, count) >> 1


def first(count, occ, virt, tiles_hbm, coulomb, *refs):
    outs, (tiles, gs, fs, part, sem, done) = refs[:5], refs[5:]
    d = lax.axis_index("row")
    funcs = part.shape[0]
    half = lax.rem(lax.axis_index("grp"), 2)
    list_copy = pltpu.make_async_copy(tiles_hbm, tiles, sem.at[16])
    list_copy.start()
    groups = []
    for n, by in enumerate((0, 1, -1, 2)):
        start = column_chunk(near(d, by, count), count)
        copies = []
        for c in range(2):
            chunk = lax.rem(start + c, count // 2)
            columns = pl.ds(pl.multiple_of(chunk * 128, 128), 128)
            for base, green in ((0, occ), (128, virt)):
                at = base + 64 * c
                place = gs.at[n, at : at + 64]
                copies.append(pltpu.make_async_copy(green.at[:, columns], place, sem.at[4 * n + len(copies)]))
        rows = outs[n].shape[0]
        source = fs if n == 3 else gs.at[n, 0:rows]
        groups.append((copies, pltpu.make_async_copy(source, outs[n], done.at[n])))
    for n in range(3):
        piece = pl.ds(half * funcs + n * 8, 8)
        copy = pltpu.make_async_copy(coulomb.at[0, piece], part.at[n * 8 : n * 8 + 8], sem.at[17 + n])
        out = pltpu.make_async_copy(part.at[n * 8 : n * 8 + 8], outs[4].at[n * 8 : n * 8 + 8], done.at[4 + n])
        groups.append(([copy], out))
    for copies, _ in groups:
        for copy in copies:
            copy.start()
    list_copy.wait()
    short = tile_mask(tiles, 4).astype(BF)
    for n in range(1, 3):
        for at in (256, 272):
            gs[n, at : at + 16, :] = short
    for n, (copies, out) in enumerate(groups):
        for copy in copies:
            copy.wait()
        if n == 3:
            lane = iota((64, 128), 1)
            for base, at in ((0, 0), (128, 64)):
                low = gs[3, base : base + 64, :].astype(F32)
                high = gs[3, base + 64 : base + 128, :].astype(F32)
                turned = jnp.where(lane < 64, pltpu.roll(low, 64, 1), pltpu.roll(high, 64, 1))
                fs[at : at + 64, :] = jnp.where(lax.rem(d, 2) == 1, low, turned).astype(BF)
        out.start()
    for _, out in groups:
        out.wait()


def far_tiles(count, win, tiles, tensor, far_right, far_left, mask):
    d = lax.axis_index("row")
    mine = window_at(win, d)
    funcs = tensor.shape[1] // 2
    start = lax.rem(lax.axis_index("grp"), 2) * funcs
    mask[...] = tile_mask(tiles, 32).astype(BF)
    for by, out in ((-1, far_left), (1, far_right)):
        base = near(d, by, count) * 2
        shape = (256, 128)
        row, lane = iota(shape, 0), iota(shape, 1)
        found = [find(mine, base), find(mine, base + 1)]
        here = pick4((row & 127) >> 5, mine) == base + ((lane & 63) >> 5)
        same = here & ((row & 31) == (lane & 31)) & ((row >> 7) == (lane >> 6))
        weight = jnp.where(row < 128, found[0][1], found[1][1])
        select = jnp.where(same, weight, 0.0).astype(BF)
        places = [pl.ds(pl.multiple_of(slot * 32, 32), 32) for slot, _ in found]
        masks = [mask[place, :] for place in places]
        for r in range(0, funcs, 8):
            sides = [
                jnp.concatenate([tensor[0, start + r + u, place, :] * m for u in range(8)], axis=0)
                for place, m in zip(places, masks)
            ]
            x = dot(jnp.concatenate(sides, axis=1), select)
            out[r * 32 : r * 32 + 256, :] = x.astype(BF)


def choose(count, win, g_self, g_before, g_after, g_far, out):
    d = lax.axis_index("row")
    atoms = 2 * count
    mine = window_at(win, d)
    theirs = window_at(win, near(d, -1, count))
    row0 = near(d, -2, count) * 2
    col0 = column_chunk(d, count) * 4

    def position(atom, start):
        return lax.rem(atom - start + atoms, atoms) * 32

    odd = lax.rem(d, 2) == 1
    lane = iota((64, 128), 1)

    def whole(base):
        far = g_far[base // 2 : base // 2 + 64, :].astype(F32)
        turned = pltpu.roll(far, 64, 1)
        fars = (
            jnp.where(odd, far, jnp.where(lane < 64, 0.0, turned)).astype(BF),
            jnp.where(odd, 0.0, jnp.where(lane < 64, turned, 0.0)).astype(BF),
        )
        blocks = []
        for c in range(2):
            at = base + 64 * c
            parts = [fars[c]] + [g[at : at + 64, :] for g in (g_before, g_self, g_after)]
            blocks.append(jnp.concatenate(parts, axis=0))
        return jnp.concatenate(blocks, axis=1)

    occ, virt = whole(0), whole(128)
    rows_mine = [position(a, row0) for a in mine]
    rows_theirs = [position(a, row0) for a in theirs]
    columns_mine = [position(a, col0) for a in mine]
    columns_both = []
    for i in range(4):
        _, there = find(theirs, mine[i])
        columns_both.append(jnp.where(there > 0, columns_mine[i], jnp.int32(MISSING)))
    for base, rows, columns in ((0, rows_mine, columns_mine), (256, rows_theirs, columns_both)):
        left = one_hot((128, 256), 0, columns)
        x = dot_t(left, occ).astype(BF)
        out[base : base + 128, :] = dot(x, one_hot((256, 128), 1, rows)).astype(BF)
        y = dot(one_hot((128, 256), 0, rows), virt).astype(BF)
        out[base + 128 : base + 256, :] = dot(y, one_hot((256, 128), 1, columns)).astype(BF)


def frame_map(atoms_from, wanted):
    bases = []
    for w in wanted:
        slot, there = find(atoms_from, w)
        bases.append(jnp.where(there > 0, slot * 32, jnp.int32(MISSING)))
    return one_hot((128, 128), 1, bases)


PITCH = 136


def halves(occ, blocks, outs, ms):
    rows = occ.shape[0] // len(outs)
    for i in range(0, len(blocks), 2):
        m0, m1 = blocks[i](), blocks[i + 1]()
        if ms is not None:
            ms[i * PITCH : i * PITCH + 128, :] = m0.astype(F32)
            ms[(i + 1) * PITCH : (i + 1) * PITCH + 128, :] = m1.astype(F32)
        h = dot(occ, jnp.concatenate([m0, m1], axis=1))
        for n, out in enumerate(outs):
            part = h[n * rows : (n + 1) * rows]
            out[i * PITCH : i * PITCH + 128, :] = part[:, :128]
            out[(i + 1) * PITCH : (i + 1) * PITCH + 128, :] = part[:, 128:]


def gather(ref, funcs, start):
    return [ref[pl.ds(start + t, funcs, stride=PITCH), :] for t in range(8)]


def dress(count, own, win, tiles, tensor, greens, *refs):
    if own:
        polar0, flat, dressed, far, hs, ms, same = refs
    else:
        (dressed, far, hs), ms = refs, None
    d = lax.axis_index("row")
    funcs = tensor.shape[1]
    mine = window_at(win, d)
    theirs = window_at(win, near(d, -1, count))
    left, right = near(d, -1, count) * 2, near(d, 1, count) * 2
    mask = tile_mask(tiles, 32).astype(BF)
    occ, virt = greens[0:128, :], greens[128:256, :]
    halves(occ, [functools.partial(lambda r: tensor[0, r] * mask, r) for r in range(funcs)], [hs], ms)
    wide, outs = dot(virt, frame_map(mine, theirs)).astype(BF), [dressed]
    if own:
        wide, outs = jnp.concatenate([virt, wide], axis=1), [same, dressed]
    lane = iota((128, 256), 1)
    atom = jnp.where(lane < 128, left, right)
    column_here = pick4(iota((128, 256), 0) >> 5, mine) == atom + ((lane & 63) >> 5)
    column_here = column_here & ((iota((128, 256), 0) & 31) == (lane & 31))
    both = dot(virt, jnp.where(column_here, 1.0, 0.0).astype(BF))
    row_atom = atom + ((lane & 127) >> 6)
    packs = jnp.concatenate([jnp.where(row_atom == a, both, 0.0).astype(BF) for a in mine], axis=0)
    for c in range(4):
        parts = []
        for i in range(4):
            parts.append(jnp.concatenate(gather(hs, funcs, i * 32 + c * 8), axis=0).astype(BF))
            x = dot(parts[-1], wide)
            for t in range(8):
                at = (i * 32 + c * 8 + t) * 128
                block = x[t * funcs : (t + 1) * funcs].astype(BF)
                for n, out in enumerate(outs):
                    out[:, at : at + 128] = block[:, n * 128 : (n + 1) * 128]
            if own:
                for t, rows in enumerate(gather(ms, funcs, i * 32 + c * 8)):
                    at = (i * 32 + c * 8 + t) * 128
                    flat[:, at : at + 128] = rows.astype(BF)
        x = dot(jnp.concatenate(parts, axis=1), packs)
        for t in range(8):
            at = (c * 8 + t) * 128
            block = x[t * funcs : (t + 1) * funcs].astype(BF)
            far[:, at : at + 128] = block[:, :128]
            far[:, 4096 + at : 4224 + at] = block[:, 128:]
    if own:
        polar0[...] = dot_t(same[...], flat[...])


def stacked(a, b, start, other):
    total = None
    for at in range(0, other.shape[1], 1024):
        left = jnp.concatenate([x[:, start + at : start + at + 1024] for x in (a, b)], axis=0)
        part = dot_t(left, other[:, at : at + 1024])
        total = part if total is None else total + part
    return total


def neighbour_mask(g_before):
    short = g_before[256:272, :].astype(F32)
    return jnp.concatenate(
        [jnp.broadcast_to(short[4 * i : 4 * i + 1, :], (32, 128)) for i in range(4)], axis=0
    ).astype(BF)


def join_back(tensor, g_before, g0, g1, flat, up, hs0, hs1, backs):
    funcs = tensor.shape[0]
    full = 2 * funcs
    mask = neighbour_mask(g_before)
    occ = jnp.concatenate([g0[256:384, :], g1[256:384, :]], axis=0)
    halves(occ, [functools.partial(lambda r: tensor[r] * mask, r) for r in range(funcs)], [hs0, hs1], None)
    virts = [g0[384:512, :], g1[384:512, :]]
    for i in range(16):
        xs = []
        for hs, virt in zip((hs0, hs1), virts):
            xs.append(dot(jnp.concatenate(gather(hs, funcs, i * 8), axis=0).astype(BF), virt))
        for t in range(8):
            at = (i * 8 + t) * 128
            part = slice(t * funcs, (t + 1) * funcs)
            backs[:, at : at + 128] = jnp.concatenate([x[part] for x in xs], axis=0).astype(BF)
    total = dot_t(backs[...], flat[...])
    up[...] = jnp.concatenate([total, jnp.zeros((full, 128 - full), F32)], axis=1)


def join(count, win, tensor, g_before, dressed0, dressed1, down, ms, moved):
    d = lax.axis_index("row")
    funcs = tensor.shape[0]
    full = 2 * funcs
    mine = window_at(win, d)
    theirs = window_at(win, near(d, -1, count))
    mask = neighbour_mask(g_before)
    for r in range(funcs):
        ms[r * PITCH : r * PITCH + 128, :] = (tensor[r] * mask).astype(F32)
    for i in range(16):
        slot, there = find(theirs, mine[i // 4])
        rows = gather(ms, funcs, slot * 32 + (i % 4) * 8)
        for t in range(8):
            at = (i * 8 + t) * 128
            moved[:, at : at + 128] = (rows[t] * there).astype(BF)
    total = stacked(dressed0, dressed1, 0, moved)
    down[...] = jnp.concatenate([total, jnp.zeros((2 * full, 128 - funcs), F32)], axis=1)


FAR_PITCH = 40


def join_far(far0, far1, from_left, from_right, down, after, own, other, es, turned):
    full = far0.shape[0]
    funcs = full // 2
    for e in (from_left, from_right):
        side = 0 if e is from_left else 1
        for r in range(funcs):
            at = r * FAR_PITCH
            es[side, at : at + 32, :] = e[r * 32 : (r + 1) * 32, :].astype(F32)
        for t in range(32):
            rows = es[side, pl.ds(t, funcs, stride=FAR_PITCH), :]
            turned[side, :, t * 128 : (t + 1) * 128] = rows.astype(BF)
    far_left = stacked(far0, far1, 0, turned.at[0])
    far_right = stacked(far0, far1, 4096, turned.at[1])
    padding = jnp.zeros((full, 128 - 3 * funcs - full), F32)
    for n, out in enumerate((own, other)):
        part = slice(n * full, (n + 1) * full)
        back = after[n * funcs : (n + 1) * funcs, :full]
        back = jnp.concatenate([back, jnp.zeros((funcs, full), F32)], axis=0)
        out[...] = jnp.concatenate(
            [far_left[part], down[part, :funcs], far_right[part], back, padding], axis=1
        )


def assemble(polar0, own, recv, out):
    is_first = lax.rem(lax.axis_index("grp"), 2) == 0
    full = polar0.shape[0]
    funcs = full // 2
    a, b = own[...], recv[...]
    low, high = jnp.where(is_first, a, b), jnp.where(is_first, b, a)
    back = slice(3 * funcs, 3 * funcs + full)
    after = jnp.concatenate([low[:funcs, back], high[:funcs, back]], axis=0)
    pieces = []
    for i in range(3):
        part = slice(i * funcs, (i + 1) * funcs)
        if i == 2:
            pieces += [polar0[...], after]
        pieces += [low[:, part], high[:, part]]
    out[...] = jnp.concatenate(pieces, axis=1)


def vmem(count):
    return [pl.BlockSpec(memory_space=pltpu.VMEM)] * count


def hbm(count):
    return [pl.BlockSpec(memory_space=pltpu.HBM)] * count


def smem(count):
    return [pl.BlockSpec(memory_space=pltpu.SMEM)] * count


def call(kernel, name, specs, outs, args, scratch=(), flops=0, limit=40 << 20, space=None):
    return pl.pallas_call(
        kernel,
        name=name,
        in_specs=specs,
        out_specs=tuple((space or vmem)(len(outs))),
        out_shape=tuple(outs),
        scratch_shapes=list(scratch),
        compiler_params=pltpu.CompilerParams(vmem_limit_bytes=limit),
        cost_estimate=pl.CostEstimate(flops=flops, bytes_accessed=0, transcendentals=0),
    )(*args)


def body(groups, count, green_occ, green_virt, coulomb3c, tile_list, window):
    full = coulomb3c.shape[1]
    funcs = full // 2
    shape = jax.ShapeDtypeStruct

    def send(array, row_by, swap=False):
        pairs = []
        for g in range(groups):
            for d in range(count):
                to = (g ^ 1 if swap else g) * count + (d + row_by) % count
                pairs.append((g * count + d, to))
        return lax.ppermute(array, ("grp", "row"), pairs)

    far_rows = funcs * 32
    g_self, g_right, g_left, g_far, tensor = call(
        functools.partial(first, count),
        "first",
        hbm(4),
        [
            shape((256, 128), BF),
            shape((272, 128), BF),
            shape((288, 128), BF),
            shape((128, 128), BF),
            shape((funcs, 128, 128), BF),
        ],
        (green_occ, green_virt, tile_list, coulomb3c),
        [
            pltpu.SMEM((1, 4, 4), jnp.int32),
            pltpu.VMEM((4, 288, 128), BF),
            pltpu.VMEM((128, 128), BF),
            pltpu.VMEM((funcs, 128, 128), BF),
            pltpu.SemaphoreType.DMA((20,)),
            pltpu.SemaphoreType.DMA((7,)),
        ],
        limit=60 << 20,
        space=hbm,
    )
    g_before = send(g_right, 1)
    g_after = send(g_left, -1)
    g_beyond = send(g_far, 2)
    wide = send(tensor, 1)
    far_right, far_left = call(
        functools.partial(far_tiles, count),
        "far_tiles",
        smem(2) + vmem(1),
        [shape((far_rows, 128), BF), shape((far_rows, 128), BF)],
        (window, tile_list, coulomb3c),
        [pltpu.VMEM((128, 128), BF)],
        flops=1 << 36,
    )
    from_left = send(far_right, 2)
    from_right = send(far_left, -2)
    g_before, g_after, g_beyond, far_right, far_left = lax.optimization_barrier(
        (g_before, g_after, g_beyond, far_right, far_left)
    )
    (mine,) = call(
        functools.partial(choose, count),
        "choose",
        smem(1) + vmem(4),
        [shape((512, 128), BF)],
        (window, g_self, g_before, g_after, g_beyond),
    )
    partner = send(mine, 0, True)
    flat_shape, far_shape = shape((full, 128 * 128), BF), shape((full, 64 * 128), BF)
    tall = pltpu.VMEM((full * PITCH, 128), F32)
    short = pltpu.VMEM((funcs * PITCH, 128), F32)
    message = shape((full, 128), F32)
    polar0, flat, dressed0, far0 = call(
        functools.partial(dress, count, True),
        "dress_own",
        smem(2) + vmem(2),
        [shape((full, full), F32), flat_shape, flat_shape, far_shape],
        (window, tile_list, coulomb3c, mine),
        [tall, tall, pltpu.VMEM((full, 128 * 128), BF)],
    )
    dressed1, far1 = call(
        functools.partial(dress, count, False),
        "dress_partner",
        smem(2) + vmem(2),
        [flat_shape, far_shape],
        (window, tile_list, coulomb3c, partner),
        [tall],
    )
    g_before, dressed1 = lax.optimization_barrier((g_before, dressed1))
    (up,) = call(
        join_back,
        "join_back",
        vmem(5),
        [message],
        (wide, g_before, mine, partner, flat),
        [short, short, pltpu.VMEM((full, 128 * 128), BF)],
    )
    after = send(up, -1)
    (down,) = call(
        functools.partial(join, count),
        "join",
        smem(1) + vmem(4),
        [shape((2 * full, 128), F32)],
        (window, wide, g_before, dressed0, dressed1),
        [short, pltpu.VMEM((funcs, 128 * 128), BF)],
    )
    own, other = call(
        join_far,
        "join_far",
        vmem(6),
        [message, message],
        (far0, far1, from_left, from_right, down, after),
        [pltpu.VMEM((2, funcs * FAR_PITCH, 128), F32), pltpu.VMEM((2, funcs, 32 * 128), BF)],
    )
    recv = send(other, 0, True)
    (out,) = call(
        assemble,
        "assemble",
        vmem(3),
        [shape((full, 5 * full), F32)],
        (polar0, own, recv),
    )
    return out


def solution(mesh):
    placed = (
        P(("grp", "row"), None),
        P(("grp", "row"), None),
        P("row", None, None, None),
        P("row", None, None),
        P(),
    )
    return jax.shard_map(
        functools.partial(body, mesh.shape["grp"], mesh.shape["row"]),
        mesh=mesh,
        in_specs=placed,
        out_specs=P(("grp", "row"), None),
        check_vma=False,
    )
```

```python
import functools

import jax
import jax.numpy as jnp
from jax import lax
from jax.experimental import pallas as pl
from jax.experimental.pallas import tpu as pltpu
from jax.sharding import PartitionSpec as P

BF = jnp.bfloat16
F32 = jnp.float32
MISSING = -(1 << 20)


def dot(a, b):
    return lax.dot_general(a, b, (((1,), (0,)), ((), ())), preferred_element_type=F32)


def dot_t(a, b):
    return lax.dot_general(a, b, (((1,), (1,)), ((), ())), preferred_element_type=F32)


def iota(shape, dim):
    return lax.broadcasted_iota(jnp.int32, shape, dim)


def pick4(index, values):
    return jnp.where(
        index == 0, values[0], jnp.where(index == 1, values[1], jnp.where(index == 2, values[2], values[3]))
    )


def one_hot(shape, dim, bases):
    index = iota(shape, dim)
    position = pick4(index >> 5, bases) + (index & 31)
    return jnp.where(iota(shape, 1 - dim) == position, 1.0, 0.0).astype(BF)


def window_at(win, row):
    return [win[row, i] for i in range(4)]


def find(atoms, wanted):
    slot, there = jnp.int32(0), jnp.float32(0)
    for i in range(4):
        hit = atoms[i] == wanted
        slot = jnp.where(hit, jnp.int32(i), slot)
        there = jnp.where(hit, jnp.float32(1), there)
    return slot, there


def tile_mask(tiles, rows):
    shape = (4 * rows, 128)
    row, lane = iota(shape, 0) // rows, iota(shape, 1) >> 5
    mask = jnp.zeros(shape, F32)
    for i in range(4):
        for j in range(4):
            mask = jnp.where((row == i) & (lane == j), tiles[0, i, j].astype(F32), mask)
    return mask


def near(row, by, count):
    return lax.rem(row + by + count, count)


def column_chunk(row, count):
    return near(row, -1, count) >> 1


def first(count, occ, virt, tiles_hbm, coulomb, *refs):
    outs, (tiles, gs, part, sem, done) = refs[:5], refs[5:]
    d = lax.axis_index("row")
    funcs = part.shape[0]
    half = lax.rem(lax.axis_index("grp"), 2)
    list_copy = pltpu.make_async_copy(tiles_hbm, tiles, sem.at[16])
    list_copy.start()
    groups = []
    for n, by in enumerate((0, 1, -1, 2)):
        start = column_chunk(near(d, by, count), count)
        copies = []
        for c in range(2):
            chunk = lax.rem(start + c, count // 2)
            columns = pl.ds(pl.multiple_of(chunk * 128, 128), 128)
            for base, green in ((0, occ), (128, virt)):
                at = base + 64 * c
                place = gs.at[n, at : at + 64]
                copies.append(pltpu.make_async_copy(green.at[:, columns], place, sem.at[4 * n + len(copies)]))
        rows = outs[n].shape[0]
        groups.append((copies, pltpu.make_async_copy(gs.at[n, 0:rows], outs[n], done.at[n])))
    for n in range(3):
        piece = pl.ds(half * funcs + n * 8, 8)
        copy = pltpu.make_async_copy(coulomb.at[0, piece], part.at[n * 8 : n * 8 + 8], sem.at[17 + n])
        out = pltpu.make_async_copy(part.at[n * 8 : n * 8 + 8], outs[4].at[n * 8 : n * 8 + 8], done.at[4 + n])
        groups.append(([copy], out))
    groups = groups[4:] + groups[:4]
    for copies, _ in groups:
        for copy in copies:
            copy.start()
    list_copy.wait()
    short = tile_mask(tiles, 4).astype(BF)
    for n in range(1, 4):
        for at in (256, 272, 288):
            gs[n, at : at + 16, :] = short
    for copies, out in groups:
        for copy in copies:
            copy.wait()
        out.start()
    for _, out in groups:
        out.wait()


def far_tiles(count, win, tiles, tensor, far_right, far_left, mask):
    d = lax.axis_index("row")
    mine = window_at(win, d)
    funcs = tensor.shape[1] // 2
    start = lax.rem(lax.axis_index("grp"), 2) * funcs
    mask[...] = tile_mask(tiles, 32).astype(BF)
    for by, out in ((-1, far_left), (1, far_right)):
        base = near(d, by, count) * 2
        shape = (256, 128)
        row, lane = iota(shape, 0), iota(shape, 1)
        found = [find(mine, base), find(mine, base + 1)]
        here = pick4((row & 127) >> 5, mine) == base + ((lane & 63) >> 5)
        same = here & ((row & 31) == (lane & 31)) & ((row >> 7) == (lane >> 6))
        weight = jnp.where(row < 128, found[0][1], found[1][1])
        select = jnp.where(same, weight, 0.0).astype(BF)
        places = [pl.ds(pl.multiple_of(slot * 32, 32), 32) for slot, _ in found]
        masks = [mask[place, :] for place in places]
        for r in range(0, funcs, 8):
            sides = [
                jnp.concatenate([tensor[0, start + r + u, place, :] * m for u in range(8)], axis=0)
                for place, m in zip(places, masks)
            ]
            x = dot(jnp.concatenate(sides, axis=1), select)
            out[r * 32 : r * 32 + 256, :] = x.astype(BF)


def choose(count, win, g_self, g_before, g_after, g_far, out):
    d = lax.axis_index("row")
    atoms = 2 * count
    mine = window_at(win, d)
    theirs = window_at(win, near(d, -1, count))
    row0 = near(d, -2, count) * 2
    col0 = column_chunk(d, count) * 4

    def position(atom, start):
        return lax.rem(atom - start + atoms, atoms) * 32

    def whole(base):
        blocks = []
        for c in range(2):
            at = base + 64 * c
            blocks.append(
                jnp.concatenate(
                    [
                        g_far[at : at + 64, :],
                        g_before[at : at + 64, :],
                        g_self[at : at + 64, :],
                        g_after[at : at + 64, :],
                    ],
                    axis=0,
                )
            )
        return jnp.concatenate(blocks, axis=1)

    occ, virt = whole(0), whole(128)
    rows_mine = [position(a, row0) for a in mine]
    rows_theirs = [position(a, row0) for a in theirs]
    columns_mine = [position(a, col0) for a in mine]
    columns_both = []
    for i in range(4):
        _, there = find(theirs, mine[i])
        columns_both.append(jnp.where(there > 0, columns_mine[i], jnp.int32(MISSING)))
    for base, rows, columns in ((0, rows_mine, columns_mine), (256, rows_theirs, columns_both)):
        left = one_hot((128, 256), 0, columns)
        x = dot_t(left, occ).astype(BF)
        out[base : base + 128, :] = dot(x, one_hot((256, 128), 1, rows)).astype(BF)
        y = dot(one_hot((128, 256), 0, rows), virt).astype(BF)
        out[base + 128 : base + 256, :] = dot(y, one_hot((256, 128), 1, columns)).astype(BF)


def frame_map(atoms_from, wanted):
    bases = []
    for w in wanted:
        slot, there = find(atoms_from, w)
        bases.append(jnp.where(there > 0, slot * 32, jnp.int32(MISSING)))
    return one_hot((128, 128), 1, bases)


PITCH = 136


def halves(occ, blocks, outs, ms):
    rows = occ.shape[0] // len(outs)
    for i in range(0, len(blocks), 2):
        m0, m1 = blocks[i](), blocks[i + 1]()
        if ms is not None:
            ms[i * PITCH : i * PITCH + 128, :] = m0.astype(F32)
            ms[(i + 1) * PITCH : (i + 1) * PITCH + 128, :] = m1.astype(F32)
        h = dot(occ, jnp.concatenate([m0, m1], axis=1))
        for n, out in enumerate(outs):
            part = h[n * rows : (n + 1) * rows]
            out[i * PITCH : i * PITCH + 128, :] = part[:, :128]
            out[(i + 1) * PITCH : (i + 1) * PITCH + 128, :] = part[:, 128:]


def gather(ref, funcs, start):
    return [ref[pl.ds(start + t, funcs, stride=PITCH), :] for t in range(8)]


def dress(count, own, win, tiles, tensor, greens, *refs):
    if own:
        polar0, flat, dressed, far, hs, ms, same = refs
    else:
        (dressed, far, hs), ms = refs, None
    d = lax.axis_index("row")
    funcs = tensor.shape[1]
    mine = window_at(win, d)
    theirs = window_at(win, near(d, -1, count))
    left, right = near(d, -1, count) * 2, near(d, 1, count) * 2
    mask = tile_mask(tiles, 32).astype(BF)
    occ, virt = greens[0:128, :], greens[128:256, :]
    halves(occ, [functools.partial(lambda r: tensor[0, r] * mask, r) for r in range(funcs)], [hs], ms)
    wide, outs = dot(virt, frame_map(mine, theirs)).astype(BF), [dressed]
    if own:
        wide, outs = jnp.concatenate([virt, wide], axis=1), [same, dressed]
    lane = iota((128, 256), 1)
    atom = jnp.where(lane < 128, left, right)
    column_here = pick4(iota((128, 256), 0) >> 5, mine) == atom + ((lane & 63) >> 5)
    column_here = column_here & ((iota((128, 256), 0) & 31) == (lane & 31))
    both = dot(virt, jnp.where(column_here, 1.0, 0.0).astype(BF))
    row_atom = atom + ((lane & 127) >> 6)
    packs = jnp.concatenate([jnp.where(row_atom == a, both, 0.0).astype(BF) for a in mine], axis=0)
    for c in range(4):
        parts = []
        for i in range(4):
            parts.append(jnp.concatenate(gather(hs, funcs, i * 32 + c * 8), axis=0).astype(BF))
            x = dot(parts[-1], wide)
            for t in range(8):
                at = (i * 32 + c * 8 + t) * 128
                block = x[t * funcs : (t + 1) * funcs].astype(BF)
                for n, out in enumerate(outs):
                    out[:, at : at + 128] = block[:, n * 128 : (n + 1) * 128]
            if own:
                for t, rows in enumerate(gather(ms, funcs, i * 32 + c * 8)):
                    at = (i * 32 + c * 8 + t) * 128
                    flat[:, at : at + 128] = rows.astype(BF)
        x = dot(jnp.concatenate(parts, axis=1), packs)
        for t in range(8):
            at = (c * 8 + t) * 128
            block = x[t * funcs : (t + 1) * funcs].astype(BF)
            far[:, at : at + 128] = block[:, :128]
            far[:, 4096 + at : 4224 + at] = block[:, 128:]
    if own:
        polar0[...] = dot_t(same[...], flat[...])


def stacked(a, b, start, other):
    total = None
    for at in range(0, other.shape[1], 1024):
        left = jnp.concatenate([x[:, start + at : start + at + 1024] for x in (a, b)], axis=0)
        part = dot_t(left, other[:, at : at + 1024])
        total = part if total is None else total + part
    return total


def neighbour_mask(g_before):
    short = g_before[256:272, :].astype(F32)
    return jnp.concatenate(
        [jnp.broadcast_to(short[4 * i : 4 * i + 1, :], (32, 128)) for i in range(4)], axis=0
    ).astype(BF)


def join_back(tensor, g_before, g0, g1, flat, up, hs0, hs1, backs):
    funcs = tensor.shape[0]
    full = 2 * funcs
    mask = neighbour_mask(g_before)
    occ = jnp.concatenate([g0[256:384, :], g1[256:384, :]], axis=0)
    halves(occ, [functools.partial(lambda r: tensor[r] * mask, r) for r in range(funcs)], [hs0, hs1], None)
    virts = [g0[384:512, :], g1[384:512, :]]
    for i in range(16):
        xs = []
        for hs, virt in zip((hs0, hs1), virts):
            xs.append(dot(jnp.concatenate(gather(hs, funcs, i * 8), axis=0).astype(BF), virt))
        for t in range(8):
            at = (i * 8 + t) * 128
            part = slice(t * funcs, (t + 1) * funcs)
            backs[:, at : at + 128] = jnp.concatenate([x[part] for x in xs], axis=0).astype(BF)
    total = dot_t(backs[...], flat[...])
    up[...] = jnp.concatenate([total, jnp.zeros((full, 128 - full), F32)], axis=1)


def join(count, win, tensor, g_before, dressed0, dressed1, down, ms, moved):
    d = lax.axis_index("row")
    funcs = tensor.shape[0]
    full = 2 * funcs
    mine = window_at(win, d)
    theirs = window_at(win, near(d, -1, count))
    mask = neighbour_mask(g_before)
    for r in range(funcs):
        ms[r * PITCH : r * PITCH + 128, :] = (tensor[r] * mask).astype(F32)
    for i in range(16):
        slot, there = find(theirs, mine[i // 4])
        rows = gather(ms, funcs, slot * 32 + (i % 4) * 8)
        for t in range(8):
            at = (i * 8 + t) * 128
            moved[:, at : at + 128] = (rows[t] * there).astype(BF)
    total = stacked(dressed0, dressed1, 0, moved)
    down[...] = jnp.concatenate([total, jnp.zeros((2 * full, 128 - funcs), F32)], axis=1)


FAR_PITCH = 40


def join_far(far0, far1, from_left, from_right, down, after, own, other, es, turned):
    full = far0.shape[0]
    funcs = full // 2
    for e in (from_left, from_right):
        side = 0 if e is from_left else 1
        for r in range(funcs):
            at = r * FAR_PITCH
            es[side, at : at + 32, :] = e[r * 32 : (r + 1) * 32, :].astype(F32)
        for t in range(32):
            rows = es[side, pl.ds(t, funcs, stride=FAR_PITCH), :]
            turned[side, :, t * 128 : (t + 1) * 128] = rows.astype(BF)
    far_left = stacked(far0, far1, 0, turned.at[0])
    far_right = stacked(far0, far1, 4096, turned.at[1])
    padding = jnp.zeros((full, 128 - 3 * funcs - full), F32)
    for n, out in enumerate((own, other)):
        part = slice(n * full, (n + 1) * full)
        back = after[n * funcs : (n + 1) * funcs, :full]
        back = jnp.concatenate([back, jnp.zeros((funcs, full), F32)], axis=0)
        out[...] = jnp.concatenate(
            [far_left[part], down[part, :funcs], far_right[part], back, padding], axis=1
        )


def assemble(polar0, own, recv, out):
    is_first = lax.rem(lax.axis_index("grp"), 2) == 0
    full = polar0.shape[0]
    funcs = full // 2
    a, b = own[...], recv[...]
    low, high = jnp.where(is_first, a, b), jnp.where(is_first, b, a)
    back = slice(3 * funcs, 3 * funcs + full)
    after = jnp.concatenate([low[:funcs, back], high[:funcs, back]], axis=0)
    pieces = []
    for i in range(3):
        part = slice(i * funcs, (i + 1) * funcs)
        if i == 2:
            pieces += [polar0[...], after]
        pieces += [low[:, part], high[:, part]]
    out[...] = jnp.concatenate(pieces, axis=1)


def vmem(count):
    return [pl.BlockSpec(memory_space=pltpu.VMEM)] * count


def hbm(count):
    return [pl.BlockSpec(memory_space=pltpu.HBM)] * count


def smem(count):
    return [pl.BlockSpec(memory_space=pltpu.SMEM)] * count


def call(kernel, name, specs, outs, args, scratch=(), flops=0, limit=40 << 20, space=None):
    return pl.pallas_call(
        kernel,
        name=name,
        in_specs=specs,
        out_specs=tuple((space or vmem)(len(outs))),
        out_shape=tuple(outs),
        scratch_shapes=list(scratch),
        compiler_params=pltpu.CompilerParams(vmem_limit_bytes=limit),
        cost_estimate=pl.CostEstimate(flops=flops, bytes_accessed=0, transcendentals=0),
    )(*args)


def body(groups, count, green_occ, green_virt, coulomb3c, tile_list, window):
    full = coulomb3c.shape[1]
    funcs = full // 2
    shape = jax.ShapeDtypeStruct

    def send(array, row_by, swap=False):
        pairs = []
        for g in range(groups):
            for d in range(count):
                to = (g ^ 1 if swap else g) * count + (d + row_by) % count
                pairs.append((g * count + d, to))
        return lax.ppermute(array, ("grp", "row"), pairs)

    far_rows = funcs * 32
    g_self, g_right, g_left, g_far, tensor = call(
        functools.partial(first, count),
        "first",
        hbm(4),
        [
            shape((256, 128), BF),
            shape((272, 128), BF),
            shape((304, 128), BF),
            shape((288, 128), BF),
            shape((funcs, 128, 128), BF),
        ],
        (green_occ, green_virt, tile_list, coulomb3c),
        [
            pltpu.SMEM((1, 4, 4), jnp.int32),
            pltpu.VMEM((4, 304, 128), BF),
            pltpu.VMEM((funcs, 128, 128), BF),
            pltpu.SemaphoreType.DMA((20,)),
            pltpu.SemaphoreType.DMA((7,)),
        ],
        limit=60 << 20,
        space=hbm,
    )
    g_before = send(g_right, 1)
    g_after = send(g_left, -1)
    g_beyond = send(g_far, 2)
    wide = send(tensor, 1)
    far_right, far_left = call(
        functools.partial(far_tiles, count),
        "far_tiles",
        smem(2) + vmem(1),
        [shape((far_rows, 128), BF), shape((far_rows, 128), BF)],
        (window, tile_list, coulomb3c),
        [pltpu.VMEM((128, 128), BF)],
        flops=1 << 36,
    )
    from_left = send(far_right, 2)
    from_right = send(far_left, -2)
    g_before, g_after, g_beyond, far_right, far_left = lax.optimization_barrier(
        (g_before, g_after, g_beyond, far_right, far_left)
    )
    (mine,) = call(
        functools.partial(choose, count),
        "choose",
        smem(1) + vmem(4),
        [shape((512, 128), BF)],
        (window, g_self, g_before, g_after, g_beyond),
    )
    partner = send(mine, 0, True)
    flat_shape, far_shape = shape((full, 128 * 128), BF), shape((full, 64 * 128), BF)
    tall = pltpu.VMEM((full * PITCH, 128), F32)
    short = pltpu.VMEM((funcs * PITCH, 128), F32)
    message = shape((full, 128), F32)
    polar0, flat, dressed0, far0 = call(
        functools.partial(dress, count, True),
        "dress_own",
        smem(2) + vmem(2),
        [shape((full, full), F32), flat_shape, flat_shape, far_shape],
        (window, tile_list, coulomb3c, mine),
        [tall, tall, pltpu.VMEM((full, 128 * 128), BF)],
    )
    dressed1, far1 = call(
        functools.partial(dress, count, False),
        "dress_partner",
        smem(2) + vmem(2),
        [flat_shape, far_shape],
        (window, tile_list, coulomb3c, partner),
        [tall],
    )
    g_before, dressed1 = lax.optimization_barrier((g_before, dressed1))
    (up,) = call(
        join_back,
        "join_back",
        vmem(5),
        [message],
        (wide, g_before, mine, partner, flat),
        [short, short, pltpu.VMEM((full, 128 * 128), BF)],
    )
    after = send(up, -1)
    (down,) = call(
        functools.partial(join, count),
        "join",
        smem(1) + vmem(4),
        [shape((2 * full, 128), F32)],
        (window, wide, g_before, dressed0, dressed1),
        [short, pltpu.VMEM((funcs, 128 * 128), BF)],
    )
    own, other = call(
        join_far,
        "join_far",
        vmem(6),
        [message, message],
        (far0, far1, from_left, from_right, down, after),
        [pltpu.VMEM((2, funcs * FAR_PITCH, 128), F32), pltpu.VMEM((2, funcs, 32 * 128), BF)],
    )
    recv = send(other, 0, True)
    (out,) = call(
        assemble,
        "assemble",
        vmem(3),
        [shape((full, 5 * full), F32)],
        (polar0, own, recv),
    )
    return out


def solution(mesh):
    placed = (
        P(("grp", "row"), None),
        P(("grp", "row"), None),
        P("row", None, None, None),
        P("row", None, None),
        P(),
    )
    return jax.shard_map(
        functools.partial(body, mesh.shape["grp"], mesh.shape["row"]),
        mesh=mesh,
        in_specs=placed,
        out_specs=P(("grp", "row"), None),
        check_vma=False,
    )
```

```python
import functools

import jax
import jax.numpy as jnp
from jax import lax
from jax.experimental import pallas as pl
from jax.experimental.pallas import tpu as pltpu
from jax.sharding import PartitionSpec as P

BF = jnp.bfloat16
F32 = jnp.float32
MISSING = -(1 << 20)


def dot(a, b):
    return lax.dot_general(a, b, (((1,), (0,)), ((), ())), preferred_element_type=F32)


def dot_t(a, b):
    return lax.dot_general(a, b, (((1,), (1,)), ((), ())), preferred_element_type=F32)


def iota(shape, dim):
    return lax.broadcasted_iota(jnp.int32, shape, dim)


def pick4(index, values):
    return jnp.where(
        index == 0, values[0], jnp.where(index == 1, values[1], jnp.where(index == 2, values[2], values[3]))
    )


def one_hot(shape, dim, bases):
    index = iota(shape, dim)
    position = pick4(index >> 5, bases) + (index & 31)
    return jnp.where(iota(shape, 1 - dim) == position, 1.0, 0.0).astype(BF)


def window_at(win, row):
    return [win[row, i] for i in range(4)]


def find(atoms, wanted):
    slot, there = jnp.int32(0), jnp.float32(0)
    for i in range(4):
        hit = atoms[i] == wanted
        slot = jnp.where(hit, jnp.int32(i), slot)
        there = jnp.where(hit, jnp.float32(1), there)
    return slot, there


def tile_mask(tiles, rows):
    shape = (4 * rows, 128)
    row, lane = iota(shape, 0) // rows, iota(shape, 1) >> 5
    mask = jnp.zeros(shape, F32)
    for i in range(4):
        for j in range(4):
            mask = jnp.where((row == i) & (lane == j), tiles[0, i, j].astype(F32), mask)
    return mask


def near(row, by, count):
    return lax.rem(row + by + count, count)


def column_chunk(row, count):
    return near(row, -1, count) >> 1


def first(count, occ, virt, tiles_hbm, coulomb, *refs):
    outs, (tiles, gs, part, sem, done) = refs[:5], refs[5:]
    d = lax.axis_index("row")
    funcs = part.shape[0]
    half = lax.rem(lax.axis_index("grp"), 2)
    list_copy = pltpu.make_async_copy(tiles_hbm, tiles, sem.at[16])
    list_copy.start()
    groups = []
    for n, by in enumerate((0, 1, -1, 2)):
        start = column_chunk(near(d, by, count), count)
        copies = []
        for c in range(2):
            chunk = lax.rem(start + c, count // 2)
            columns = pl.ds(pl.multiple_of(chunk * 128, 128), 128)
            for base, green in ((0, occ), (128, virt)):
                at = base + 64 * c
                place = gs.at[n, at : at + 64]
                copies.append(pltpu.make_async_copy(green.at[:, columns], place, sem.at[4 * n + len(copies)]))
        rows = outs[n].shape[0]
        groups.append((copies, pltpu.make_async_copy(gs.at[n, 0:rows], outs[n], done.at[n])))
    for n in range(3):
        piece = pl.ds(half * funcs + n * 8, 8)
        copy = pltpu.make_async_copy(coulomb.at[0, piece], part.at[n * 8 : n * 8 + 8], sem.at[17 + n])
        out = pltpu.make_async_copy(part.at[n * 8 : n * 8 + 8], outs[4].at[n * 8 : n * 8 + 8], done.at[4 + n])
        groups.append(([copy], out))
    for copies, _ in groups:
        for copy in copies:
            copy.start()
    list_copy.wait()
    short = tile_mask(tiles, 4).astype(BF)
    for n in range(1, 4):
        for at in (256, 272, 288):
            gs[n, at : at + 16, :] = short
    for copies, out in groups:
        for copy in copies:
            copy.wait()
        out.start()
    for _, out in groups:
        out.wait()


def far_tiles(count, win, tiles, tensor, far_right, far_left, mask):
    d = lax.axis_index("row")
    mine = window_at(win, d)
    funcs = tensor.shape[1] // 2
    start = lax.rem(lax.axis_index("grp"), 2) * funcs
    mask[...] = tile_mask(tiles, 32).astype(BF)
    for by, out in ((-1, far_left), (1, far_right)):
        base = near(d, by, count) * 2
        shape = (256, 128)
        row, lane = iota(shape, 0), iota(shape, 1)
        found = [find(mine, base), find(mine, base + 1)]
        here = pick4((row & 127) >> 5, mine) == base + ((lane & 63) >> 5)
        same = here & ((row & 31) == (lane & 31)) & ((row >> 7) == (lane >> 6))
        weight = jnp.where(row < 128, found[0][1], found[1][1])
        select = jnp.where(same, weight, 0.0).astype(BF)
        places = [pl.ds(pl.multiple_of(slot * 32, 32), 32) for slot, _ in found]
        masks = [mask[place, :] for place in places]
        for r in range(0, funcs, 8):
            sides = [
                jnp.concatenate([tensor[0, start + r + u, place, :] * m for u in range(8)], axis=0)
                for place, m in zip(places, masks)
            ]
            x = dot(jnp.concatenate(sides, axis=1), select)
            out[r * 32 : r * 32 + 256, :] = x.astype(BF)
    far_right[funcs * 32 : funcs * 32 + 16, :] = jnp.zeros((16, 128), BF)


def choose(count, win, g_self, g_before, g_after, g_far, out):
    d = lax.axis_index("row")
    atoms = 2 * count
    mine = window_at(win, d)
    theirs = window_at(win, near(d, -1, count))
    row0 = near(d, -2, count) * 2
    col0 = column_chunk(d, count) * 4

    def position(atom, start):
        return lax.rem(atom - start + atoms, atoms) * 32

    def whole(base):
        blocks = []
        for c in range(2):
            at = base + 64 * c
            blocks.append(
                jnp.concatenate(
                    [
                        g_far[at : at + 64, :],
                        g_before[at : at + 64, :],
                        g_self[at : at + 64, :],
                        g_after[at : at + 64, :],
                    ],
                    axis=0,
                )
            )
        return jnp.concatenate(blocks, axis=1)

    occ, virt = whole(0), whole(128)
    rows_mine = [position(a, row0) for a in mine]
    rows_theirs = [position(a, row0) for a in theirs]
    columns_mine = [position(a, col0) for a in mine]
    columns_both = []
    for i in range(4):
        _, there = find(theirs, mine[i])
        columns_both.append(jnp.where(there > 0, columns_mine[i], jnp.int32(MISSING)))
    for base, rows, columns in ((0, rows_mine, columns_mine), (256, rows_theirs, columns_both)):
        left = one_hot((128, 256), 0, columns)
        x = dot_t(left, occ).astype(BF)
        out[base : base + 128, :] = dot(x, one_hot((256, 128), 1, rows)).astype(BF)
        y = dot(one_hot((128, 256), 0, rows), virt).astype(BF)
        out[base + 128 : base + 256, :] = dot(y, one_hot((256, 128), 1, columns)).astype(BF)


def frame_map(atoms_from, wanted):
    bases = []
    for w in wanted:
        slot, there = find(atoms_from, w)
        bases.append(jnp.where(there > 0, slot * 32, jnp.int32(MISSING)))
    return one_hot((128, 128), 1, bases)


PITCH = 136


def halves(occ, blocks, outs, ms):
    rows = occ.shape[0] // len(outs)
    for i in range(0, len(blocks), 2):
        m0, m1 = blocks[i](), blocks[i + 1]()
        if ms is not None:
            ms[i * PITCH : i * PITCH + 128, :] = m0.astype(F32)
            ms[(i + 1) * PITCH : (i + 1) * PITCH + 128, :] = m1.astype(F32)
        h = dot(occ, jnp.concatenate([m0, m1], axis=1))
        for n, out in enumerate(outs):
            part = h[n * rows : (n + 1) * rows]
            out[i * PITCH : i * PITCH + 128, :] = part[:, :128]
            out[(i + 1) * PITCH : (i + 1) * PITCH + 128, :] = part[:, 128:]


def gather(ref, funcs, start):
    return [ref[pl.ds(start + t, funcs, stride=PITCH), :] for t in range(8)]


def dress(count, own, win, tiles, tensor, greens, *refs):
    if own:
        polar0, flat, dressed, far, hs, ms, same = refs
    else:
        (dressed, far, hs), ms = refs, None
    d = lax.axis_index("row")
    funcs = tensor.shape[1]
    mine = window_at(win, d)
    theirs = window_at(win, near(d, -1, count))
    left, right = near(d, -1, count) * 2, near(d, 1, count) * 2
    mask = tile_mask(tiles, 32).astype(BF)
    occ, virt = greens[0:128, :], greens[128:256, :]
    halves(occ, [functools.partial(lambda r: tensor[0, r] * mask, r) for r in range(funcs)], [hs], ms)
    wide, outs = dot(virt, frame_map(mine, theirs)).astype(BF), [dressed]
    if own:
        wide, outs = jnp.concatenate([virt, wide], axis=1), [same, dressed]
    lane = iota((128, 256), 1)
    atom = jnp.where(lane < 128, left, right)
    column_here = pick4(iota((128, 256), 0) >> 5, mine) == atom + ((lane & 63) >> 5)
    column_here = column_here & ((iota((128, 256), 0) & 31) == (lane & 31))
    both = dot(virt, jnp.where(column_here, 1.0, 0.0).astype(BF))
    row_atom = atom + ((lane & 127) >> 6)
    packs = jnp.concatenate([jnp.where(row_atom == a, both, 0.0).astype(BF) for a in mine], axis=0)
    for c in range(4):
        parts = []
        for i in range(4):
            parts.append(jnp.concatenate(gather(hs, funcs, i * 32 + c * 8), axis=0).astype(BF))
            x = dot(parts[-1], wide)
            for t in range(8):
                at = (i * 32 + c * 8 + t) * 128
                block = x[t * funcs : (t + 1) * funcs].astype(BF)
                for n, out in enumerate(outs):
                    out[:, at : at + 128] = block[:, n * 128 : (n + 1) * 128]
            if own:
                for t, rows in enumerate(gather(ms, funcs, i * 32 + c * 8)):
                    at = (i * 32 + c * 8 + t) * 128
                    flat[:, at : at + 128] = rows.astype(BF)
        x = dot(jnp.concatenate(parts, axis=1), packs)
        for t in range(8):
            at = (c * 8 + t) * 128
            block = x[t * funcs : (t + 1) * funcs].astype(BF)
            far[:, at : at + 128] = block[:, :128]
            far[:, 4096 + at : 4224 + at] = block[:, 128:]
    if own:
        polar0[...] = dot_t(same[...], flat[...])


def stacked(a, b, start, other):
    total = None
    for at in range(0, other.shape[1], 1024):
        left = jnp.concatenate([x[:, start + at : start + at + 1024] for x in (a, b)], axis=0)
        part = dot_t(left, other[:, at : at + 1024])
        total = part if total is None else total + part
    return total


def neighbour_mask(g_before):
    short = g_before[256:272, :].astype(F32)
    return jnp.concatenate(
        [jnp.broadcast_to(short[4 * i : 4 * i + 1, :], (32, 128)) for i in range(4)], axis=0
    ).astype(BF)


def join_back(tensor, g_before, g0, g1, flat, up, hs0, hs1, backs):
    funcs = tensor.shape[0]
    full = 2 * funcs
    mask = neighbour_mask(g_before)
    occ = jnp.concatenate([g0[256:384, :], g1[256:384, :]], axis=0)
    halves(occ, [functools.partial(lambda r: tensor[r] * mask, r) for r in range(funcs)], [hs0, hs1], None)
    virts = [g0[384:512, :], g1[384:512, :]]
    for i in range(16):
        xs = []
        for hs, virt in zip((hs0, hs1), virts):
            xs.append(dot(jnp.concatenate(gather(hs, funcs, i * 8), axis=0).astype(BF), virt))
        for t in range(8):
            at = (i * 8 + t) * 128
            part = slice(t * funcs, (t + 1) * funcs)
            backs[:, at : at + 128] = jnp.concatenate([x[part] for x in xs], axis=0).astype(BF)
    total = dot_t(backs[...], flat[...])
    up[...] = jnp.concatenate([total, jnp.zeros((full, 128 - full), F32)], axis=1)


def join(count, win, tensor, g_before, dressed0, dressed1, down, ms, moved):
    d = lax.axis_index("row")
    funcs = tensor.shape[0]
    full = 2 * funcs
    mine = window_at(win, d)
    theirs = window_at(win, near(d, -1, count))
    mask = neighbour_mask(g_before)
    for r in range(funcs):
        ms[r * PITCH : r * PITCH + 128, :] = (tensor[r] * mask).astype(F32)
    for i in range(16):
        slot, there = find(theirs, mine[i // 4])
        rows = gather(ms, funcs, slot * 32 + (i % 4) * 8)
        for t in range(8):
            at = (i * 8 + t) * 128
            moved[:, at : at + 128] = (rows[t] * there).astype(BF)
    total = stacked(dressed0, dressed1, 0, moved)
    down[...] = jnp.concatenate([total, jnp.zeros((2 * full, 128 - funcs), F32)], axis=1)


FAR_PITCH = 40


def join_far(far0, far1, from_left, from_right, down, after, own, other, es, turned):
    full = far0.shape[0]
    funcs = full // 2
    for e in (from_left, from_right):
        side = 0 if e is from_left else 1
        for r in range(funcs):
            at = r * FAR_PITCH
            es[side, at : at + 32, :] = e[r * 32 : (r + 1) * 32, :].astype(F32)
        for t in range(32):
            rows = es[side, pl.ds(t, funcs, stride=FAR_PITCH), :]
            turned[side, :, t * 128 : (t + 1) * 128] = rows.astype(BF)
    far_left = stacked(far0, far1, 0, turned.at[0])
    far_right = stacked(far0, far1, 4096, turned.at[1])
    padding = jnp.zeros((full, 128 - 3 * funcs - full), F32)
    for n, out in enumerate((own, other)):
        part = slice(n * full, (n + 1) * full)
        back = after[n * funcs : (n + 1) * funcs, :full]
        back = jnp.concatenate([back, jnp.zeros((funcs, full), F32)], axis=0)
        out[...] = jnp.concatenate(
            [far_left[part], down[part, :funcs], far_right[part], back, padding], axis=1
        )


def assemble(polar0, own, recv, out):
    is_first = lax.rem(lax.axis_index("grp"), 2) == 0
    full = polar0.shape[0]
    funcs = full // 2
    a, b = own[...], recv[...]
    low, high = jnp.where(is_first, a, b), jnp.where(is_first, b, a)
    back = slice(3 * funcs, 3 * funcs + full)
    after = jnp.concatenate([low[:funcs, back], high[:funcs, back]], axis=0)
    pieces = []
    for i in range(3):
        part = slice(i * funcs, (i + 1) * funcs)
        if i == 2:
            pieces += [polar0[...], after]
        pieces += [low[:, part], high[:, part]]
    out[...] = jnp.concatenate(pieces, axis=1)


def vmem(count):
    return [pl.BlockSpec(memory_space=pltpu.VMEM)] * count


def hbm(count):
    return [pl.BlockSpec(memory_space=pltpu.HBM)] * count


def smem(count):
    return [pl.BlockSpec(memory_space=pltpu.SMEM)] * count


def call(kernel, name, specs, outs, args, scratch=(), flops=0, limit=40 << 20, space=None):
    return pl.pallas_call(
        kernel,
        name=name,
        in_specs=specs,
        out_specs=tuple((space or vmem)(len(outs))),
        out_shape=tuple(outs),
        scratch_shapes=list(scratch),
        compiler_params=pltpu.CompilerParams(vmem_limit_bytes=limit),
        cost_estimate=pl.CostEstimate(flops=flops, bytes_accessed=0, transcendentals=0),
    )(*args)


def body(groups, count, green_occ, green_virt, coulomb3c, tile_list, window):
    full = coulomb3c.shape[1]
    funcs = full // 2
    shape = jax.ShapeDtypeStruct

    def send(array, row_by, swap=False):
        pairs = []
        for g in range(groups):
            for d in range(count):
                to = (g ^ 1 if swap else g) * count + (d + row_by) % count
                pairs.append((g * count + d, to))
        return lax.ppermute(array, ("grp", "row"), pairs)

    far_rows = funcs * 32
    g_self, g_right, g_left, g_far, tensor = call(
        functools.partial(first, count),
        "first",
        hbm(4),
        [
            shape((256, 128), BF),
            shape((272, 128), BF),
            shape((304, 128), BF),
            shape((288, 128), BF),
            shape((funcs, 128, 128), BF),
        ],
        (green_occ, green_virt, tile_list, coulomb3c),
        [
            pltpu.SMEM((1, 4, 4), jnp.int32),
            pltpu.VMEM((4, 304, 128), BF),
            pltpu.VMEM((funcs, 128, 128), BF),
            pltpu.SemaphoreType.DMA((20,)),
            pltpu.SemaphoreType.DMA((7,)),
        ],
        limit=60 << 20,
        space=hbm,
    )
    g_before = send(g_right, 1)
    g_after = send(g_left, -1)
    g_beyond = send(g_far, 2)
    wide = send(tensor, 1)
    far_right, far_left = call(
        functools.partial(far_tiles, count),
        "far_tiles",
        smem(2) + vmem(1),
        [shape((far_rows + 16, 128), BF), shape((far_rows, 128), BF)],
        (window, tile_list, coulomb3c),
        [pltpu.VMEM((128, 128), BF)],
        flops=1 << 36,
    )
    from_left = send(far_right, 2)
    from_right = send(far_left, -2)
    g_before, g_after, g_beyond, far_right, far_left = lax.optimization_barrier(
        (g_before, g_after, g_beyond, far_right, far_left)
    )
    (mine,) = call(
        functools.partial(choose, count),
        "choose",
        smem(1) + vmem(4),
        [shape((512, 128), BF)],
        (window, g_self, g_before, g_after, g_beyond),
    )
    partner = send(mine, 0, True)
    flat_shape, far_shape = shape((full, 128 * 128), BF), shape((full, 64 * 128), BF)
    tall = pltpu.VMEM((full * PITCH, 128), F32)
    short = pltpu.VMEM((funcs * PITCH, 128), F32)
    message = shape((full, 128), F32)
    polar0, flat, dressed0, far0 = call(
        functools.partial(dress, count, True),
        "dress_own",
        smem(2) + vmem(2),
        [shape((full, full), F32), flat_shape, flat_shape, far_shape],
        (window, tile_list, coulomb3c, mine),
        [tall, tall, pltpu.VMEM((full, 128 * 128), BF)],
    )
    dressed1, far1 = call(
        functools.partial(dress, count, False),
        "dress_partner",
        smem(2) + vmem(2),
        [flat_shape, far_shape],
        (window, tile_list, coulomb3c, partner),
        [tall],
    )
    g_before, dressed1 = lax.optimization_barrier((g_before, dressed1))
    (up,) = call(
        join_back,
        "join_back",
        vmem(5),
        [message],
        (wide, g_before, mine, partner, flat),
        [short, short, pltpu.VMEM((full, 128 * 128), BF)],
    )
    after = send(up, -1)
    (down,) = call(
        functools.partial(join, count),
        "join",
        smem(1) + vmem(4),
        [shape((2 * full, 128), F32)],
        (window, wide, g_before, dressed0, dressed1),
        [short, pltpu.VMEM((funcs, 128 * 128), BF)],
    )
    own, other = call(
        join_far,
        "join_far",
        vmem(6),
        [message, message],
        (far0, far1, from_left, from_right, down, after),
        [pltpu.VMEM((2, funcs * FAR_PITCH, 128), F32), pltpu.VMEM((2, funcs, 32 * 128), BF)],
    )
    recv = send(other, 0, True)
    (out,) = call(
        assemble,
        "assemble",
        vmem(3),
        [shape((full, 5 * full), F32)],
        (polar0, own, recv),
    )
    return out


def solution(mesh):
    placed = (
        P(("grp", "row"), None),
        P(("grp", "row"), None),
        P("row", None, None, None),
        P("row", None, None),
        P(),
    )
    return jax.shard_map(
        functools.partial(body, mesh.shape["grp"], mesh.shape["row"]),
        mesh=mesh,
        in_specs=placed,
        out_specs=P(("grp", "row"), None),
        check_vma=False,
    )
```
